256 devices in a mesh: ka: 8 (over z_lo, core), ga: 32 (over x, y, z_hi).
Axes of the slice: x: 4, y: 4, z: 8 (z_hi: 2, z_lo: 4; z = z_hi * 4 + z_lo), core: 2. Of those that a mesh axis runs over, the one named last changes fastest.
Arguments:
- wavefunctions: bfloat16 [64, 2, 16, 32, 256], P('ka', None, None, 'ga'), may hold values from -6 to 6
- partner: int32 [64], replicated, may hold values from 0 to 63, each once
- gmap: int32 [8192], replicated, may hold values from 0 to 8191, as said below
- screened: bfloat16 [8192, 8192], P('ga'), may hold values from -0.0007324219 to 0.0007324219
Outputs:
- kernel_rows: float32 [64, 2, 4096], P('ka')
- kernel_mirror: float32 [64, 2, 4096], P('ka')
The draws below stay inside these ranges and needn't reach their ends.
Inputs may be any that keep to these rules, and one draw needn't show every extreme that they name: `partner`: each k-point appears exactly once. Entries j and gmap[j] lie in the same aligned block of 32; within each block every index appears once.
All inputs are finite; a program needn't handle non-finite values.
Results may differ from the reference program's by a relative error of at most 0.0042.
Values may be sent and summed in bfloat16 or wider, within the bound.
No kernel may reach another device: no remote copies, remote signals or barrier semaphores. Data moves between devices by JAX's collectives and lax.ppermute only.
A program may use at most 256 MiB of HBM per device.

```python
import jax
import jax.numpy as jnp
from jax import lax

NV = 8
NC = 8
NX = 16
NY = 16
NZ = 32
NB = 16
NXY = 256
NG = 8192
NF = 128
NK = 64


def draw_gmap(key, part):
    key = jax.random.fold_in(key, 11)
    column_keys = jax.random.split(key, NX * NY)
    shuffled = jax.vmap(lambda column_key: jax.random.permutation(column_key, NZ))(column_keys)
    offsets = NZ * jnp.arange(NX * NY, dtype=jnp.int32)[:, None]
    return (shuffled.astype(jnp.int32) + offsets).reshape(NX * NY * NZ).astype(jnp.int32)


def shard_levels(own_key, extent, cuts, smallest, high):
    factor_of = 1.0
    for dim, shards_of in cuts:
        steps = jax.random.uniform(jax.random.fold_in(jax.random.fold_in(own_key, 6), dim), (shards_of,), jnp.float32, smallest / len(cuts), high / len(cuts))
        factor_of = factor_of * jnp.repeat(jnp.exp(steps), extent[dim] // shards_of).reshape((-1,) + (1,) * (len(extent) - 1 - dim))
    return factor_of


def bell_draw(own_key, extent, width, most, shards=(), kind=jnp.bfloat16):
    values = jax.random.normal(own_key, extent, jnp.float32) * width
    if len(shards) > 0:
        values = shard_levels(own_key, extent, shards, -0.22, 0.18) * values
    return jnp.clip(values, min=-most, max=most).astype(kind)


def setup_inputs(seed: int = 0) -> dict:
    key_of = jax.random.split(jax.random.key(seed), 5)
    return {
        "wavefunctions": bell_draw(key_of[0], (NK, 2, NB, NZ, NXY), 1.0, 6.0, ((0, 8), (3, 32))),
        "partner": jax.random.permutation(key_of[1], NK).astype(jnp.int32),
        "gmap": draw_gmap(jax.random.fold_in(key_of[4], 71), 0),
        "screened": bell_draw(key_of[3], (NG, NG), (NG * NG) ** -0.5, 0.0007324219, ((0, 32),)),
    }


def pair_density(left, right):
    product = jnp.conj(left[:, :, None]) * right[:, None, :]
    return product.reshape(left.shape[0], left.shape[1] * right.shape[1], NX, NY, NZ)

def swap_blocks(blocks):
    count = blocks.shape[0]
    moved = blocks.reshape(count, 2, NC, NC, NV, NV).transpose(0, 1, 3, 2, 5, 4).reshape(count, 2, NC * NC * NV * NV)
    return moved * jnp.array([1.0, -1.0], dtype=jnp.float32)[None, :, None]

def reference(wavefunctions, partner, gmap, screened):
    values = wavefunctions.astype(jnp.float32)
    waves = values[:, 0] + 1j * values[:, 1]
    waves = waves.reshape(NK, NB, NZ, NX, NY).transpose(0, 1, 3, 4, 2)
    home = waves
    away = waves[partner]
    cond_rho = pair_density(home[:, NV:], away[:, NV:])
    val_rho = pair_density(home[:, :NV], away[:, :NV])
    density = jnp.concatenate([cond_rho, val_rho], axis=1)
    spectrum = jnp.fft.fftn(density, axes=(-3, -2, -1)) / jnp.sqrt(jnp.float32(NG))
    spectrum = spectrum.reshape(NK, NF, NG)
    parts = jnp.stack([jnp.real(spectrum).astype(jnp.bfloat16), jnp.imag(spectrum).astype(jnp.bfloat16)], axis=1)
    ordered = parts[:, :, :, gmap]
    cond_part = ordered[:, :, :NC * NC, :]
    val_part = ordered[:, :, NC * NC:, :]
    val_cols = val_part.transpose(3, 0, 1, 2).reshape(NG, NK * 2 * NV * NV)
    response = jnp.dot(screened.astype(jnp.float32), val_cols.astype(jnp.float32), precision=lax.Precision.HIGHEST)
    response = response.reshape(NG, NK, 2, NV * NV)
    cond_f = cond_part.astype(jnp.float32).transpose(3, 0, 1, 2)
    highest = lax.Precision.HIGHEST
    real_out = jnp.einsum('gkc,gkv->kcv', cond_f[:, :, 0], response[:, :, 0], precision=highest) + jnp.einsum('gkc,gkv->kcv', cond_f[:, :, 1], response[:, :, 1], precision=highest)
    imag_out = jnp.einsum('gkc,gkv->kcv', cond_f[:, :, 0], response[:, :, 1], precision=highest) - jnp.einsum('gkc,gkv->kcv', cond_f[:, :, 1], response[:, :, 0], precision=highest)
    kernel = jnp.stack([real_out, imag_out], axis=1).reshape(NK, 2, NC * NC * NV * NV)
    kernel_rows = kernel
    kernel_mirror = jnp.zeros_like(kernel).at[partner].set(swap_blocks(kernel))
    return (kernel_rows, kernel_mirror)
```

```python
import math

import jax
import jax.numpy as jnp
import numpy as np
from jax import lax
from jax.experimental import pallas as pl
from jax.experimental.pallas import tpu as pltpu
from jax.sharding import PartitionSpec as P

NX = 16
NY = 16
NZ = 32
NG = 8192
PLANE = NX * NY
HALF = NZ // 2 + 1
NORM = 1.0 / math.sqrt(NG)
EXACT = lax.Precision.HIGHEST
BF = jnp.bfloat16
F32 = jnp.float32
MIB = 1 << 20

SHAPE = (4, 4, 2)
XS = ((1, 0, 0), (3, 0, 0), (2, 0, 0))
YS = ((0, 1, 0), (0, 3, 0), (0, 2, 0))
ZS = ((0, 0, 1),)
SLOT = (0, 1, 3, 2)


def split_table(table):
    high = table.astype(np.float32).astype(BF)
    low = (table - high.astype(np.float64)).astype(np.float32).astype(BF)
    return high, low


def plane_angles():
    index = np.arange(PLANE)
    x, y = index // NY, index % NY
    turns = (np.outer(x, x) % NX) / NX + (np.outer(y, y) % NY) / NY
    return 2.0 * np.pi * turns


def line_angles():
    index = np.arange(NZ)
    return 2.0 * np.pi * (np.outer(index, index) % NZ) / NZ


def shifted(value, offset):
    pairs = []
    for source in range(32):
        place = (source // 8, source // 2 % 4, source % 2)
        x, y, z = ((a + b) % n for a, b, n in zip(place, offset, SHAPE))
        pairs.append((source, x * 8 + y * 2 + z))
    return lax.ppermute(value, "ga", pairs)


def spread(value, offsets):
    return jnp.stack([value] + [shifted(value, offset) for offset in offsets])


def around_ka(value):
    return [value] + [
        lax.ppermute(value, "ka", [(i, (i + d) % 8) for i in range(8)]) for d in range(1, 8)
    ]


def gather_planes(value):
    both = spread(value, ZS)
    first, second = both[:, :4], both[:, 4:]
    first, second = spread(first, XS), spread(second, YS)
    first, second = spread(first, YS), spread(second, XS)
    return first.reshape((32,) + value[:4].shape), second.reshape((32,) + value[4:].shape)


def plane_slots(place):
    z = jnp.arange(32, dtype=jnp.int32)
    slot = jnp.array(SLOT, dtype=jnp.int32)
    sx = slot[(place // 8 - z // 8) % 4]
    sy = slot[(place // 2 - z // 2) % 4]
    sz = (place - z) % 2
    return (sy * 4 + sx) * 2 + sz, (sx * 4 + sy) * 2 + sz


def dot(a, b, contract=((1,), (0,)), precision=None):
    return lax.dot_general(
        a, b, (contract, ((), ())), precision=precision, preferred_element_type=F32
    )


def line_kernel(gmap_ref, high_ref, low_ref, w_ref, y_ref):
    level = gmap_ref[0] & (NZ - 1)
    hot = (lax.broadcasted_iota(jnp.int32, (NZ, 256), 0) == level).astype(F32).astype(BF)
    rows = 2 * HALF * 8
    keep = (lax.broadcasted_iota(jnp.int32, (rows, 256), 0) & 7) == (
        lax.broadcasted_iota(jnp.int32, (rows, 256), 1) >> 5
    )
    block = w_ref[...]
    total = None
    for table in (high_ref, low_ref):
        picked = jnp.where(keep, dot(table[...], hot), 0.0).astype(BF)
        part = dot(picked, block, ((1,), (1,)))
        total = part if total is None else total + part
    y_ref[...] = total.reshape(2, HALF, 8, 256)


def line_transform(screened, gmap):
    angles = line_angles()[:HALF]
    table = np.stack([np.cos(angles), -np.sin(angles)])
    table = np.repeat(table.reshape(2 * HALF, NZ), 8, axis=0)
    high, low = split_table(table)
    rows = 2 * HALF * 8
    return pl.pallas_call(
        line_kernel,
        grid=(32,),
        in_specs=[
            pl.BlockSpec((1, 1, 256), lambda b: (b, 0, 0)),
            pl.BlockSpec((rows, NZ), lambda b: (0, 0)),
            pl.BlockSpec((rows, NZ), lambda b: (0, 0)),
            pl.BlockSpec((256, 256), lambda b: (0, b)),
        ],
        out_specs=pl.BlockSpec((2, HALF, 8, 256), lambda b: (0, 0, b, 0)),
        out_shape=jax.ShapeDtypeStruct((2, HALF, PLANE, 256), F32),
        compiler_params=pltpu.CompilerParams(vmem_limit_bytes=24 * MIB),
        cost_estimate=pl.CostEstimate(
            flops=4 * rows * 256 * 8192, bytes_accessed=14 * MIB, transcendentals=0
        ),
        name="screened_line",
    )(gmap.reshape(32, 1, 256), jnp.asarray(high), jnp.asarray(low), screened)


def plane_kernel(high_ref, low_ref, y_ref, w_ref):
    real, imag = y_ref[0, 0], y_ref[1, 0]
    both = jnp.concatenate([real, imag], axis=1)
    top = both.astype(BF)
    rest = (both - top.astype(F32)).astype(BF)
    prod = dot(high_ref[...], top) + (dot(high_ref[...], rest) + dot(low_ref[...], top))
    w_ref[0, :256] = (prod[:256, :256] + prod[256:, 256:]).astype(BF)
    w_ref[0, 256:] = (prod[256:, :256] - prod[:256, 256:]).astype(BF)


def plane_transform(lines):
    angles = plane_angles()
    high, low = split_table(np.concatenate([np.cos(angles), np.sin(angles)], axis=0))
    return pl.pallas_call(
        plane_kernel,
        grid=(HALF,),
        in_specs=[
            pl.BlockSpec((512, 256), lambda z: (0, 0)),
            pl.BlockSpec((512, 256), lambda z: (0, 0)),
            pl.BlockSpec((2, 1, 256, 256), lambda z: (0, z, 0, 0)),
        ],
        out_specs=pl.BlockSpec((1, 512, 256), lambda z: (z, 0, 0)),
        out_shape=jax.ShapeDtypeStruct((HALF, 512, 256), BF),
        compiler_params=pltpu.CompilerParams(vmem_limit_bytes=24 * MIB),
        cost_estimate=pl.CostEstimate(
            flops=6 * 512 * 256 * 512 * HALF, bytes_accessed=14 * MIB, transcendentals=0
        ),
        name="screened_plane",
    )(jnp.asarray(high), jnp.asarray(low), lines)


def choose_kernel(slot_ref, flip_ref, *refs):
    slots, (val_ref, cond_ref) = refs[:8], refs[8:]
    for m in range(8):
        wanted = slot_ref[m]
        for d in range(8):

            @pl.when(wanted // 8 == d)
            def _(m=m, d=d):
                row = slots[d][wanted % 8]
                val_ref[m] = dot(row[:16], flip_ref[...]).astype(BF)
                cond_ref[m] = row[16:]


def choose(slots, wanted, flip):
    shape = jax.ShapeDtypeStruct((8, 16, 256), BF)
    return pl.pallas_call(
        choose_kernel,
        in_specs=[pl.BlockSpec(memory_space=pltpu.SMEM)]
        + [pl.BlockSpec(memory_space=pltpu.VMEM)] * 9,
        out_specs=[pl.BlockSpec(memory_space=pltpu.VMEM)] * 2,
        out_shape=[shape, shape],
        compiler_params=pltpu.CompilerParams(vmem_limit_bytes=16 * MIB),
        name="partner_choice",
    )(wanted, flip, *slots)


def cond_kernel(table_ref, home_ref, away_ref, x_ref, rows_ref):
    for k in range(8):
        home, away = home_ref[k].astype(F32), away_ref[k].astype(F32)
        hr, hi = home[:8], home[8:]
        for place, band in enumerate((0, 2, 4, 6, 1, 3, 5, 7)):
            ar, ai = away[band : band + 1], away[8 + band : 9 + band]
            real = hr * ar + hi * ai
            imag = hr * ai - hi * ar
            at = k * 128 + place * 8
            rows_ref[at : at + 8, :256] = real
            rows_ref[at : at + 8, 256:] = imag
            rows_ref[at + 64 : at + 72, :256] = imag
            rows_ref[at + 64 : at + 72, 256:] = -real
    for k in range(8):
        x_ref[:, k * 128 : (k + 1) * 128] = dot(
            table_ref[...], rows_ref[k * 128 : (k + 1) * 128], ((1,), (1,)), EXACT
        )


def cond_planes(home, away):
    angles = plane_angles()
    table = np.concatenate([np.cos(angles), np.sin(angles)], axis=1).astype(np.float32)
    return pl.pallas_call(
        cond_kernel,
        out_shape=jax.ShapeDtypeStruct((256, 1024), F32),
        in_specs=[pl.BlockSpec(memory_space=pltpu.VMEM)] * 3,
        out_specs=pl.BlockSpec(memory_space=pltpu.VMEM),
        scratch_shapes=[pltpu.VMEM((1024, 512), F32)],
        compiler_params=pltpu.CompilerParams(vmem_limit_bytes=24 * MIB),
        cost_estimate=pl.CostEstimate(
            flops=12 * 256 * 512 * 1024, bytes_accessed=2 * MIB, transcendentals=0
        ),
        name="cond_planes",
    )(jnp.asarray(table), home, away)


def response_kernel(ia_ref, ib_ref, *refs):
    waves, (w_ref, out_ref, rows_ref) = refs[:8], refs[8:]
    z = pl.program_id(0)
    mirrored = jnp.where(lax.rem(z, 16) == 0, 0.0, 1.0)

    @pl.when(z == 0)
    def _():
        out_ref[...] = jnp.zeros_like(out_ref)

    def density(home, away, v):
        hr, hi = home[v : v + 1], home[8 + v : 9 + v]
        ar, ai = away[:8], away[8:]
        return hr * ar + hi * ai, hr * ai - hi * ar

    for part in range(2):
        home_ref, away_ref, home_back_ref, away_back_ref = waves[part * 4 : part * 4 + 4]

        def one(k, carry):
            home, away = home_ref[0, k].astype(F32), away_ref[0, k].astype(F32)
            home_back = home_back_ref[0, k].astype(F32) * mirrored
            away_back = away_back_ref[0, k].astype(F32)
            at = (part * 4 + k) * 128
            for pair in range(4):
                pieces = []
                for v in (2 * pair, 2 * pair + 1):
                    real, imag = density(home, away, v)
                    real_back, imag_back = density(home_back, away_back, v)
                    pieces.append(
                        (
                            real + real_back,
                            imag - imag_back,
                            imag + imag_back,
                            real_back - real,
                        )
                    )
                even_re, odd_im, even_im, odd_re = (
                    jnp.concatenate(p, axis=0).astype(BF) for p in zip(*pieces)
                )
                here = pl.ds(pl.multiple_of(at + pair * 16, 16), 16)
                there = pl.ds(pl.multiple_of(at + 64 + pair * 16, 16), 16)
                rows_ref[here, :256] = even_re
                rows_ref[here, 256:] = odd_im
                rows_ref[there, :256] = even_im
                rows_ref[there, 256:] = odd_re
            return carry

        lax.fori_loop(0, 4, one, 0)
    out_ref[...] += dot(rows_ref[...], w_ref[0])


def response(place, home, away, screened):
    ia, ib = plane_slots(place)
    specs = []
    for part in range(2):
        for back in (False, True):
            for _ in range(2):

                def index(z, ia, ib, part=part, back=back):
                    plane = lax.rem(NZ - z, NZ) if back else z
                    return ((ia, ib)[part][plane], 0, 0, 0)

                specs.append(pl.BlockSpec((1, 4, 16, 256), index))
    waves = []
    for part in range(2):
        waves += [home[part], away[part], home[part], away[part]]
    return pl.pallas_call(
        response_kernel,
        grid_spec=pltpu.PrefetchScalarGridSpec(
            num_scalar_prefetch=2,
            grid=(HALF,),
            in_specs=specs + [pl.BlockSpec((1, 512, 256), lambda z, ia, ib: (z, 0, 0))],
            out_specs=pl.BlockSpec((1024, 256), lambda z, ia, ib: (0, 0)),
            scratch_shapes=[pltpu.VMEM((1024, 512), BF)],
        ),
        out_shape=jax.ShapeDtypeStruct((1024, 256), F32),
        compiler_params=pltpu.CompilerParams(vmem_limit_bytes=32 * MIB),
        cost_estimate=pl.CostEstimate(
            flops=2 * 1024 * 512 * 256 * HALF, bytes_accessed=9 * MIB, transcendentals=0
        ),
        name="valence_response",
    )(ia, ib, *waves, screened)


def block_kernel(cos_ref, sin_ref, x_ref, r_ref, out_ref):
    lane = lax.broadcasted_iota(jnp.int32, (1, 128), 1)
    first = lane < 64
    for k in range(8):
        x = x_ref[:, k * 128 : (k + 1) * 128]
        turned = pltpu.roll(x, 64, 1)
        turned = jnp.where(first, turned, -turned)
        cond = dot(cos_ref[...], x, precision=EXACT) + dot(sin_ref[...], turned, precision=EXACT)
        cond = (cond * NORM).astype(BF).astype(F32).T.astype(BF)
        rows = r_ref[k * 128 : (k + 1) * 128] * NORM
        top = rows.astype(BF)
        rest = (rows - top.astype(F32)).astype(BF)
        prod = dot(cond, top, ((1,), (1,))) + dot(cond, rest, ((1,), (1,)))
        swapped = pltpu.roll(prod[64:], 64, 1)
        both = prod[:64] + jnp.where(first, swapped, -swapped)
        even, odd = both[:32], both[32:]
        out_ref[:, 2 * k, :] = jnp.where(first, even, pltpu.roll(odd, 64, 1))
        out_ref[:, 2 * k + 1, :] = jnp.where(first, pltpu.roll(even, 64, 1), odd)


def kernel_blocks(cosine, sine, columns, rows):
    return pl.pallas_call(
        block_kernel,
        out_shape=jax.ShapeDtypeStruct((32, 16, 128), F32),
        in_specs=[pl.BlockSpec(memory_space=pltpu.VMEM)] * 4,
        out_specs=pl.BlockSpec(memory_space=pltpu.VMEM),
        compiler_params=pltpu.CompilerParams(vmem_limit_bytes=24 * MIB),
        cost_estimate=pl.CostEstimate(
            flops=24 * 256 * 256 * 1024, bytes_accessed=4 * MIB, transcendentals=0
        ),
        name="kernel_blocks",
    )(cosine, sine, columns, rows)


def line_tables(gmap, place):
    level = lax.dynamic_slice_in_dim(gmap, place * 256, 256) & (NZ - 1)
    column = jnp.arange(256, dtype=jnp.int32)
    angle = (level[:, None] * (column // 8)[None, :]) % NZ
    same = (column // NZ)[:, None] == (column % 8)[None, :]
    angle = angle.astype(F32) * (2.0 * math.pi / NZ)
    return jnp.where(same, jnp.cos(angle), 0.0), jnp.where(same, jnp.sin(angle), 0.0)


def on_device(wavefunctions, partner, gmap, screened):
    ka_place = lax.axis_index("ka")
    place = lax.axis_index("ga")
    owned = ka_place * 8 + jnp.arange(8, dtype=jnp.int32)
    source = (ka_place - jnp.arange(8, dtype=jnp.int32)) % 8
    slot_owner = (source[:, None] * 8 + jnp.arange(8, dtype=jnp.int32)[None, :]).reshape(64)

    waves = wavefunctions.reshape(8, 2, 2, 8, 256).transpose(0, 2, 1, 3, 4).reshape(8, 32, 256)
    slots = around_ka(waves)
    index = jnp.arange(PLANE, dtype=jnp.int32)
    negative = (NX - index // NY) % NX * NY + (NY - index % NY) % NY
    negative = jnp.where(place > NZ // 2, negative, index)
    flip = (index[:, None] == negative[None, :]).astype(BF)
    home_val = dot(waves[:, :16].reshape(128, 256), flip).astype(BF).reshape(8, 16, 256)
    home = gather_planes(home_val)

    wide = plane_transform(line_transform(screened, gmap))

    wanted = partner[owned]
    wanted_slot = jnp.argmax(wanted[:, None] == slot_owner[None, :], axis=1).astype(jnp.int32)
    away_val, away_cond = choose(slots, wanted_slot, flip)
    away = gather_planes(away_val)

    planes = cond_planes(waves[:, 16:], away_cond)
    columns = lax.all_to_all(planes, "ga", split_axis=0, concat_axis=0, tiled=True)
    cosine, sine = line_tables(gmap, place)

    rows = response(place, home, away, wide)
    blocks = kernel_blocks(cosine, sine, columns, rows)

    parts = lax.all_to_all(blocks, "ga", split_axis=0, concat_axis=0, tiled=True)
    mine = jnp.sum(parts, axis=0)
    everyone = jnp.stack(around_ka(mine)).reshape(64, 256)
    select = (partner[slot_owner][None, :] == owned[:, None]).astype(F32)
    mirror = jnp.dot(select, everyone, precision=EXACT).reshape(16, 128)
    lane = jnp.arange(128, dtype=jnp.int32)
    moved = lane // 64 * 64 + lane % 8 * 8 + lane // 8 % 8
    turn = (lane[:, None] == moved[None, :]).astype(F32)
    sign = jnp.where(jnp.arange(16) % 2 == 0, 1.0, -1.0).astype(F32)
    mirror = jnp.dot(mirror, turn, precision=EXACT) * sign[:, None]
    both = jnp.stack([mine, mirror])
    full = lax.all_to_all(
        jnp.broadcast_to(both[None], (32, 2, 16, 128)), "ga", split_axis=0, concat_axis=0, tiled=True
    )
    full = full.reshape(4, 8, 2, 8, 2, 2, 64)
    rows_out = full[:, :, 0].transpose(2, 3, 1, 0, 4, 5).reshape(8, 2, 4096)
    mirror_out = full[:, :, 1].transpose(2, 3, 0, 4, 1, 5).reshape(8, 2, 4096)
    return rows_out, mirror_out


def solution(mesh):
    in_specs = (P("ka", None, None, "ga", None), P(), P(), P("ga", None))
    out_specs = (P("ka", None, None), P("ka", None, None))
    return jax.shard_map(
        on_device, mesh=mesh, in_specs=in_specs, out_specs=out_specs, check_vma=False
    )
```

```python
import math

import jax
import jax.numpy as jnp
import numpy as np
from jax import lax
from jax.experimental import pallas as pl
from jax.experimental.pallas import tpu as pltpu
from jax.sharding import PartitionSpec as P

NX = 16
NY = 16
NZ = 32
NG = 8192
PLANE = NX * NY
HALF = NZ // 2 + 1
LINE_BLOCKS = 4
NORM = 1.0 / math.sqrt(NG)
EXACT = lax.Precision.HIGHEST
BF = jnp.bfloat16
F32 = jnp.float32
MIB = 1 << 20

SHAPE = (4, 4, 2)
XS = ((1, 0, 0), (3, 0, 0), (2, 0, 0))
YS = ((0, 1, 0), (0, 3, 0), (0, 2, 0))
ZS = ((0, 0, 1),)
SLOT = (0, 1, 3, 2)
LEVELS = [[place * 2 + z for place in range(16)] for z in range(2)]


def split_table(table):
    high = table.astype(np.float32).astype(BF)
    low = (table - high.astype(np.float64)).astype(np.float32).astype(BF)
    return high, low


def plane_angles():
    index = np.arange(PLANE)
    x, y = index // NY, index % NY
    turns = (np.outer(x, x) % NX) / NX + (np.outer(y, y) % NY) / NY
    return 2.0 * np.pi * turns


def line_angles():
    index = np.arange(NZ)
    return 2.0 * np.pi * (np.outer(index, index) % NZ) / NZ


def shifted(value, offset):
    pairs = []
    for source in range(32):
        place = (source // 8, source // 2 % 4, source % 2)
        x, y, z = ((a + b) % n for a, b, n in zip(place, offset, SHAPE))
        pairs.append((source, x * 8 + y * 2 + z))
    return lax.ppermute(value, "ga", pairs)


def spread(value, offsets):
    return jnp.stack([value] + [shifted(value, offset) for offset in offsets])


def around_ka(value):
    return [value] + [
        lax.ppermute(value, "ka", [(i, (i + d) % 8) for i in range(8)]) for d in range(1, 8)
    ]


def gather_planes(value):
    for offsets in (ZS, XS, YS):
        value = spread(value, offsets)
    return value.reshape((32,) + value.shape[3:])


def copies_to_all(value, count, axis, groups=None):
    copies = jnp.broadcast_to(value[None], (count,) + value.shape)
    return lax.all_to_all(
        copies, axis, split_axis=0, concat_axis=0, axis_index_groups=groups, tiled=True
    )


def gather_early(value):
    both = spread(value, ZS)
    full = lax.all_gather(both, "ga", axis_index_groups=LEVELS)
    return full.reshape((32,) + value.shape)


def plane_slots(place):
    z = jnp.arange(32, dtype=jnp.int32)
    slot = jnp.array(SLOT, dtype=jnp.int32)
    sx = slot[(place // 8 - z // 8) % 4]
    sy = slot[(place // 2 - z // 2) % 4]
    sz = (place - z) % 2
    return z // 2 * 2 + sz, (sy * 4 + sx) * 2 + sz


def dot(a, b, contract=((1,), (0,)), precision=None):
    return lax.dot_general(
        a, b, (contract, ((), ())), precision=precision, preferred_element_type=F32
    )


def line_kernel(gmap_ref, high_ref, low_ref, w_ref, y_ref):
    rows = 2 * HALF * 8
    keep = (lax.broadcasted_iota(jnp.int32, (rows, 256), 0) & 7) == (
        lax.broadcasted_iota(jnp.int32, (rows, 256), 1) >> 5
    )
    for b in range(LINE_BLOCKS):
        level = gmap_ref[b] & (NZ - 1)
        hot = (lax.broadcasted_iota(jnp.int32, (NZ, 256), 0) == level).astype(F32).astype(BF)
        block = w_ref[:, b * 256 : (b + 1) * 256]
        total = None
        for table in (high_ref, low_ref):
            picked = jnp.where(keep, dot(table[...], hot), 0.0).astype(BF)
            part = dot(picked, block, ((1,), (1,)))
            total = part if total is None else total + part
        y_ref[:, :, b * 8 : (b + 1) * 8, :] = total.reshape(2, HALF, 8, 256)


def line_transform(screened, gmap):
    angles = line_angles()[:HALF]
    table = np.stack([np.cos(angles), -np.sin(angles)])
    table = np.repeat(table.reshape(2 * HALF, NZ), 8, axis=0)
    high, low = split_table(table)
    rows = 2 * HALF * 8
    n = LINE_BLOCKS
    return pl.pallas_call(
        line_kernel,
        grid=(32 // n,),
        in_specs=[
            pl.BlockSpec((n, 1, 256), lambda b: (b, 0, 0)),
            pl.BlockSpec((rows, NZ), lambda b: (0, 0)),
            pl.BlockSpec((rows, NZ), lambda b: (0, 0)),
            pl.BlockSpec((256, n * 256), lambda b: (0, b)),
        ],
        out_specs=pl.BlockSpec((2, HALF, n * 8, 256), lambda b: (0, 0, b, 0)),
        out_shape=jax.ShapeDtypeStruct((2, HALF, PLANE, 256), F32),
        compiler_params=pltpu.CompilerParams(vmem_limit_bytes=32 * MIB),
        cost_estimate=pl.CostEstimate(
            flops=4 * rows * 256 * 8192, bytes_accessed=14 * MIB, transcendentals=0
        ),
        name="screened_line",
    )(gmap.reshape(32, 1, 256), jnp.asarray(high), jnp.asarray(low), screened)


def plane_kernel(high_ref, low_ref, y_ref, w_ref):
    real, imag = y_ref[0, 0], y_ref[1, 0]
    for odd in range(2):
        if odd:
            both = [real[:128] - real[128:], imag[:128] - imag[128:]]
        else:
            both = [real[:128] + real[128:], imag[:128] + imag[128:]]
        both = jnp.concatenate(both, axis=0)
        top = both.astype(BF)
        rest = (both - top.astype(F32)).astype(BF)
        high, low = high_ref[odd], low_ref[odd]
        prod = (dot(high, top) + (dot(high, rest) + dot(low, top))).astype(BF)
        for half in range(8):
            at = (2 * half + odd) * NY
            w_ref[0, at : at + NY] = prod[half * NY : (half + 1) * NY]
            w_ref[0, 256 + at : 256 + at + NY] = prod[128 + half * NY : 128 + (half + 1) * NY]


def plane_transform(lines):
    angles = plane_angles().reshape(NX, NY, PLANE)[:, :, :128]
    tables = []
    for odd in range(2):
        part = angles[odd::2].reshape(128, 128)
        cosine, sine = np.cos(part), np.sin(part)
        tables.append(np.block([[cosine, sine], [sine, -cosine]]))
    high, low = split_table(np.stack(tables))
    return pl.pallas_call(
        plane_kernel,
        grid=(HALF,),
        in_specs=[
            pl.BlockSpec((2, 256, 256), lambda z: (0, 0, 0)),
            pl.BlockSpec((2, 256, 256), lambda z: (0, 0, 0)),
            pl.BlockSpec((2, 1, 256, 256), lambda z: (0, z, 0, 0)),
        ],
        out_specs=pl.BlockSpec((1, 512, 256), lambda z: (z, 0, 0)),
        out_shape=jax.ShapeDtypeStruct((HALF, 512, 256), BF),
        compiler_params=pltpu.CompilerParams(vmem_limit_bytes=24 * MIB),
        cost_estimate=pl.CostEstimate(
            flops=12 * 256 * 256 * 256 * HALF, bytes_accessed=14 * MIB, transcendentals=0
        ),
        name="screened_plane",
    )(jnp.asarray(high), jnp.asarray(low), lines)


def choose_kernel(slot_ref, flip_ref, *refs):
    slots, (val_ref, cond_ref) = refs[:8], refs[8:]
    for m in range(8):
        wanted = slot_ref[m]
        for d in range(8):

            @pl.when(wanted // 8 == d)
            def _(m=m, d=d):
                row = slots[d][wanted % 8]
                val_ref[m] = dot(row[:16], flip_ref[...]).astype(BF)
                cond_ref[m] = row[16:]


def choose(slots, wanted, flip):
    shape = jax.ShapeDtypeStruct((8, 16, 256), BF)
    return pl.pallas_call(
        choose_kernel,
        in_specs=[pl.BlockSpec(memory_space=pltpu.SMEM)]
        + [pl.BlockSpec(memory_space=pltpu.VMEM)] * 9,
        out_specs=[pl.BlockSpec(memory_space=pltpu.VMEM)] * 2,
        out_shape=[shape, shape],
        compiler_params=pltpu.CompilerParams(vmem_limit_bytes=16 * MIB),
        name="partner_choice",
    )(wanted, flip, *slots)


def cond_kernel(table_ref, home_ref, away_ref, x_ref, rows_ref):
    for k in range(8):
        home, away = home_ref[k].astype(F32), away_ref[k].astype(F32)
        hr, hi = home[:8], home[8:]
        for place, band in enumerate((0, 2, 4, 6, 1, 3, 5, 7)):
            ar, ai = away[band : band + 1], away[8 + band : 9 + band]
            real = hr * ar + hi * ai
            imag = hr * ai - hi * ar
            at = k * 128 + place * 8
            rows_ref[at : at + 8, :256] = real
            rows_ref[at : at + 8, 256:] = imag
            rows_ref[at + 64 : at + 72, :256] = imag
            rows_ref[at + 64 : at + 72, 256:] = -real
    for k in range(8):
        x_ref[:, k * 128 : (k + 1) * 128] = dot(
            table_ref[...], rows_ref[k * 128 : (k + 1) * 128], ((1,), (1,)), EXACT
        )


def cond_planes(home, away):
    angles = plane_angles()
    table = np.concatenate([np.cos(angles), np.sin(angles)], axis=1).astype(np.float32)
    return pl.pallas_call(
        cond_kernel,
        out_shape=jax.ShapeDtypeStruct((256, 1024), F32),
        in_specs=[pl.BlockSpec(memory_space=pltpu.VMEM)] * 3,
        out_specs=pl.BlockSpec(memory_space=pltpu.VMEM),
        scratch_shapes=[pltpu.VMEM((1024, 512), F32)],
        compiler_params=pltpu.CompilerParams(vmem_limit_bytes=24 * MIB),
        cost_estimate=pl.CostEstimate(
            flops=12 * 256 * 512 * 1024, bytes_accessed=2 * MIB, transcendentals=0
        ),
        name="cond_planes",
    )(jnp.asarray(table), home, away)


def response_kernel(ih_ref, ia_ref, *refs):
    (home_ref, away_ref, home_back_ref, away_back_ref), (w_ref, out_ref, rows_ref) = refs[:4], refs[4:]
    z = pl.program_id(0)
    mirrored = jnp.where(lax.rem(z, 16) == 0, 0.0, 1.0)

    @pl.when(z == 0)
    def _():
        out_ref[...] = jnp.zeros_like(out_ref)

    def density(home, away, v):
        hr, hi = home[v : v + 1], home[8 + v : 9 + v]
        ar, ai = away[:8], away[8:]
        return hr * ar + hi * ai, hr * ai - hi * ar

    def one(k, carry):
        home, away = home_ref[0, k].astype(F32), away_ref[0, k].astype(F32)
        home_back = home_back_ref[0, k].astype(F32) * mirrored
        away_back = away_back_ref[0, k].astype(F32)
        at = k * 128
        for pair in range(4):
            pieces = []
            for v in (2 * pair, 2 * pair + 1):
                real, imag = density(home, away, v)
                real_back, imag_back = density(home_back, away_back, v)
                pieces.append(
                    (real + real_back, imag - imag_back, imag + imag_back, real_back - real)
                )
            even_re, odd_im, even_im, odd_re = (
                jnp.concatenate(p, axis=0).astype(BF) for p in zip(*pieces)
            )
            here = pl.ds(pl.multiple_of(at + pair * 16, 16), 16)
            there = pl.ds(pl.multiple_of(at + 64 + pair * 16, 16), 16)
            rows_ref[here, :256] = even_re
            rows_ref[here, 256:] = odd_im
            rows_ref[there, :256] = even_im
            rows_ref[there, 256:] = odd_re
        return carry

    lax.fori_loop(0, 8, one, 0)
    out_ref[...] += dot(rows_ref[...], w_ref[0])


def response(place, home, away, screened):
    ih, ia = plane_slots(place)

    def block(which, back):
        def index(z, ih, ia):
            plane = lax.rem(NZ - z, NZ) if back else z
            return ((ih, ia)[which][plane], 0, 0, 0)

        return pl.BlockSpec((1, 8, 16, 256), index)

    return pl.pallas_call(
        response_kernel,
        grid_spec=pltpu.PrefetchScalarGridSpec(
            num_scalar_prefetch=2,
            grid=(HALF,),
            in_specs=[
                block(0, False),
                block(1, False),
                block(0, True),
                block(1, True),
                pl.BlockSpec((1, 512, 256), lambda z, ih, ia: (z, 0, 0)),
            ],
            out_specs=pl.BlockSpec((1024, 256), lambda z, ih, ia: (0, 0)),
            scratch_shapes=[pltpu.VMEM((1024, 512), BF)],
        ),
        out_shape=jax.ShapeDtypeStruct((1024, 256), F32),
        compiler_params=pltpu.CompilerParams(vmem_limit_bytes=56 * MIB),
        cost_estimate=pl.CostEstimate(
            flops=2 * 1024 * 512 * 256 * HALF, bytes_accessed=9 * MIB, transcendentals=0
        ),
        name="valence_response",
    )(ih, ia, home, away, home, away, screened)


def spectrum_kernel(cos_ref, sin_ref, x_ref, out_ref):
    first = lax.broadcasted_iota(jnp.int32, (1, 128), 1) < 64
    for k in range(8):
        x = x_ref[:, k * 128 : (k + 1) * 128]
        turned = pltpu.roll(x, 64, 1)
        turned = jnp.where(first, turned, -turned)
        cond = dot(cos_ref[...], x, precision=EXACT) + dot(sin_ref[...], turned, precision=EXACT)
        cond = (cond * NORM).astype(BF).astype(F32).T
        out_ref[k * 128 : (k + 1) * 128] = cond.astype(BF)


def cond_spectrum(cosine, sine, columns):
    return pl.pallas_call(
        spectrum_kernel,
        out_shape=jax.ShapeDtypeStruct((1024, 256), BF),
        in_specs=[pl.BlockSpec(memory_space=pltpu.VMEM)] * 3,
        out_specs=pl.BlockSpec(memory_space=pltpu.VMEM),
        compiler_params=pltpu.CompilerParams(vmem_limit_bytes=24 * MIB),
        cost_estimate=pl.CostEstimate(
            flops=24 * 256 * 256 * 1024, bytes_accessed=2 * MIB, transcendentals=0
        ),
        name="cond_spectrum",
    )(cosine, sine, columns)


def block_kernel(cond_ref, r_ref, out_ref):
    first = lax.broadcasted_iota(jnp.int32, (1, 128), 1) < 64
    for k in range(8):
        cond = cond_ref[k * 128 : (k + 1) * 128]
        rows = r_ref[k * 128 : (k + 1) * 128] * NORM
        top = rows.astype(BF)
        rest = (rows - top.astype(F32)).astype(BF)
        prod = dot(cond, top, ((1,), (1,))) + dot(cond, rest, ((1,), (1,)))
        swapped = pltpu.roll(prod[64:], 64, 1)
        both = prod[:64] + jnp.where(first, swapped, -swapped)
        even, odd = both[:32], both[32:]
        out_ref[:, 2 * k, :] = jnp.where(first, even, pltpu.roll(odd, 64, 1))
        out_ref[:, 2 * k + 1, :] = jnp.where(first, pltpu.roll(even, 64, 1), odd)


def kernel_blocks(cond, rows):
    return pl.pallas_call(
        block_kernel,
        out_shape=jax.ShapeDtypeStruct((32, 16, 128), F32),
        in_specs=[pl.BlockSpec(memory_space=pltpu.VMEM)] * 2,
        out_specs=pl.BlockSpec(memory_space=pltpu.VMEM),
        compiler_params=pltpu.CompilerParams(vmem_limit_bytes=24 * MIB),
        cost_estimate=pl.CostEstimate(
            flops=4 * 128 * 256 * 1024, bytes_accessed=2 * MIB, transcendentals=0
        ),
        name="kernel_blocks",
    )(cond, rows)


def line_tables(gmap, place):
    level = lax.dynamic_slice_in_dim(gmap, place * 256, 256) & (NZ - 1)
    column = jnp.arange(256, dtype=jnp.int32)
    angle = (level[:, None] * (column // 8)[None, :]) % NZ
    same = (column // NZ)[:, None] == (column % 8)[None, :]
    angle = angle.astype(F32) * (2.0 * math.pi / NZ)
    return jnp.where(same, jnp.cos(angle), 0.0), jnp.where(same, jnp.sin(angle), 0.0)


def on_device(wavefunctions, partner, gmap, screened):
    ka_place = lax.axis_index("ka")
    place = lax.axis_index("ga")
    owned = ka_place * 8 + jnp.arange(8, dtype=jnp.int32)
    source = (ka_place - jnp.arange(8, dtype=jnp.int32)) % 8
    slot_owner = (source[:, None] * 8 + jnp.arange(8, dtype=jnp.int32)[None, :]).reshape(64)

    waves = wavefunctions.reshape(8, 2, 2, 8, 256).transpose(0, 2, 1, 3, 4).reshape(8, 32, 256)
    slots = around_ka(waves)
    index = jnp.arange(PLANE, dtype=jnp.int32)
    negative = (NX - index // NY) % NX * NY + (NY - index % NY) % NY
    negative = jnp.where(place > NZ // 2, negative, index)
    flip = (index[:, None] == negative[None, :]).astype(BF)
    home_val = dot(waves[:, :16].reshape(128, 256), flip).astype(BF).reshape(8, 16, 256)
    home = gather_early(home_val)

    lines = line_transform(screened, gmap)

    wanted = partner[owned]
    wanted_slot = jnp.argmax(wanted[:, None] == slot_owner[None, :], axis=1).astype(jnp.int32)
    away_val, away_cond = choose(slots, wanted_slot, flip)
    lines, away_val, away_cond = lax.optimization_barrier((lines, away_val, away_cond))
    away = gather_planes(away_val)

    planes = cond_planes(waves[:, 16:], away_cond)
    columns = lax.all_to_all(planes, "ga", split_axis=0, concat_axis=0, tiled=True)
    wide = plane_transform(lines)
    cond = cond_spectrum(*line_tables(gmap, place), columns)

    blocks = kernel_blocks(cond, response(place, home, away, wide))

    parts = lax.all_to_all(blocks, "ga", split_axis=0, concat_axis=0, tiled=True)
    mine = jnp.sum(parts, axis=0)
    everyone = copies_to_all(mine, 8, "ka").reshape(64, 256)
    select = (partner[None, :] == owned[:, None]).astype(F32)
    mirror = jnp.dot(select, everyone, precision=EXACT).reshape(16, 128)
    lane = jnp.arange(128, dtype=jnp.int32)
    moved = lane // 64 * 64 + lane % 8 * 8 + lane // 8 % 8
    turn = (lane[:, None] == moved[None, :]).astype(F32)
    sign = jnp.where(jnp.arange(16) % 2 == 0, 1.0, -1.0).astype(F32)
    mirror = jnp.dot(mirror, turn, precision=EXACT) * sign[:, None]
    both = spread(jnp.stack([mine, mirror]), ZS)
    full = copies_to_all(both, 16, "ga", LEVELS)
    full = jnp.where(place % 2 == 0, full, full[:, ::-1])
    full = full.reshape(4, 8, 2, 8, 2, 2, 64)
    rows_out = full[:, :, 0].transpose(2, 3, 1, 0, 4, 5).reshape(8, 2, 4096)
    mirror_out = full[:, :, 1].transpose(2, 3, 0, 4, 1, 5).reshape(8, 2, 4096)
    return rows_out, mirror_out


def solution(mesh):
    in_specs = (P("ka", None, None, "ga", None), P(), P(), P("ga", None))
    out_specs = (P("ka", None, None), P("ka", None, None))
    return jax.shard_map(
        on_device, mesh=mesh, in_specs=in_specs, out_specs=out_specs, check_vma=False
    )
```

```python
import functools
import math

import jax
import jax.numpy as jnp
import numpy as np
from jax import lax
from jax.experimental import pallas as pl
from jax.experimental.pallas import tpu as pltpu
from jax.sharding import Mesh
from jax.sharding import PartitionSpec as P

NX = 16
NY = 16
NZ = 32
NG = 8192
PLANE = NX * NY
HALF = NZ // 2 + 1
LINE_BLOCKS = 4
NORM = 1.0 / math.sqrt(NG)
EXACT = lax.Precision.HIGHEST
BF = jnp.bfloat16
F32 = jnp.float32
MIB = 1 << 20

AXES = ("zl", "co", "x", "y", "zh")
SIZES = (4, 2, 4, 4, 2)
SIZE = dict(zip(AXES, SIZES))
KA = ("zl", "co")
GA = ("x", "y", "zh")
VMEM = 48 * MIB


def split_table(table):
    high = table.astype(np.float32).astype(BF)
    low = (table - high.astype(np.float64)).astype(np.float32).astype(BF)
    return high, low


def plane_angles():
    index = np.arange(PLANE)
    x, y = index // NY, index % NY
    turns = (np.outer(x, x) % NX) / NX + (np.outer(y, y) % NY) / NY
    return 2.0 * np.pi * turns


def line_angles():
    index = np.arange(NZ)
    return 2.0 * np.pi * (np.outer(index, index) % NZ) / NZ


def turned(value, axis, step):
    size = SIZE[axis]
    return lax.ppermute(value, axis, [(i, (i + step) % size) for i in range(size)])


def spread(value, axis):
    return jnp.stack([value] + [turned(value, axis, d) for d in range(1, SIZE[axis])])


def copies_to_all(value, axes):
    count = math.prod(SIZE[axis] for axis in axes)
    copies = jnp.broadcast_to(value[None], (count,) + value.shape)
    return lax.all_to_all(copies, axes, split_axis=0, concat_axis=0, tiled=True)


def dot(a, b, contract=((1,), (0,)), precision=None):
    return lax.dot_general(
        a, b, (contract, ((), ())), precision=precision, preferred_element_type=F32
    )


def line_kernel(gmap_ref, high_ref, low_ref, w_ref, y_ref):
    rows = 2 * HALF * 8
    keep = (lax.broadcasted_iota(jnp.int32, (rows, 256), 0) & 7) == (
        lax.broadcasted_iota(jnp.int32, (rows, 256), 1) >> 5
    )
    for b in range(LINE_BLOCKS):
        level = gmap_ref[b] & (NZ - 1)
        hot = (lax.broadcasted_iota(jnp.int32, (NZ, 256), 0) == level).astype(F32).astype(BF)
        block = w_ref[:, b * 256 : (b + 1) * 256]
        total = None
        for table in (high_ref, low_ref):
            picked = jnp.where(keep, dot(table[...], hot), 0.0).astype(BF)
            part = dot(picked, block, ((1,), (1,)))
            total = part if total is None else total + part
        y_ref[:, :, b * 8 : (b + 1) * 8, :] = total.reshape(2, HALF, 8, 256)


def line_transform(screened, gmap):
    angles = line_angles()[:HALF]
    table = np.stack([np.cos(angles), -np.sin(angles)])
    table = np.repeat(table.reshape(2 * HALF, NZ), 8, axis=0)
    high, low = split_table(table)
    rows = 2 * HALF * 8
    n = LINE_BLOCKS
    return pl.pallas_call(
        line_kernel,
        grid=(32 // n,),
        in_specs=[
            pl.BlockSpec((n, 1, 256), lambda b: (b, 0, 0)),
            pl.BlockSpec((rows, NZ), lambda b: (0, 0)),
            pl.BlockSpec((rows, NZ), lambda b: (0, 0)),
            pl.BlockSpec((256, n * 256), lambda b: (0, b)),
        ],
        out_specs=pl.BlockSpec((2, HALF, n * 8, 256), lambda b: (0, 0, b, 0)),
        out_shape=jax.ShapeDtypeStruct((2, HALF, PLANE, 256), F32),
        compiler_params=pltpu.CompilerParams(vmem_limit_bytes=VMEM),
        cost_estimate=pl.CostEstimate(
            flops=4 * rows * 256 * 8192, bytes_accessed=14 * MIB, transcendentals=0
        ),
        name="screened_line",
    )(gmap.reshape(32, 1, 256), jnp.asarray(high), jnp.asarray(low), screened)


def plane_kernel(high_ref, low_ref, y_ref, w_ref):
    real, imag = y_ref[0, 0], y_ref[1, 0]
    for odd in range(2):
        if odd:
            both = [real[:128] - real[128:], imag[:128] - imag[128:]]
        else:
            both = [real[:128] + real[128:], imag[:128] + imag[128:]]
        both = jnp.concatenate(both, axis=0)
        top = both.astype(BF)
        rest = (both - top.astype(F32)).astype(BF)
        high, low = high_ref[odd], low_ref[odd]
        prod = (dot(high, top) + (dot(high, rest) + dot(low, top))).astype(BF)
        for half in range(8):
            at = (2 * half + odd) * NY
            w_ref[0, at : at + NY] = prod[half * NY : (half + 1) * NY]
            w_ref[0, 256 + at : 256 + at + NY] = prod[128 + half * NY : 128 + (half + 1) * NY]


def plane_transform(lines):
    angles = plane_angles().reshape(NX, NY, PLANE)[:, :, :128]
    tables = []
    for odd in range(2):
        part = angles[odd::2].reshape(128, 128)
        cosine, sine = np.cos(part), np.sin(part)
        tables.append(np.block([[cosine, sine], [sine, -cosine]]))
    high, low = split_table(np.stack(tables))
    return pl.pallas_call(
        plane_kernel,
        grid=(HALF,),
        in_specs=[
            pl.BlockSpec((2, 256, 256), lambda z: (0, 0, 0)),
            pl.BlockSpec((2, 256, 256), lambda z: (0, 0, 0)),
            pl.BlockSpec((2, 1, 256, 256), lambda z: (0, z, 0, 0)),
        ],
        out_specs=pl.BlockSpec((1, 512, 256), lambda z: (z, 0, 0)),
        out_shape=jax.ShapeDtypeStruct((HALF, 512, 256), BF),
        compiler_params=pltpu.CompilerParams(vmem_limit_bytes=VMEM),
        cost_estimate=pl.CostEstimate(
            flops=12 * 256 * 256 * 256 * HALF, bytes_accessed=14 * MIB, transcendentals=0
        ),
        name="screened_plane",
    )(jnp.asarray(high), jnp.asarray(low), lines)


def choose_kernel(partner_ref, place_ref, flip_ref, near_ref, far_ref, val_ref, cond_ref):
    level, core = place_ref[0], place_ref[1]
    for m in range(8):
        wanted = partner_ref[(level * 2 + core) * 8 + m]
        back = (level - wanted // 16) & 3
        at = back * 8 + (wanted & 7)
        near = (wanted // 8) % 2 == core

        def take(ref, m=m, at=at):
            row = ref[at]
            val_ref[m] = dot(row[:16], flip_ref[...]).astype(BF)
            cond_ref[m] = row[16:]

        pl.when(near)(functools.partial(take, near_ref))
        pl.when(jnp.logical_not(near))(functools.partial(take, far_ref))


def choose(partner, near, far, flip):
    shape = jax.ShapeDtypeStruct((8, 16, 256), BF)
    place = jnp.stack([lax.axis_index("zl"), lax.axis_index("co")]).astype(jnp.int32)
    return pl.pallas_call(
        choose_kernel,
        in_specs=[pl.BlockSpec(memory_space=pltpu.SMEM)] * 2
        + [pl.BlockSpec(memory_space=pltpu.VMEM)] * 3,
        out_specs=[pl.BlockSpec(memory_space=pltpu.VMEM)] * 2,
        out_shape=[shape, shape],
        compiler_params=pltpu.CompilerParams(vmem_limit_bytes=16 * MIB),
        name="partner_choice",
    )(partner, place, flip, near, far)


def cond_kernel(table_ref, home_ref, away_ref, x_ref, rows_ref):
    for k in range(8):
        home, away = home_ref[k].astype(F32), away_ref[k].astype(F32)
        hr, hi = home[:8], home[8:]
        for place, band in enumerate((0, 2, 4, 6, 1, 3, 5, 7)):
            ar, ai = away[band : band + 1], away[8 + band : 9 + band]
            real = hr * ar + hi * ai
            imag = hr * ai - hi * ar
            at = k * 128 + place * 8
            rows_ref[at : at + 8, :256] = real
            rows_ref[at : at + 8, 256:] = imag
            rows_ref[at + 64 : at + 72, :256] = imag
            rows_ref[at + 64 : at + 72, 256:] = -real
    for k in range(8):
        x_ref[:, k * 128 : (k + 1) * 128] = dot(
            table_ref[...], rows_ref[k * 128 : (k + 1) * 128], ((1,), (1,)), EXACT
        )


def cond_planes(home, away):
    angles = plane_angles()
    table = np.concatenate([np.cos(angles), np.sin(angles)], axis=1).astype(np.float32)
    return pl.pallas_call(
        cond_kernel,
        out_shape=jax.ShapeDtypeStruct((256, 1024), F32),
        in_specs=[pl.BlockSpec(memory_space=pltpu.VMEM)] * 3,
        out_specs=pl.BlockSpec(memory_space=pltpu.VMEM),
        scratch_shapes=[pltpu.VMEM((1024, 512), F32)],
        compiler_params=pltpu.CompilerParams(vmem_limit_bytes=24 * MIB),
        cost_estimate=pl.CostEstimate(
            flops=12 * 256 * 512 * 1024, bytes_accessed=2 * MIB, transcendentals=0
        ),
        name="cond_planes",
    )(jnp.asarray(table), home, away)


def build_rows(rows_ref, waves, mirrored):
    home_ref, away_ref, home_back_ref, away_back_ref = waves

    def density(home, away, v):
        hr, hi = home[v : v + 1], home[8 + v : 9 + v]
        ar, ai = away[:8], away[8:]
        return hr * ar + hi * ai, hr * ai - hi * ar

    for k in range(8):
        home, away = home_ref[0, k].astype(F32), away_ref[0, k].astype(F32)
        home_back, away_back = home_back_ref[0, k].astype(F32), away_back_ref[0, k].astype(F32)
        if mirrored is not None:
            home_back = home_back * mirrored
        for pair in range(4):
            pieces = []
            for v in (2 * pair, 2 * pair + 1):
                real, imag = density(home, away, v)
                real_back, imag_back = density(home_back, away_back, v)
                pieces.append(
                    (real + real_back, imag - imag_back, imag + imag_back, real_back - real)
                )
            even_re, odd_im, even_im, odd_re = (
                jnp.concatenate(p, axis=0).astype(BF) for p in zip(*pieces)
            )
            at = k * 128 + pair * 16
            rows_ref[at : at + 16, :256] = even_re
            rows_ref[at : at + 16, 256:] = odd_im
            rows_ref[at + 64 : at + 80, :256] = even_im
            rows_ref[at + 64 : at + 80, 256:] = odd_re


def response_kernel(place_ref, *refs):
    first_waves, second_waves = refs[:4], refs[4:8]
    before_ref, w_ref, cond_ref, out_ref, sum_ref, first_ref, second_ref = refs[8:]
    step = pl.program_id(0)
    mirrored = jnp.where(step % 8 == 0, 0.0, 1.0)
    before = dot(second_ref[...], before_ref[0])
    build_rows(first_ref, first_waves, mirrored)
    total = jnp.where(step == 0, 0.0, sum_ref[...] + before)
    total = total + dot(first_ref[...], w_ref[0])
    build_rows(second_ref, second_waves, None)
    sum_ref[...] = total

    @pl.when(step == HALF // 2)
    def _():
        low = lax.broadcasted_iota(jnp.int32, (1, 128), 1) < 64
        for k in range(8):
            cond = cond_ref[k * 128 : (k + 1) * 128]
            rows = sum_ref[k * 128 : (k + 1) * 128] * NORM
            top = rows.astype(BF)
            rest = (rows - top.astype(F32)).astype(BF)
            prod = dot(cond, top, ((1,), (1,))) + dot(cond, rest, ((1,), (1,)))
            swapped = pltpu.roll(prod[64:], 64, 1)
            both = prod[:64] + jnp.where(low, swapped, -swapped)
            even, odd = both[:32], both[32:]
            real = jnp.where(low, even, pltpu.roll(odd, 64, 1))
            imag = jnp.where(low, pltpu.roll(even, 64, 1), odd)
            out_ref[:, 2 * k, :] = real
            out_ref[:, 2 * k + 1, :] = imag


def response(place, home, away, screened, cond):
    def block(which, second, back):
        def index(step, place_ref):
            z = jnp.minimum(2 * step + second, HALF - 1)
            z = (NZ - z) & (NZ - 1) if back else z
            place = place_ref[0]
            level = (place ^ z) & 1
            if which == 0:
                return ((z & 30) + level, 0, 0, 0)
            x = ((place >> 3) - (z >> 3)) & 3
            y = ((place >> 1) - (z >> 1)) & 3
            return ((y * 4 + x) * 2 + level, 0, 0, 0)

        return pl.BlockSpec((1, 8, 16, 256), index)

    waves = [block(w, s, b) for s in range(2) for b in (False, True) for w in range(2)]
    return pl.pallas_call(
        response_kernel,
        grid_spec=pltpu.PrefetchScalarGridSpec(
            num_scalar_prefetch=1,
            grid=(HALF // 2 + 1,),
            in_specs=waves
            + [
                pl.BlockSpec((1, 512, 256), lambda i, p: (jnp.maximum(2 * i - 1, 0), 0, 0)),
                pl.BlockSpec((1, 512, 256), lambda i, p: (2 * i, 0, 0)),
                pl.BlockSpec((1024, 256), lambda i, p: (0, 0)),
            ],
            out_specs=pl.BlockSpec((32, 16, 128), lambda i, p: (0, 0, 0)),
            scratch_shapes=[
                pltpu.VMEM((1024, 256), F32),
                pltpu.VMEM((1024, 512), BF),
                pltpu.VMEM((1024, 512), BF),
            ],
        ),
        out_shape=jax.ShapeDtypeStruct((32, 16, 128), F32),
        compiler_params=pltpu.CompilerParams(vmem_limit_bytes=VMEM),
        cost_estimate=pl.CostEstimate(
            flops=2 * 1024 * 512 * 256 * HALF, bytes_accessed=9 * MIB, transcendentals=0
        ),
        name="valence_response",
    )(place.reshape(1), *([home, away] * 4), screened, screened, cond)


def spectrum_kernel(cos_ref, sin_ref, x_ref, out_ref):
    first = lax.broadcasted_iota(jnp.int32, (1, 128), 1) < 64
    for k in range(8):
        x = x_ref[:, k * 128 : (k + 1) * 128]
        turned = pltpu.roll(x, 64, 1)
        turned = jnp.where(first, turned, -turned)
        cond = dot(cos_ref[...], x, precision=EXACT) + dot(sin_ref[...], turned, precision=EXACT)
        cond = (cond * NORM).astype(BF).astype(F32).T
        out_ref[k * 128 : (k + 1) * 128] = cond.astype(BF)


def cond_spectrum(cosine, sine, columns):
    return pl.pallas_call(
        spectrum_kernel,
        out_shape=jax.ShapeDtypeStruct((1024, 256), BF),
        in_specs=[pl.BlockSpec(memory_space=pltpu.VMEM)] * 3,
        out_specs=pl.BlockSpec(memory_space=pltpu.VMEM),
        compiler_params=pltpu.CompilerParams(vmem_limit_bytes=24 * MIB),
        cost_estimate=pl.CostEstimate(
            flops=24 * 256 * 256 * 1024, bytes_accessed=2 * MIB, transcendentals=0
        ),
        name="cond_spectrum",
    )(cosine, sine, columns)


def line_tables(gmap, place):
    level = lax.dynamic_slice_in_dim(gmap, place * 256, 256) & (NZ - 1)
    column = jnp.arange(256, dtype=jnp.int32)
    angle = (level[:, None] * (column // 8)[None, :]) % NZ
    same = (column // NZ)[:, None] == (column % 8)[None, :]
    angle = angle.astype(F32) * (2.0 * math.pi / NZ)
    return jnp.where(same, jnp.cos(angle), 0.0), jnp.where(same, jnp.sin(angle), 0.0)


def on_device(wavefunctions, partner, gmap, screened):
    ka_place = lax.axis_index(KA)
    place = lax.axis_index(GA)
    owned = ka_place * 8 + jnp.arange(8, dtype=jnp.int32)

    waves = wavefunctions.reshape(8, 2, 2, 8, 256).transpose(0, 2, 1, 3, 4).reshape(8, 32, 256)
    near = spread(waves, "zl").reshape(32, 32, 256)
    far = turned(near, "co", 1)

    index = jnp.arange(PLANE, dtype=jnp.int32)
    negative = (NX - index // NY) % NX * NY + (NY - index % NY) % NY
    negative = jnp.where(place > NZ // 2, negative, index)
    flip = (index[:, None] == negative[None, :]).astype(BF)
    home_val = dot(waves[:, :16].reshape(128, 256), flip).astype(BF).reshape(8, 16, 256)
    home = lax.all_gather(spread(home_val, "zh"), ("x", "y")).reshape(32, 8, 16, 256)

    lines = line_transform(screened, gmap)

    away_val, away_cond = choose(partner, near, far, flip)
    away = spread(spread(away_val, "zh"), "x")
    planes = cond_planes(waves[:, 16:], away_cond)
    away, planes, lines = lax.optimization_barrier((away, planes, lines))
    columns = lax.all_to_all(planes, GA, split_axis=0, concat_axis=0, tiled=True)
    away = spread(away, "y").reshape(32, 8, 16, 256)
    wide = plane_transform(lines)
    cond = cond_spectrum(*line_tables(gmap, place), columns)

    blocks = response(place, home, away, wide, cond)

    parts = lax.all_to_all(blocks, ("x", "y"), split_axis=0, concat_axis=0, tiled=True)
    mine = jnp.sum(parts.reshape(16, 2, 16, 128), axis=0)
    mine = mine + turned(mine, "zh", 1)
    everyone = copies_to_all(mine, KA)
    everyone = everyone.reshape(8, 2, 8, 256).transpose(0, 2, 1, 3).reshape(64, 512)
    select = (partner[None, :] == owned[:, None]).astype(F32)
    mirror = jnp.dot(select, everyone, precision=EXACT)
    mirror = mirror.reshape(8, 2, 2, 128).transpose(1, 0, 2, 3).reshape(32, 128)
    lane = jnp.arange(128, dtype=jnp.int32)
    moved = lane // 64 * 64 + lane % 8 * 8 + lane // 8 % 8
    turn = (lane[:, None] == moved[None, :]).astype(F32)
    sign = jnp.where(jnp.arange(32) % 2 == 0, 1.0, -1.0).astype(F32)
    mirror = jnp.dot(mirror, turn, precision=EXACT) * sign[:, None]
    full = copies_to_all(jnp.stack([mine.reshape(32, 128), mirror]), ("x", "y"))
    full = full.reshape(4, 4, 2, 2, 8, 2, 2, 64)
    rows_out = full[:, :, 0].transpose(3, 4, 1, 2, 0, 5, 6).reshape(8, 2, 4096)
    mirror_out = full[:, :, 1].transpose(3, 4, 0, 5, 1, 2, 6).reshape(8, 2, 4096)
    return rows_out, mirror_out


def solution(mesh):
    fine = Mesh(mesh.devices.reshape(SIZES), AXES)
    in_specs = (P(KA, None, None, GA, None), P(), P(), P(GA, None))
    out_specs = (P(KA, None, None), P(KA, None, None))
    return jax.shard_map(
        on_device, mesh=fine, in_specs=in_specs, out_specs=out_specs, check_vma=False
    )
```

```python
import functools
import math

import jax
import jax.numpy as jnp
import numpy as np
from jax import lax
from jax.experimental import pallas as pl
from jax.experimental.pallas import tpu as pltpu
from jax.sharding import Mesh
from jax.sharding import PartitionSpec as P

NX = 16
NY = 16
NZ = 32
NG = 8192
PLANE = NX * NY
HALF = NZ // 2 + 1
LINE_BLOCKS = 4
LINE_STEPS = 32 // LINE_BLOCKS
LINE_ROWS = 48
NORM = 1.0 / math.sqrt(NG)
EXACT = lax.Precision.HIGHEST
BF = jnp.bfloat16
F32 = jnp.float32
MIB = 1 << 20

AXES = ("zl", "co", "x", "y", "zh")
SIZES = (4, 2, 4, 4, 2)
SIZE = dict(zip(AXES, SIZES))
KA = ("zl", "co")
GA = ("x", "y", "zh")


def split_table(table):
    high = table.astype(np.float32).astype(BF)
    low = (table - high.astype(np.float64)).astype(np.float32).astype(BF)
    return high, low


def plane_angles():
    index = np.arange(PLANE)
    x, y = index // NY, index % NY
    turns = (np.outer(x, x) % NX) / NX + (np.outer(y, y) % NY) / NY
    return 2.0 * np.pi * turns


def line_angles():
    index = np.arange(NZ)
    return 2.0 * np.pi * (np.outer(index, index) % NZ) / NZ


def turned(value, axis, step):
    size = SIZE[axis]
    return lax.ppermute(value, axis, [(i, (i + step) % size) for i in range(size)])


def spread(value, axis):
    return jnp.stack([value] + [turned(value, axis, d) for d in range(1, SIZE[axis])])


def copies_to_all(value, axes):
    count = math.prod(SIZE[axis] for axis in axes)
    copies = jnp.broadcast_to(value[None], (count,) + value.shape)
    return lax.all_to_all(copies, axes, split_axis=0, concat_axis=0, tiled=True)


def dot(a, b, contract=((1,), (0,)), precision=None):
    return lax.dot_general(
        a, b, (contract, ((), ())), precision=precision, preferred_element_type=F32
    )


def screened_kernel(gmap_ref, line_ref, high_ref, low_ref, w_ref, out_ref, lines_ref):
    step = pl.program_id(0)

    @pl.when(step < LINE_STEPS)
    def _():
        rows = 2 * HALF
        keep = lax.broadcasted_iota(jnp.int32, (1, 8, 256), 1) == (
            lax.broadcasted_iota(jnp.int32, (1, 8, 256), 2) >> 5
        )
        for b in range(LINE_BLOCKS):
            level = gmap_ref[b] & (NZ - 1)
            hot = (lax.broadcasted_iota(jnp.int32, (NZ, 256), 0) == level).astype(F32).astype(BF)
            picked = dot(line_ref[...], hot)
            tables = []
            for at in (0, LINE_ROWS):
                wide = jnp.broadcast_to(picked[at : at + rows][:, None, :], (rows, 8, 256))
                tables.append(jnp.where(keep, wide, 0.0).reshape(rows * 8, 256).astype(BF))
            block = w_ref[:, b * 256 : (b + 1) * 256]
            both = dot(jnp.concatenate(tables, axis=0), block, ((1,), (1,)))
            total = both[: rows * 8] + both[rows * 8 :]
            at = pl.multiple_of((step * LINE_BLOCKS + b) * 8, 8)
            lines_ref[:, pl.ds(at, 8), :] = total.reshape(rows, 8, 256)

    @pl.when(step >= LINE_STEPS)
    def _():
        z = step - LINE_STEPS
        real, imag = lines_ref[z], lines_ref[HALF + z]
        for odd in range(2):
            if odd:
                both = [real[:128] - real[128:], imag[:128] - imag[128:]]
            else:
                both = [real[:128] + real[128:], imag[:128] + imag[128:]]
            both = jnp.concatenate(both, axis=0)
            top = both.astype(BF)
            rest = (both - top.astype(F32)).astype(BF)
            high, low = high_ref[odd], low_ref[odd]
            prod = (dot(high, top) + (dot(high, rest) + dot(low, top))).astype(BF)
            for half in range(8):
                at = (2 * half + odd) * NY
                out_ref[0, at : at + NY] = prod[half * NY : (half + 1) * NY]
                out_ref[0, 256 + at : 256 + at + NY] = prod[128 + half * NY : 144 + half * NY]


def screened_transform(screened, gmap):
    angles = line_angles()[:HALF]
    table = np.concatenate([np.cos(angles), -np.sin(angles)], axis=0)
    padding = np.zeros((LINE_ROWS - 2 * HALF, NZ), BF)
    line = np.concatenate([x for part in split_table(table) for x in (part, padding)], axis=0)
    angles = plane_angles().reshape(NX, NY, PLANE)[:, :, :128]
    tables = []
    for odd in range(2):
        part = angles[odd::2].reshape(128, 128)
        cosine, sine = np.cos(part), np.sin(part)
        tables.append(np.block([[cosine, sine], [sine, -cosine]]))
    high, low = split_table(np.stack(tables))
    n = LINE_BLOCKS
    last = LINE_STEPS - 1
    return pl.pallas_call(
        screened_kernel,
        grid=(LINE_STEPS + HALF,),
        in_specs=[
            pl.BlockSpec((n, 1, 256), lambda i: (jnp.minimum(i, last), 0, 0)),
            pl.BlockSpec((2 * LINE_ROWS, NZ), lambda i: (0, 0)),
            pl.BlockSpec((2, 256, 256), lambda i: (0, 0, 0)),
            pl.BlockSpec((2, 256, 256), lambda i: (0, 0, 0)),
            pl.BlockSpec((256, n * 256), lambda i: (0, jnp.minimum(i, last))),
        ],
        out_specs=pl.BlockSpec((1, 512, 256), lambda i: (jnp.maximum(i - LINE_STEPS, 0), 0, 0)),
        out_shape=jax.ShapeDtypeStruct((HALF, 512, 256), BF),
        scratch_shapes=[pltpu.VMEM((2 * HALF, PLANE, 256), F32)],
        compiler_params=pltpu.CompilerParams(vmem_limit_bytes=40 * MIB),
        cost_estimate=pl.CostEstimate(
            flops=12 * 256 * 256 * 256 * HALF, bytes_accessed=9 * MIB, transcendentals=0
        ),
        name="screened_transform",
    )(gmap.reshape(32, 1, 256), jnp.asarray(line), jnp.asarray(high), jnp.asarray(low), screened)


def choose_kernel(partner_ref, place_ref, flip_ref, near_ref, far_ref, val_ref, cond_ref):
    level, core = place_ref[0], place_ref[1]
    for m in range(8):
        wanted = partner_ref[(level * 2 + core) * 8 + m]
        back = (level - wanted // 16) & 3
        at = back * 8 + (wanted & 7)
        near = (wanted // 8) % 2 == core

        def take(ref, m=m, at=at):
            row = ref[at]
            val_ref[m] = dot(row[:16], flip_ref[...]).astype(BF)
            cond_ref[m] = row[16:]

        pl.when(near)(functools.partial(take, near_ref))
        pl.when(jnp.logical_not(near))(functools.partial(take, far_ref))


def choose(partner, near, far, flip):
    shape = jax.ShapeDtypeStruct((8, 16, 256), BF)
    place = jnp.stack([lax.axis_index("zl"), lax.axis_index("co")]).astype(jnp.int32)
    return pl.pallas_call(
        choose_kernel,
        in_specs=[pl.BlockSpec(memory_space=pltpu.SMEM)] * 2
        + [pl.BlockSpec(memory_space=pltpu.VMEM)] * 3,
        out_specs=[pl.BlockSpec(memory_space=pltpu.VMEM)] * 2,
        out_shape=[shape, shape],
        compiler_params=pltpu.CompilerParams(vmem_limit_bytes=16 * MIB),
        name="partner_choice",
    )(partner, place, flip, near, far)


def cond_kernel(table_ref, home_ref, away_ref, x_ref, rows_ref):
    for k in range(8):
        home, away = home_ref[k].astype(F32), away_ref[k].astype(F32)
        hr, hi = home[:8], home[8:]
        for place, band in enumerate((0, 2, 4, 6, 1, 3, 5, 7)):
            ar, ai = away[band : band + 1], away[8 + band : 9 + band]
            real = hr * ar + hi * ai
            imag = hr * ai - hi * ar
            at = k * 128 + place * 8
            rows_ref[at : at + 8, :256] = real
            rows_ref[at : at + 8, 256:] = imag
            rows_ref[at + 64 : at + 72, :256] = imag
            rows_ref[at + 64 : at + 72, 256:] = -real
    for k in range(8):
        x_ref[:, k * 128 : (k + 1) * 128] = dot(
            table_ref[...], rows_ref[k * 128 : (k + 1) * 128], ((1,), (1,)), EXACT
        )


def cond_planes(home, away):
    angles = plane_angles()
    table = np.concatenate([np.cos(angles), np.sin(angles)], axis=1).astype(np.float32)
    return pl.pallas_call(
        cond_kernel,
        out_shape=jax.ShapeDtypeStruct((256, 1024), F32),
        in_specs=[pl.BlockSpec(memory_space=pltpu.VMEM)] * 3,
        out_specs=pl.BlockSpec(memory_space=pltpu.VMEM),
        scratch_shapes=[pltpu.VMEM((1024, 512), F32)],
        compiler_params=pltpu.CompilerParams(vmem_limit_bytes=24 * MIB),
        cost_estimate=pl.CostEstimate(
            flops=12 * 256 * 512 * 1024, bytes_accessed=2 * MIB, transcendentals=0
        ),
        name="cond_planes",
    )(jnp.asarray(table), home, away)


def build_rows(rows_ref, waves, mirrored):
    home_ref, away_ref, home_back_ref, away_back_ref = waves

    def density(home, away, v):
        hr, hi = home[v : v + 1], home[8 + v : 9 + v]
        ar, ai = away[:8], away[8:]
        return hr * ar + hi * ai, hr * ai - hi * ar

    for k in range(8):
        home, away = home_ref[0, k].astype(F32), away_ref[0, k].astype(F32)
        home_back, away_back = home_back_ref[0, k].astype(F32), away_back_ref[0, k].astype(F32)
        if mirrored is not None:
            home_back = home_back * mirrored
        for pair in range(4):
            pieces = []
            for v in (2 * pair, 2 * pair + 1):
                real, imag = density(home, away, v)
                real_back, imag_back = density(home_back, away_back, v)
                pieces.append(
                    (real + real_back, imag - imag_back, imag + imag_back, real_back - real)
                )
            even_re, odd_im, even_im, odd_re = (
                jnp.concatenate(p, axis=0).astype(BF) for p in zip(*pieces)
            )
            at = k * 128 + pair * 16
            rows_ref[at : at + 16, :256] = even_re
            rows_ref[at : at + 16, 256:] = odd_im
            rows_ref[at + 64 : at + 80, :256] = even_im
            rows_ref[at + 64 : at + 80, 256:] = odd_re


def response_kernel(place_ref, *refs):
    first_waves, second_waves = refs[:4], refs[4:8]
    before_ref, w_ref, cond_ref, out_ref, sum_ref, first_ref, second_ref = refs[8:]
    step = pl.program_id(0)
    mirrored = jnp.where(step % 8 == 0, 0.0, 1.0)
    before = dot(second_ref[...], before_ref[0])
    build_rows(first_ref, first_waves, mirrored)
    total = jnp.where(step == 0, 0.0, sum_ref[...] + before)
    total = total + dot(first_ref[...], w_ref[0])
    build_rows(second_ref, second_waves, None)
    sum_ref[...] = total

    @pl.when(step == HALF // 2)
    def _():
        low = lax.broadcasted_iota(jnp.int32, (1, 128), 1) < 64
        for k in range(8):
            cond = cond_ref[k * 128 : (k + 1) * 128]
            rows = sum_ref[k * 128 : (k + 1) * 128] * NORM
            top = rows.astype(BF)
            rest = (rows - top.astype(F32)).astype(BF)
            prod = dot(cond, top, ((1,), (1,))) + dot(cond, rest, ((1,), (1,)))
            swapped = pltpu.roll(prod[64:], 64, 1)
            both = prod[:64] + jnp.where(low, swapped, -swapped)
            even, odd = both[:32], both[32:]
            real = jnp.where(low, even, pltpu.roll(odd, 64, 1))
            imag = jnp.where(low, pltpu.roll(even, 64, 1), odd)
            out_ref[:, 2 * k, :] = real
            out_ref[:, 2 * k + 1, :] = imag


def response(place, home, away, screened, cond):
    def block(second, back):
        def index(step, place_ref):
            z = jnp.minimum(2 * step + second, HALF - 1)
            z = (NZ - z) & (NZ - 1) if back else z
            place = place_ref[0]
            level = (place ^ z) & 1
            x = ((place >> 3) - (z >> 3)) & 3
            y = ((place >> 1) - (z >> 1)) & 3
            return ((y * 4 + x) * 2 + level, 0, 0, 0)

        return pl.BlockSpec((1, 8, 16, 256), index)

    waves = [block(s, b) for s in range(2) for b in (False, True) for _ in range(2)]
    return pl.pallas_call(
        response_kernel,
        grid_spec=pltpu.PrefetchScalarGridSpec(
            num_scalar_prefetch=1,
            grid=(HALF // 2 + 1,),
            in_specs=waves
            + [
                pl.BlockSpec((1, 512, 256), lambda i, p: (jnp.maximum(2 * i - 1, 0), 0, 0)),
                pl.BlockSpec((1, 512, 256), lambda i, p: (2 * i, 0, 0)),
                pl.BlockSpec((1024, 256), lambda i, p: (0, 0)),
            ],
            out_specs=pl.BlockSpec((32, 16, 128), lambda i, p: (0, 0, 0)),
            scratch_shapes=[
                pltpu.VMEM((1024, 256), F32),
                pltpu.VMEM((1024, 512), BF),
                pltpu.VMEM((1024, 512), BF),
            ],
        ),
        out_shape=jax.ShapeDtypeStruct((32, 16, 128), F32),
        compiler_params=pltpu.CompilerParams(vmem_limit_bytes=20 * MIB),
        cost_estimate=pl.CostEstimate(
            flops=2 * 1024 * 512 * 256 * HALF, bytes_accessed=9 * MIB, transcendentals=0
        ),
        name="valence_response",
    )(place.reshape(1), *([home, away] * 4), screened, screened, cond)


def spectrum_kernel(cos_ref, sin_ref, x_ref, out_ref):
    first = lax.broadcasted_iota(jnp.int32, (1, 128), 1) < 64
    for k in range(8):
        x = x_ref[:, k * 128 : (k + 1) * 128]
        turned = pltpu.roll(x, 64, 1)
        turned = jnp.where(first, turned, -turned)
        cond = dot(cos_ref[...], x, precision=EXACT) + dot(sin_ref[...], turned, precision=EXACT)
        cond = (cond * NORM).astype(BF).astype(F32).T
        out_ref[k * 128 : (k + 1) * 128] = cond.astype(BF)


def cond_spectrum(cosine, sine, columns):
    return pl.pallas_call(
        spectrum_kernel,
        out_shape=jax.ShapeDtypeStruct((1024, 256), BF),
        in_specs=[pl.BlockSpec(memory_space=pltpu.VMEM)] * 3,
        out_specs=pl.BlockSpec(memory_space=pltpu.VMEM),
        compiler_params=pltpu.CompilerParams(vmem_limit_bytes=24 * MIB),
        cost_estimate=pl.CostEstimate(
            flops=24 * 256 * 256 * 1024, bytes_accessed=2 * MIB, transcendentals=0
        ),
        name="cond_spectrum",
    )(cosine, sine, columns)


def line_tables(gmap, place):
    level = lax.dynamic_slice_in_dim(gmap, place * 256, 256) & (NZ - 1)
    column = jnp.arange(256, dtype=jnp.int32)
    angle = (level[:, None] * (column // 8)[None, :]) % NZ
    same = (column // NZ)[:, None] == (column % 8)[None, :]
    angle = angle.astype(F32) * (2.0 * math.pi / NZ)
    return jnp.where(same, jnp.cos(angle), 0.0), jnp.where(same, jnp.sin(angle), 0.0)


def lay_out_kernel(full_ref, rows_ref, mirror_ref):
    low = lax.broadcasted_iota(jnp.int32, (1, 128), 1) < 64
    for m in range(4):
        for n in range(4):
            for c in (2 * n, 2 * n + 1):
                piece = full_ref[m * 4 + n, 0, (c & 1) * 16 : (c & 1) * 16 + 16]
                at = (c * 4 + m) * 128
                rows_ref[:, :, at : at + 128] = piece.reshape(8, 2, 128)
            even, odd = full_ref[m * 4 + n, 1, :16], full_ref[m * 4 + n, 1, 16:]
            first = jnp.where(low, even, pltpu.roll(odd, 64, 1))
            second = jnp.where(low, pltpu.roll(even, 64, 1), odd)
            at = (2 * m * 4 + n) * 128
            mirror_ref[:, :, at : at + 128] = first.reshape(8, 2, 128)
            mirror_ref[:, :, at + 512 : at + 640] = second.reshape(8, 2, 128)


def lay_out(full):
    shape = jax.ShapeDtypeStruct((8, 2, 4096), F32)
    return pl.pallas_call(
        lay_out_kernel,
        in_specs=[pl.BlockSpec(memory_space=pltpu.VMEM)],
        out_specs=[pl.BlockSpec(memory_space=pltpu.VMEM)] * 2,
        out_shape=[shape, shape],
        compiler_params=pltpu.CompilerParams(vmem_limit_bytes=16 * MIB),
        name="lay_out",
    )(full)


def on_device(wavefunctions, partner, gmap, screened):
    ka_place = lax.axis_index(KA)
    place = lax.axis_index(GA)
    owned = ka_place * 8 + jnp.arange(8, dtype=jnp.int32)

    waves = wavefunctions.reshape(8, 2, 2, 8, 256).transpose(0, 2, 1, 3, 4).reshape(8, 32, 256)
    near = spread(waves, "zl").reshape(32, 32, 256)

    index = jnp.arange(PLANE, dtype=jnp.int32)
    negative = (NX - index // NY) % NX * NY + (NY - index % NY) % NY
    negative = jnp.where(place > NZ // 2, negative, index)
    flip = (index[:, None] == negative[None, :]).astype(BF)
    home_val = dot(waves[:, :16].reshape(128, 256), flip).astype(BF).reshape(8, 16, 256)
    home_val, near = lax.optimization_barrier((home_val, near))
    far = turned(near, "co", 1)

    away_val, away_cond = choose(partner, near, far, flip)
    home = spread(spread(home_val, "zh"), "x")
    away = spread(spread(away_val, "zh"), "x")
    planes = cond_planes(waves[:, 16:], away_cond)
    away, planes, screened = lax.optimization_barrier((away, planes, screened))
    home = spread(home, "y").reshape(32, 8, 16, 256)
    columns = lax.all_to_all(planes, GA, split_axis=0, concat_axis=0, tiled=True)
    away = spread(away, "y").reshape(32, 8, 16, 256)
    wide = screened_transform(screened, gmap)
    cond = cond_spectrum(*line_tables(gmap, place), columns)

    blocks = response(place, home, away, wide, cond)

    parts = lax.all_to_all(blocks, ("x", "y"), split_axis=0, concat_axis=0, tiled=True)
    mine = jnp.sum(parts.reshape(16, 2, 16, 128), axis=0)
    mine = mine + turned(mine, "zh", 1)
    everyone = copies_to_all(mine, KA)
    everyone = everyone.reshape(8, 2, 8, 256).transpose(0, 2, 1, 3).reshape(64, 512)
    select = (partner[None, :] == owned[:, None]).astype(F32)
    mirror = jnp.dot(select, everyone, precision=EXACT)
    mirror = mirror.reshape(8, 2, 2, 128).transpose(1, 0, 2, 3).reshape(32, 128)
    lane = jnp.arange(128, dtype=jnp.int32)
    moved = lane // 64 * 64 + lane % 8 * 8 + lane // 8 % 8
    turn = (lane[:, None] == moved[None, :]).astype(F32)
    sign = jnp.where(jnp.arange(32) % 2 == 0, 1.0, -1.0).astype(F32)
    mirror = jnp.dot(mirror, turn, precision=EXACT) * sign[:, None]
    full = copies_to_all(jnp.stack([mine.reshape(32, 128), mirror]), ("x", "y"))
    return lay_out(full)


def solution(mesh):
    fine = Mesh(mesh.devices.reshape(SIZES), AXES)
    in_specs = (P(KA, None, None, GA, None), P(), P(), P(GA, None))
    out_specs = (P(KA, None, None), P(KA, None, None))
    return jax.shard_map(
        on_device, mesh=fine, in_specs=in_specs, out_specs=out_specs, check_vma=False
    )
```

```python
import functools
import math

import jax
import jax.numpy as jnp
import numpy as np
from jax import lax
from jax.experimental import pallas as pl
from jax.experimental.pallas import tpu as pltpu
from jax.sharding import Mesh
from jax.sharding import PartitionSpec as P

NX = 16
NY = 16
NZ = 32
NG = 8192
PLANE = NX * NY
HALF = NZ // 2 + 1
LINE_BLOCKS = 4
LINE_ROWS = 48
NORM = 1.0 / math.sqrt(NG)
EXACT = lax.Precision.HIGHEST
BF = jnp.bfloat16
F32 = jnp.float32
MIB = 1 << 20

AXES = ("zl", "co", "x", "y", "zh")
SIZES = (4, 2, 4, 4, 2)
SIZE = dict(zip(AXES, SIZES))
KA = ("zl", "co")
GA = ("x", "y", "zh")


def split_table(table):
    high = table.astype(np.float32).astype(BF)
    low = (table - high.astype(np.float64)).astype(np.float32).astype(BF)
    return high, low


def plane_angles():
    index = np.arange(PLANE)
    x, y = index // NY, index % NY
    turns = (np.outer(x, x) % NX) / NX + (np.outer(y, y) % NY) / NY
    return 2.0 * np.pi * turns


def line_angles():
    index = np.arange(NZ)
    return 2.0 * np.pi * (np.outer(index, index) % NZ) / NZ


def turned(value, axis, step):
    size = SIZE[axis]
    return lax.ppermute(value, axis, [(i, (i + step) % size) for i in range(size)])


def spread(value, axis):
    return jnp.stack([value] + [turned(value, axis, d) for d in range(1, SIZE[axis])])


def copies_to_all(value, axes):
    count = math.prod(SIZE[axis] for axis in axes)
    copies = jnp.broadcast_to(value[None], (count,) + value.shape)
    return lax.all_to_all(copies, axes, split_axis=0, concat_axis=0, tiled=True)


def dot(a, b, contract=((1,), (0,)), precision=None):
    return lax.dot_general(
        a, b, (contract, ((), ())), precision=precision, preferred_element_type=F32
    )


def line_kernel(gmap_ref, line_ref, w_ref, out_ref):
    rows = 2 * HALF
    keep = lax.broadcasted_iota(jnp.int32, (1, 8, 256), 1) == (
        lax.broadcasted_iota(jnp.int32, (1, 8, 256), 2) >> 5
    )
    for b in range(LINE_BLOCKS):
        level = gmap_ref[b] & (NZ - 1)
        hot = (lax.broadcasted_iota(jnp.int32, (NZ, 256), 0) == level).astype(F32).astype(BF)
        picked = dot(line_ref[...], hot)
        tables = []
        for at in (0, LINE_ROWS):
            wide = jnp.broadcast_to(picked[at : at + rows][:, None, :], (rows, 8, 256))
            tables.append(jnp.where(keep, wide, 0.0).reshape(rows * 8, 256).astype(BF))
        block = w_ref[:, b * 256 : (b + 1) * 256]
        both = dot(jnp.concatenate(tables, axis=0), block, ((1,), (1,)))
        total = both[: rows * 8] + both[rows * 8 :]
        out_ref[:, b * 8 : (b + 1) * 8, :] = total.reshape(rows, 8, 256)


def line_transform(screened, gmap):
    angles = line_angles()[:HALF]
    table = np.concatenate([np.cos(angles), -np.sin(angles)], axis=0)
    padding = np.zeros((LINE_ROWS - 2 * HALF, NZ), BF)
    line = np.concatenate([x for part in split_table(table) for x in (part, padding)], axis=0)
    n = LINE_BLOCKS
    return pl.pallas_call(
        line_kernel,
        grid=(32 // n,),
        in_specs=[
            pl.BlockSpec((n, 1, 256), lambda i: (i, 0, 0)),
            pl.BlockSpec((2 * LINE_ROWS, NZ), lambda i: (0, 0)),
            pl.BlockSpec((256, n * 256), lambda i: (0, i)),
        ],
        out_specs=pl.BlockSpec((2 * HALF, n * 8, 256), lambda i: (0, i, 0)),
        out_shape=jax.ShapeDtypeStruct((2 * HALF, PLANE, 256), F32),
        compiler_params=pltpu.CompilerParams(vmem_limit_bytes=16 * MIB),
        cost_estimate=pl.CostEstimate(
            flops=4 * 272 * 256 * 8192, bytes_accessed=14 * MIB, transcendentals=0
        ),
        name="screened_line",
    )(gmap.reshape(32, 1, 256), jnp.asarray(line), screened)


def plane_kernel(high_ref, low_ref, real_ref, imag_ref, out_ref):
    real, imag = real_ref[0], imag_ref[0]
    for odd in range(2):
        if odd:
            both = [real[:128] - real[128:], imag[:128] - imag[128:]]
        else:
            both = [real[:128] + real[128:], imag[:128] + imag[128:]]
        both = jnp.concatenate(both, axis=0)
        top = both.astype(BF)
        rest = (both - top.astype(F32)).astype(BF)
        high, low = high_ref[odd], low_ref[odd]
        prod = (dot(high, top) + (dot(high, rest) + dot(low, top))).astype(BF)
        for half in range(8):
            at = (2 * half + odd) * NY
            out_ref[0, at : at + NY] = prod[half * NY : (half + 1) * NY]
            out_ref[0, 256 + at : 256 + at + NY] = prod[128 + half * NY : 144 + half * NY]


def plane_transform(lines):
    angles = plane_angles().reshape(NX, NY, PLANE)[:, :, :128]
    tables = []
    for odd in range(2):
        part = angles[odd::2].reshape(128, 128)
        cosine, sine = np.cos(part), np.sin(part)
        tables.append(np.block([[cosine, sine], [sine, -cosine]]))
    high, low = split_table(np.stack(tables))
    return pl.pallas_call(
        plane_kernel,
        grid=(HALF,),
        in_specs=[
            pl.BlockSpec((2, 256, 256), lambda z: (0, 0, 0)),
            pl.BlockSpec((2, 256, 256), lambda z: (0, 0, 0)),
            pl.BlockSpec((1, 256, 256), lambda z: (z, 0, 0)),
            pl.BlockSpec((1, 256, 256), lambda z: (z + HALF, 0, 0)),
        ],
        out_specs=pl.BlockSpec((1, 512, 256), lambda z: (z, 0, 0)),
        out_shape=jax.ShapeDtypeStruct((HALF, 512, 256), BF),
        compiler_params=pltpu.CompilerParams(vmem_limit_bytes=16 * MIB),
        cost_estimate=pl.CostEstimate(
            flops=12 * 256 * 256 * 256 * HALF, bytes_accessed=14 * MIB, transcendentals=0
        ),
        name="screened_plane",
    )(jnp.asarray(high), jnp.asarray(low), lines, lines)


def choose_kernel(partner_ref, place_ref, flip_ref, near_ref, far_ref, val_ref, cond_ref):
    level, core = place_ref[0], place_ref[1]
    for m in range(8):
        val_ref[0, m] = dot(near_ref[m, :16], flip_ref[...]).astype(BF)
        wanted = partner_ref[(level * 2 + core) * 8 + m]
        back = (level - wanted // 16) & 3
        at = back * 8 + (wanted & 7)
        near = (wanted // 8) % 2 == core

        def take(ref, m=m, at=at):
            row = ref[at]
            val_ref[1, m] = dot(row[:16], flip_ref[...]).astype(BF)
            cond_ref[m] = row[16:]

        pl.when(near)(functools.partial(take, near_ref))
        pl.when(jnp.logical_not(near))(functools.partial(take, far_ref))


def choose(partner, near, far, flip):
    shape = jax.ShapeDtypeStruct((8, 16, 256), BF)
    place = jnp.stack([lax.axis_index("zl"), lax.axis_index("co")]).astype(jnp.int32)
    return pl.pallas_call(
        choose_kernel,
        in_specs=[pl.BlockSpec(memory_space=pltpu.SMEM)] * 2
        + [pl.BlockSpec(memory_space=pltpu.VMEM)] * 3,
        out_specs=[pl.BlockSpec(memory_space=pltpu.VMEM)] * 2,
        out_shape=[jax.ShapeDtypeStruct((2, 8, 16, 256), BF), shape],
        compiler_params=pltpu.CompilerParams(vmem_limit_bytes=16 * MIB),
        name="partner_choice",
    )(partner, place, flip, near, far)


def cond_kernel(table_ref, home_ref, away_ref, x_ref, rows_ref):
    for k in range(8):
        home, away = home_ref[k].astype(F32), away_ref[k].astype(F32)
        hr, hi = home[:8], home[8:]
        for place, band in enumerate((0, 2, 4, 6, 1, 3, 5, 7)):
            ar, ai = away[band : band + 1], away[8 + band : 9 + band]
            real = hr * ar + hi * ai
            imag = hr * ai - hi * ar
            at = k * 128 + place * 8
            rows_ref[at : at + 8, :256] = real
            rows_ref[at : at + 8, 256:] = imag
            rows_ref[at + 64 : at + 72, :256] = imag
            rows_ref[at + 64 : at + 72, 256:] = -real
    for k in range(8):
        x_ref[:, k * 128 : (k + 1) * 128] = dot(
            table_ref[...], rows_ref[k * 128 : (k + 1) * 128], ((1,), (1,)), EXACT
        )


def cond_planes(home, away):
    angles = plane_angles()
    table = np.concatenate([np.cos(angles), np.sin(angles)], axis=1).astype(np.float32)
    return pl.pallas_call(
        cond_kernel,
        out_shape=jax.ShapeDtypeStruct((256, 1024), F32),
        in_specs=[pl.BlockSpec(memory_space=pltpu.VMEM)] * 3,
        out_specs=pl.BlockSpec(memory_space=pltpu.VMEM),
        scratch_shapes=[pltpu.VMEM((1024, 512), F32)],
        compiler_params=pltpu.CompilerParams(vmem_limit_bytes=24 * MIB),
        cost_estimate=pl.CostEstimate(
            flops=12 * 256 * 512 * 1024, bytes_accessed=2 * MIB, transcendentals=0
        ),
        name="cond_planes",
    )(jnp.asarray(table), home, away)


def build_rows(rows_ref, waves, mirrored):
    home_ref, away_ref, home_back_ref, away_back_ref = waves

    def density(home, away, v):
        hr, hi = home[v : v + 1], home[8 + v : 9 + v]
        ar, ai = away[:8], away[8:]
        return hr * ar + hi * ai, hr * ai - hi * ar

    for k in range(8):
        home, away = home_ref[0, k].astype(F32), away_ref[0, k].astype(F32)
        home_back, away_back = home_back_ref[0, k].astype(F32), away_back_ref[0, k].astype(F32)
        if mirrored is not None:
            home_back = home_back * mirrored
        for pair in range(4):
            pieces = []
            for v in (2 * pair, 2 * pair + 1):
                real, imag = density(home, away, v)
                real_back, imag_back = density(home_back, away_back, v)
                pieces.append(
                    (real + real_back, imag - imag_back, imag + imag_back, real_back - real)
                )
            even_re, odd_im, even_im, odd_re = (
                jnp.concatenate(p, axis=0).astype(BF) for p in zip(*pieces)
            )
            at = k * 128 + pair * 16
            rows_ref[at : at + 16, :256] = even_re
            rows_ref[at : at + 16, 256:] = odd_im
            rows_ref[at + 64 : at + 80, :256] = even_im
            rows_ref[at + 64 : at + 80, 256:] = odd_re


def response_kernel(place_ref, *refs):
    first_waves, second_waves = refs[:4], refs[4:8]
    before_ref, w_ref, cond_ref, out_ref, sum_ref, first_ref, second_ref = refs[8:]
    step = pl.program_id(0)
    mirrored = jnp.where(step % 8 == 0, 0.0, 1.0)
    before = dot(second_ref[...], before_ref[0])
    build_rows(first_ref, first_waves, mirrored)
    total = jnp.where(step == 0, 0.0, sum_ref[...] + before)
    total = total + dot(first_ref[...], w_ref[0])
    build_rows(second_ref, second_waves, None)
    sum_ref[...] = total

    @pl.when(step == HALF // 2)
    def _():
        low = lax.broadcasted_iota(jnp.int32, (1, 128), 1) < 64
        for k in range(8):
            cond = cond_ref[k * 128 : (k + 1) * 128]
            rows = sum_ref[k * 128 : (k + 1) * 128] * NORM
            top = rows.astype(BF)
            rest = (rows - top.astype(F32)).astype(BF)
            prod = dot(cond, top, ((1,), (1,))) + dot(cond, rest, ((1,), (1,)))
            swapped = pltpu.roll(prod[64:], 64, 1)
            both = prod[:64] + jnp.where(low, swapped, -swapped)
            even, odd = both[:32], both[32:]
            real = jnp.where(low, even, pltpu.roll(odd, 64, 1))
            imag = jnp.where(low, pltpu.roll(even, 64, 1), odd)
            out_ref[:, 2 * k, :] = real
            out_ref[:, 2 * k + 1, :] = imag


def response(place, home, away, screened, cond):
    def block(which, second, back):
        def index(step, place_ref):
            z = jnp.minimum(2 * step + second, HALF - 1)
            z = (NZ - z) & (NZ - 1) if back else z
            place = place_ref[0]
            level = (place ^ z) & 1
            x = ((place >> 3) - (z >> 3)) & 3
            y = ((place >> 1) - (z >> 1)) & 3
            x, y = (x, y) if which == 0 else (y, x)
            return ((y * 4 + x) * 2 + level, 0, 0, 0)

        return pl.BlockSpec((1, 8, 16, 256), index)

    waves = [block(w, s, b) for s in range(2) for b in (False, True) for w in range(2)]
    return pl.pallas_call(
        response_kernel,
        grid_spec=pltpu.PrefetchScalarGridSpec(
            num_scalar_prefetch=1,
            grid=(HALF // 2 + 1,),
            in_specs=waves
            + [
                pl.BlockSpec((1, 512, 256), lambda i, p: (jnp.maximum(2 * i - 1, 0), 0, 0)),
                pl.BlockSpec((1, 512, 256), lambda i, p: (2 * i, 0, 0)),
                pl.BlockSpec((1024, 256), lambda i, p: (0, 0)),
            ],
            out_specs=pl.BlockSpec((32, 16, 128), lambda i, p: (0, 0, 0)),
            scratch_shapes=[
                pltpu.VMEM((1024, 256), F32),
                pltpu.VMEM((1024, 512), BF),
                pltpu.VMEM((1024, 512), BF),
            ],
        ),
        out_shape=jax.ShapeDtypeStruct((32, 16, 128), F32),
        compiler_params=pltpu.CompilerParams(vmem_limit_bytes=20 * MIB),
        cost_estimate=pl.CostEstimate(
            flops=2 * 1024 * 512 * 256 * HALF, bytes_accessed=9 * MIB, transcendentals=0
        ),
        name="valence_response",
    )(place.reshape(1), *([home, away] * 4), screened, screened, cond)


def spectrum_kernel(cos_ref, sin_ref, x_ref, out_ref):
    first = lax.broadcasted_iota(jnp.int32, (1, 128), 1) < 64
    for k in range(8):
        x = x_ref[:, k * 128 : (k + 1) * 128]
        turned = pltpu.roll(x, 64, 1)
        turned = jnp.where(first, turned, -turned)
        cond = dot(cos_ref[...], x, precision=EXACT) + dot(sin_ref[...], turned, precision=EXACT)
        cond = (cond * NORM).astype(BF).astype(F32).T
        out_ref[k * 128 : (k + 1) * 128] = cond.astype(BF)


def cond_spectrum(cosine, sine, columns):
    return pl.pallas_call(
        spectrum_kernel,
        out_shape=jax.ShapeDtypeStruct((1024, 256), BF),
        in_specs=[pl.BlockSpec(memory_space=pltpu.VMEM)] * 3,
        out_specs=pl.BlockSpec(memory_space=pltpu.VMEM),
        compiler_params=pltpu.CompilerParams(vmem_limit_bytes=24 * MIB),
        cost_estimate=pl.CostEstimate(
            flops=24 * 256 * 256 * 1024, bytes_accessed=2 * MIB, transcendentals=0
        ),
        name="cond_spectrum",
    )(cosine, sine, columns)


def line_tables(gmap, place):
    level = lax.dynamic_slice_in_dim(gmap, place * 256, 256) & (NZ - 1)
    column = jnp.arange(256, dtype=jnp.int32)
    angle = (level[:, None] * (column // 8)[None, :]) % NZ
    same = (column // NZ)[:, None] == (column % 8)[None, :]
    angle = angle.astype(F32) * (2.0 * math.pi / NZ)
    return jnp.where(same, jnp.cos(angle), 0.0), jnp.where(same, jnp.sin(angle), 0.0)


def lay_out_kernel(full_ref, rows_ref, mirror_ref):
    low = lax.broadcasted_iota(jnp.int32, (1, 128), 1) < 64
    for m in range(4):
        for n in range(4):
            for c in (2 * n, 2 * n + 1):
                piece = full_ref[m * 4 + n, 0, (c & 1) * 16 : (c & 1) * 16 + 16]
                at = (c * 4 + m) * 128
                rows_ref[:, :, at : at + 128] = piece.reshape(8, 2, 128)
            even, odd = full_ref[m * 4 + n, 1, :16], full_ref[m * 4 + n, 1, 16:]
            first = jnp.where(low, even, pltpu.roll(odd, 64, 1))
            second = jnp.where(low, pltpu.roll(even, 64, 1), odd)
            at = (2 * m * 4 + n) * 128
            mirror_ref[:, :, at : at + 128] = first.reshape(8, 2, 128)
            mirror_ref[:, :, at + 512 : at + 640] = second.reshape(8, 2, 128)


def lay_out(full):
    shape = jax.ShapeDtypeStruct((8, 2, 4096), F32)
    return pl.pallas_call(
        lay_out_kernel,
        in_specs=[pl.BlockSpec(memory_space=pltpu.VMEM)],
        out_specs=[pl.BlockSpec(memory_space=pltpu.VMEM)] * 2,
        out_shape=[shape, shape],
        compiler_params=pltpu.CompilerParams(vmem_limit_bytes=16 * MIB),
        name="lay_out",
    )(full)


def on_device(wavefunctions, partner, gmap, screened):
    ka_place = lax.axis_index(KA)
    place = lax.axis_index(GA)
    owned = ka_place * 8 + jnp.arange(8, dtype=jnp.int32)

    waves = wavefunctions.reshape(8, 2, 2, 8, 256).transpose(0, 2, 1, 3, 4).reshape(8, 32, 256)
    near = spread(waves, "zl").reshape(32, 32, 256)

    index = jnp.arange(PLANE, dtype=jnp.int32)
    negative = (NX - index // NY) % NX * NY + (NY - index % NY) % NY
    negative = jnp.where(place > NZ // 2, negative, index)
    flip = (index[:, None] == negative[None, :]).astype(BF)
    lines = line_transform(screened, gmap)
    near, lines = lax.optimization_barrier((near, lines))
    far = turned(near, "co", 1)

    vals, away_cond = choose(partner, near, far, flip)
    vals = spread(vals, "zh")
    home, away = spread(vals[:, 0], "x"), spread(vals[:, 1], "y")
    planes = cond_planes(waves[:, 16:], away_cond)
    home, away, planes, lines = lax.optimization_barrier((home, away, planes, lines))
    homes = [home] + [turned(home, "y", d) for d in range(1, 4)]
    aways = [away] + [turned(away, "x", d) for d in range(1, 4)]
    homes[1], planes = lax.optimization_barrier((homes[1], planes))
    columns = lax.all_to_all(planes, GA, split_axis=0, concat_axis=0, tiled=True)
    wide = plane_transform(lines)
    home = jnp.stack(homes).reshape(32, 8, 16, 256)
    away = jnp.stack(aways).reshape(32, 8, 16, 256)
    cond = cond_spectrum(*line_tables(gmap, place), columns)

    blocks = response(place, home, away, wide, cond)

    parts = lax.all_to_all(blocks, ("x", "y"), split_axis=0, concat_axis=0, tiled=True)
    mine = jnp.sum(parts.reshape(16, 2, 16, 128), axis=0)
    mine = mine + turned(mine, "zh", 1)
    everyone = copies_to_all(mine, KA)
    everyone = everyone.reshape(8, 2, 8, 256).transpose(0, 2, 1, 3).reshape(64, 512)
    select = (partner[None, :] == owned[:, None]).astype(F32)
    mirror = jnp.dot(select, everyone, precision=EXACT)
    mirror = mirror.reshape(8, 2, 2, 128).transpose(1, 0, 2, 3).reshape(32, 128)
    lane = jnp.arange(128, dtype=jnp.int32)
    moved = lane // 64 * 64 + lane % 8 * 8 + lane // 8 % 8
    turn = (lane[:, None] == moved[None, :]).astype(F32)
    sign = jnp.where(jnp.arange(32) % 2 == 0, 1.0, -1.0).astype(F32)
    mirror = jnp.dot(mirror, turn, precision=EXACT) * sign[:, None]
    full = copies_to_all(jnp.stack([mine.reshape(32, 128), mirror]), ("x", "y"))
    return lay_out(full)


def solution(mesh):
    fine = Mesh(mesh.devices.reshape(SIZES), AXES)
    in_specs = (P(KA, None, None, GA, None), P(), P(), P(GA, None))
    out_specs = (P(KA, None, None), P(KA, None, None))
    return jax.shard_map(
        on_device, mesh=fine, in_specs=in_specs, out_specs=out_specs, check_vma=False
    )
```

```python
import functools
import math

import jax
import jax.numpy as jnp
import numpy as np
from jax import lax
from jax.experimental import pallas as pl
from jax.experimental.pallas import tpu as pltpu
from jax.sharding import Mesh
from jax.sharding import PartitionSpec as P

NX = 16
NY = 16
NZ = 32
NG = 8192
PLANE = NX * NY
HALF = NZ // 2 + 1
LINE_BLOCKS = 4
LINE_STEPS = 32 // LINE_BLOCKS
LINE_ROWS = 48
NORM = 1.0 / math.sqrt(NG)
EXACT = lax.Precision.HIGHEST
BF = jnp.bfloat16
F32 = jnp.float32
MIB = 1 << 20

AXES = ("zl", "co", "x", "y", "zh")
SIZES = (4, 2, 4, 4, 2)
SIZE = dict(zip(AXES, SIZES))
KA = ("zl", "co")
GA = ("x", "y", "zh")


def split_table(table):
    high = table.astype(np.float32).astype(BF)
    low = (table - high.astype(np.float64)).astype(np.float32).astype(BF)
    return high, low


def plane_angles():
    index = np.arange(PLANE)
    x, y = index // NY, index % NY
    turns = (np.outer(x, x) % NX) / NX + (np.outer(y, y) % NY) / NY
    return 2.0 * np.pi * turns


def line_angles():
    index = np.arange(NZ)
    return 2.0 * np.pi * (np.outer(index, index) % NZ) / NZ


def turned(value, axis, step):
    size = SIZE[axis]
    return lax.ppermute(value, axis, [(i, (i + step) % size) for i in range(size)])


def spread(value, axis):
    return jnp.stack([value] + [turned(value, axis, d) for d in range(1, SIZE[axis])])


def copies_to_all(value, axes):
    count = math.prod(SIZE[axis] for axis in axes)
    copies = jnp.broadcast_to(value[None], (count,) + value.shape)
    return lax.all_to_all(copies, axes, split_axis=0, concat_axis=0, tiled=True)


def dot(a, b, contract=((1,), (0,)), precision=None):
    return lax.dot_general(
        a, b, (contract, ((), ())), precision=precision, preferred_element_type=F32
    )


def screened_kernel(gmap_ref, line_ref, high_ref, low_ref, w_ref, out_ref, lines_ref):
    step = pl.program_id(0)

    @pl.when(step < LINE_STEPS)
    def _():
        rows = 2 * HALF
        keep = lax.broadcasted_iota(jnp.int32, (1, 8, 256), 1) == (
            lax.broadcasted_iota(jnp.int32, (1, 8, 256), 2) >> 5
        )
        for b in range(LINE_BLOCKS):
            level = gmap_ref[b] & (NZ - 1)
            hot = (lax.broadcasted_iota(jnp.int32, (NZ, 256), 0) == level).astype(F32).astype(BF)
            picked = dot(line_ref[...], hot)
            tables = []
            for at in (0, LINE_ROWS):
                wide = jnp.broadcast_to(picked[at : at + rows][:, None, :], (rows, 8, 256))
                tables.append(jnp.where(keep, wide, 0.0).reshape(rows * 8, 256).astype(BF))
            block = w_ref[:, b * 256 : (b + 1) * 256]
            both = dot(jnp.concatenate(tables, axis=0), block, ((1,), (1,)))
            total = both[: rows * 8] + both[rows * 8 :]
            at = pl.multiple_of((step * LINE_BLOCKS + b) * 8, 8)
            lines_ref[:, pl.ds(at, 8), :] = total.reshape(rows, 8, 256)

    @pl.when(step >= LINE_STEPS)
    def _():
        z = step - LINE_STEPS
        real, imag = lines_ref[z], lines_ref[HALF + z]
        for odd in range(2):
            if odd:
                both = [real[:128] - real[128:], imag[:128] - imag[128:]]
            else:
                both = [real[:128] + real[128:], imag[:128] + imag[128:]]
            both = jnp.concatenate(both, axis=0)
            top = both.astype(BF)
            rest = (both - top.astype(F32)).astype(BF)
            high, low = high_ref[odd], low_ref[odd]
            prod = (dot(high, top) + (dot(high, rest) + dot(low, top))).astype(BF)
            for half in range(8):
                at = (2 * half + odd) * NY
                out_ref[0, at : at + NY] = prod[half * NY : (half + 1) * NY]
                out_ref[0, 256 + at : 256 + at + NY] = prod[128 + half * NY : 144 + half * NY]


def screened_transform(screened, gmap):
    angles = line_angles()[:HALF]
    table = np.concatenate([np.cos(angles), -np.sin(angles)], axis=0)
    padding = np.zeros((LINE_ROWS - 2 * HALF, NZ), BF)
    line = np.concatenate([x for part in split_table(table) for x in (part, padding)], axis=0)
    angles = plane_angles().reshape(NX, NY, PLANE)[:, :, :128]
    tables = []
    for odd in range(2):
        part = angles[odd::2].reshape(128, 128)
        cosine, sine = np.cos(part), np.sin(part)
        tables.append(np.block([[cosine, sine], [sine, -cosine]]))
    high, low = split_table(np.stack(tables))
    n = LINE_BLOCKS
    last = LINE_STEPS - 1
    return pl.pallas_call(
        screened_kernel,
        grid=(LINE_STEPS + HALF,),
        in_specs=[
            pl.BlockSpec((n, 1, 256), lambda i: (jnp.minimum(i, last), 0, 0)),
            pl.BlockSpec((2 * LINE_ROWS, NZ), lambda i: (0, 0)),
            pl.BlockSpec((2, 256, 256), lambda i: (0, 0, 0)),
            pl.BlockSpec((2, 256, 256), lambda i: (0, 0, 0)),
            pl.BlockSpec((256, n * 256), lambda i: (0, jnp.minimum(i, last))),
        ],
        out_specs=pl.BlockSpec((1, 512, 256), lambda i: (jnp.maximum(i - LINE_STEPS, 0), 0, 0)),
        out_shape=jax.ShapeDtypeStruct((HALF, 512, 256), BF),
        scratch_shapes=[pltpu.VMEM((2 * HALF, PLANE, 256), F32)],
        compiler_params=pltpu.CompilerParams(vmem_limit_bytes=54 * MIB),
        cost_estimate=pl.CostEstimate(
            flops=12 * 256 * 256 * 256 * HALF, bytes_accessed=9 * MIB, transcendentals=0
        ),
        name="screened_transform",
    )(gmap.reshape(32, 1, 256), jnp.asarray(line), jnp.asarray(high), jnp.asarray(low), screened)


def choose_kernel(partner_ref, place_ref, flip_ref, near_ref, far_ref, val_ref, cond_ref):
    level, core = place_ref[0], place_ref[1]
    for m in range(8):
        val_ref[0, m] = dot(near_ref[m, :16], flip_ref[...]).astype(BF)
        wanted = partner_ref[(level * 2 + core) * 8 + m]
        back = (level - wanted // 16) & 3
        at = back * 8 + (wanted & 7)
        near = (wanted // 8) % 2 == core

        def take(ref, m=m, at=at):
            row = ref[at]
            val_ref[1, m] = dot(row[:16], flip_ref[...]).astype(BF)
            cond_ref[m] = row[16:]

        pl.when(near)(functools.partial(take, near_ref))
        pl.when(jnp.logical_not(near))(functools.partial(take, far_ref))


def choose(partner, near, far, flip):
    shape = jax.ShapeDtypeStruct((8, 16, 256), BF)
    place = jnp.stack([lax.axis_index("zl"), lax.axis_index("co")]).astype(jnp.int32)
    return pl.pallas_call(
        choose_kernel,
        in_specs=[pl.BlockSpec(memory_space=pltpu.SMEM)] * 2
        + [pl.BlockSpec(memory_space=pltpu.VMEM)] * 3,
        out_specs=[pl.BlockSpec(memory_space=pltpu.VMEM)] * 2,
        out_shape=[jax.ShapeDtypeStruct((2, 8, 16, 256), BF), shape],
        compiler_params=pltpu.CompilerParams(vmem_limit_bytes=16 * MIB),
        name="partner_choice",
    )(partner, place, flip, near, far)


def cond_kernel(table_ref, home_ref, away_ref, x_ref, rows_ref):
    for k in range(8):
        home, away = home_ref[k].astype(F32), away_ref[k].astype(F32)
        hr, hi = home[:8], home[8:]
        for place, band in enumerate((0, 2, 4, 6, 1, 3, 5, 7)):
            ar, ai = away[band : band + 1], away[8 + band : 9 + band]
            real = hr * ar + hi * ai
            imag = hr * ai - hi * ar
            at = k * 128 + place * 8
            rows_ref[at : at + 8, :256] = real
            rows_ref[at : at + 8, 256:] = imag
            rows_ref[at + 64 : at + 72, :256] = imag
            rows_ref[at + 64 : at + 72, 256:] = -real
    for k in range(8):
        x_ref[:, k * 128 : (k + 1) * 128] = dot(
            table_ref[...], rows_ref[k * 128 : (k + 1) * 128], ((1,), (1,)), EXACT
        )


def cond_planes(home, away):
    angles = plane_angles()
    table = np.concatenate([np.cos(angles), np.sin(angles)], axis=1).astype(np.float32)
    return pl.pallas_call(
        cond_kernel,
        out_shape=jax.ShapeDtypeStruct((256, 1024), F32),
        in_specs=[pl.BlockSpec(memory_space=pltpu.VMEM)] * 3,
        out_specs=pl.BlockSpec(memory_space=pltpu.VMEM),
        scratch_shapes=[pltpu.VMEM((1024, 512), F32)],
        compiler_params=pltpu.CompilerParams(vmem_limit_bytes=24 * MIB),
        cost_estimate=pl.CostEstimate(
            flops=12 * 256 * 512 * 1024, bytes_accessed=2 * MIB, transcendentals=0
        ),
        name="cond_planes",
    )(jnp.asarray(table), home, away)


def build_rows(rows_ref, waves, mirrored):
    home_ref, away_ref, home_back_ref, away_back_ref = waves

    def density(home, away, v):
        hr, hi = home[v : v + 1], home[8 + v : 9 + v]
        ar, ai = away[:8], away[8:]
        return hr * ar + hi * ai, hr * ai - hi * ar

    for k in range(8):
        home, away = home_ref[0, k].astype(F32), away_ref[0, k].astype(F32)
        home_back, away_back = home_back_ref[0, k].astype(F32), away_back_ref[0, k].astype(F32)
        if mirrored is not None:
            home_back = home_back * mirrored
        for pair in range(4):
            pieces = []
            for v in (2 * pair, 2 * pair + 1):
                real, imag = density(home, away, v)
                real_back, imag_back = density(home_back, away_back, v)
                pieces.append(
                    (real + real_back, imag - imag_back, imag + imag_back, real_back - real)
                )
            even_re, odd_im, even_im, odd_re = (
                jnp.concatenate(p, axis=0).astype(BF) for p in zip(*pieces)
            )
            at = k * 128 + pair * 16
            rows_ref[at : at + 16, :256] = even_re
            rows_ref[at : at + 16, 256:] = odd_im
            rows_ref[at + 64 : at + 80, :256] = even_im
            rows_ref[at + 64 : at + 80, 256:] = odd_re


def response_kernel(place_ref, *refs):
    first_waves, second_waves = refs[:4], refs[4:8]
    before_ref, w_ref, cond_ref, out_ref, sum_ref, first_ref, second_ref = refs[8:]
    step = pl.program_id(0)
    mirrored = jnp.where(step % 8 == 0, 0.0, 1.0)
    before = dot(second_ref[...], before_ref[0])
    build_rows(first_ref, first_waves, mirrored)
    total = jnp.where(step == 0, 0.0, sum_ref[...] + before)
    total = total + dot(first_ref[...], w_ref[0])
    build_rows(second_ref, second_waves, None)
    sum_ref[...] = total

    @pl.when(step == HALF // 2)
    def _():
        low = lax.broadcasted_iota(jnp.int32, (1, 128), 1) < 64
        for k in range(8):
            cond = cond_ref[k * 128 : (k + 1) * 128]
            rows = sum_ref[k * 128 : (k + 1) * 128] * NORM
            top = rows.astype(BF)
            rest = (rows - top.astype(F32)).astype(BF)
            prod = dot(cond, top, ((1,), (1,))) + dot(cond, rest, ((1,), (1,)))
            swapped = pltpu.roll(prod[64:], 64, 1)
            both = prod[:64] + jnp.where(low, swapped, -swapped)
            even, odd = both[:32], both[32:]
            real = jnp.where(low, even, pltpu.roll(odd, 64, 1))
            imag = jnp.where(low, pltpu.roll(even, 64, 1), odd)
            out_ref[:, 2 * k, :] = real
            out_ref[:, 2 * k + 1, :] = imag


def response(place, home, away, screened, cond):
    def block(which, second, back):
        def index(step, place_ref):
            z = jnp.minimum(2 * step + second, HALF - 1)
            z = (NZ - z) & (NZ - 1) if back else z
            place = place_ref[0]
            level = (place ^ z) & 1
            x = ((place >> 3) - (z >> 3)) & 3
            y = ((place >> 1) - (z >> 1)) & 3
            x, y = (x, y) if which == 0 else (y, x)
            return ((y * 4 + x) * 2 + level, 0, 0, 0)

        return pl.BlockSpec((1, 8, 16, 256), index)

    waves = [block(w, s, b) for s in range(2) for b in (False, True) for w in range(2)]
    return pl.pallas_call(
        response_kernel,
        grid_spec=pltpu.PrefetchScalarGridSpec(
            num_scalar_prefetch=1,
            grid=(HALF // 2 + 1,),
            in_specs=waves
            + [
                pl.BlockSpec((1, 512, 256), lambda i, p: (jnp.maximum(2 * i - 1, 0), 0, 0)),
                pl.BlockSpec((1, 512, 256), lambda i, p: (2 * i, 0, 0)),
                pl.BlockSpec((1024, 256), lambda i, p: (0, 0)),
            ],
            out_specs=pl.BlockSpec((32, 16, 128), lambda i, p: (0, 0, 0)),
            scratch_shapes=[
                pltpu.VMEM((1024, 256), F32),
                pltpu.VMEM((1024, 512), BF),
                pltpu.VMEM((1024, 512), BF),
            ],
        ),
        out_shape=jax.ShapeDtypeStruct((32, 16, 128), F32),
        compiler_params=pltpu.CompilerParams(vmem_limit_bytes=40 * MIB),
        cost_estimate=pl.CostEstimate(
            flops=2 * 1024 * 512 * 256 * HALF, bytes_accessed=9 * MIB, transcendentals=0
        ),
        name="valence_response",
    )(place.reshape(1), *([home, away] * 4), screened, screened, cond)


def spectrum_kernel(cos_ref, sin_ref, x_ref, out_ref):
    first = lax.broadcasted_iota(jnp.int32, (1, 128), 1) < 64
    for k in range(8):
        x = x_ref[:, k * 128 : (k + 1) * 128]
        turned = pltpu.roll(x, 64, 1)
        turned = jnp.where(first, turned, -turned)
        cond = dot(cos_ref[...], x, precision=EXACT) + dot(sin_ref[...], turned, precision=EXACT)
        cond = (cond * NORM).astype(BF).astype(F32).T
        out_ref[k * 128 : (k + 1) * 128] = cond.astype(BF)


def cond_spectrum(cosine, sine, columns):
    return pl.pallas_call(
        spectrum_kernel,
        out_shape=jax.ShapeDtypeStruct((1024, 256), BF),
        in_specs=[pl.BlockSpec(memory_space=pltpu.VMEM)] * 3,
        out_specs=pl.BlockSpec(memory_space=pltpu.VMEM),
        compiler_params=pltpu.CompilerParams(vmem_limit_bytes=16 * MIB),
        cost_estimate=pl.CostEstimate(
            flops=24 * 256 * 256 * 1024, bytes_accessed=2 * MIB, transcendentals=0
        ),
        name="cond_spectrum",
    )(cosine, sine, columns)


def line_tables(gmap, place):
    level = lax.dynamic_slice_in_dim(gmap, place * 256, 256) & (NZ - 1)
    column = jnp.arange(256, dtype=jnp.int32)
    angle = (level[:, None] * (column // 8)[None, :]) % NZ
    same = (column // NZ)[:, None] == (column % 8)[None, :]
    angle = angle.astype(F32) * (2.0 * math.pi / NZ)
    return jnp.where(same, jnp.cos(angle), 0.0), jnp.where(same, jnp.sin(angle), 0.0)


def lay_out_kernel(full_ref, rows_ref, mirror_ref):
    low = lax.broadcasted_iota(jnp.int32, (1, 128), 1) < 64
    for m in range(4):
        for n in range(4):
            for c in (2 * n, 2 * n + 1):
                piece = full_ref[m * 4 + n, 0, (c & 1) * 16 : (c & 1) * 16 + 16]
                at = (c * 4 + m) * 128
                rows_ref[:, :, at : at + 128] = piece.reshape(8, 2, 128)
            even, odd = full_ref[m * 4 + n, 1, :16], full_ref[m * 4 + n, 1, 16:]
            first = jnp.where(low, even, pltpu.roll(odd, 64, 1))
            second = jnp.where(low, pltpu.roll(even, 64, 1), odd)
            at = (2 * m * 4 + n) * 128
            mirror_ref[:, :, at : at + 128] = first.reshape(8, 2, 128)
            mirror_ref[:, :, at + 512 : at + 640] = second.reshape(8, 2, 128)


def lay_out(full):
    shape = jax.ShapeDtypeStruct((8, 2, 4096), F32)
    return pl.pallas_call(
        lay_out_kernel,
        in_specs=[pl.BlockSpec(memory_space=pltpu.VMEM)],
        out_specs=[pl.BlockSpec(memory_space=pltpu.VMEM)] * 2,
        out_shape=[shape, shape],
        compiler_params=pltpu.CompilerParams(vmem_limit_bytes=16 * MIB),
        name="lay_out",
    )(full)


def on_device(wavefunctions, partner, gmap, screened):
    ka_place = lax.axis_index(KA)
    place = lax.axis_index(GA)
    owned = ka_place * 8 + jnp.arange(8, dtype=jnp.int32)

    waves = wavefunctions.reshape(8, 2, 2, 8, 256).transpose(0, 2, 1, 3, 4).reshape(8, 32, 256)
    near = spread(waves, "zl").reshape(32, 32, 256)

    index = jnp.arange(PLANE, dtype=jnp.int32)
    negative = (NX - index // NY) % NX * NY + (NY - index % NY) % NY
    negative = jnp.where(place > NZ // 2, negative, index)
    flip = (index[:, None] == negative[None, :]).astype(BF)
    wide = screened_transform(screened, gmap)
    near, wide = lax.optimization_barrier((near, wide))
    far = turned(near, "co", 1)

    vals, away_cond = choose(partner, near, far, flip)
    planes = cond_planes(waves[:, 16:], away_cond)
    vals = spread(vals, "zh")
    vals, planes = lax.optimization_barrier((vals, planes))
    columns = lax.all_to_all(planes, GA, split_axis=0, concat_axis=0, tiled=True)
    home, away = spread(vals[:, 0], "x"), spread(vals[:, 1], "y")
    home, away = lax.optimization_barrier((home, away))
    homes = [home] + [turned(home, "y", d) for d in range(1, 4)]
    aways = [away] + [turned(away, "x", d) for d in range(1, 4)]
    home = jnp.stack(homes).reshape(32, 8, 16, 256)
    away = jnp.stack(aways).reshape(32, 8, 16, 256)
    cond = cond_spectrum(*line_tables(gmap, place), columns)

    blocks = response(place, home, away, wide, cond)

    parts = lax.all_to_all(blocks, ("x", "y"), split_axis=0, concat_axis=0, tiled=True)
    mine = jnp.sum(parts.reshape(16, 2, 16, 128), axis=0)
    everyone = copies_to_all(mine, ("zl", "co", "zh")).reshape(8, 2, 2, 16, 128)
    everyone = everyone[:, 0] + everyone[:, 1]
    mine = lax.dynamic_index_in_dim(everyone, ka_place, keepdims=False)
    everyone = everyone.reshape(8, 2, 8, 256).transpose(0, 2, 1, 3).reshape(64, 512)
    select = (partner[None, :] == owned[:, None]).astype(F32)
    mirror = jnp.dot(select, everyone, precision=EXACT)
    mirror = mirror.reshape(8, 2, 2, 128).transpose(1, 0, 2, 3).reshape(32, 128)
    lane = jnp.arange(128, dtype=jnp.int32)
    moved = lane // 64 * 64 + lane % 8 * 8 + lane // 8 % 8
    turn = (lane[:, None] == moved[None, :]).astype(F32)
    sign = jnp.where(jnp.arange(32) % 2 == 0, 1.0, -1.0).astype(F32)
    mirror = jnp.dot(mirror, turn, precision=EXACT) * sign[:, None]
    full = copies_to_all(jnp.stack([mine.reshape(32, 128), mirror]), ("x", "y"))
    return lay_out(full)


def solution(mesh):
    fine = Mesh(mesh.devices.reshape(SIZES), AXES)
    in_specs = (P(KA, None, None, GA, None), P(), P(), P(GA, None))
    out_specs = (P(KA, None, None), P(KA, None, None))
    return jax.shard_map(
        on_device, mesh=fine, in_specs=in_specs, out_specs=out_specs, check_vma=False
    )
```

```python
import functools
import math

import jax
import jax.numpy as jnp
import numpy as np
from jax import lax
from jax.experimental import pallas as pl
from jax.experimental.pallas import tpu as pltpu
from jax.sharding import Mesh
from jax.sharding import PartitionSpec as P

NX = 16
NY = 16
NZ = 32
NG = 8192
PLANE = NX * NY
HALF = NZ // 2 + 1
LINE_BLOCKS = 4
LINE_STEPS = 32 // LINE_BLOCKS
LINE_ROWS = 48
NORM = 1.0 / math.sqrt(NG)
EXACT = lax.Precision.HIGHEST
BF = jnp.bfloat16
F32 = jnp.float32
MIB = 1 << 20

AXES = ("zl", "co", "x", "y", "zh")
SIZES = (4, 2, 4, 4, 2)
SIZE = dict(zip(AXES, SIZES))
KA = ("zl", "co")
GA = ("x", "y", "zh")


def split_table(table):
    high = table.astype(np.float32).astype(BF)
    low = (table - high.astype(np.float64)).astype(np.float32).astype(BF)
    return high, low


def plane_angles():
    index = np.arange(PLANE)
    x, y = index // NY, index % NY
    turns = (np.outer(x, x) % NX) / NX + (np.outer(y, y) % NY) / NY
    return 2.0 * np.pi * turns


def line_angles():
    index = np.arange(NZ)
    return 2.0 * np.pi * (np.outer(index, index) % NZ) / NZ


def turned(value, axis, step):
    size = SIZE[axis]
    return lax.ppermute(value, axis, [(i, (i + step) % size) for i in range(size)])


def spread(value, axis):
    return jnp.stack([value] + [turned(value, axis, d) for d in range(1, SIZE[axis])])


def copies_to_all(value, axes):
    count = math.prod(SIZE[axis] for axis in axes)
    copies = jnp.broadcast_to(value[None], (count,) + value.shape)
    return lax.all_to_all(copies, axes, split_axis=0, concat_axis=0, tiled=True)


def dot(a, b, contract=((1,), (0,)), precision=None):
    return lax.dot_general(
        a, b, (contract, ((), ())), precision=precision, preferred_element_type=F32
    )


def screened_kernel(gmap_ref, line_ref, high_ref, low_ref, w_ref, out_ref, lines_ref):
    step = pl.program_id(0)

    @pl.when(step < LINE_STEPS)
    def _():
        rows = 2 * HALF
        keep = lax.broadcasted_iota(jnp.int32, (1, 8, 256), 1) == (
            lax.broadcasted_iota(jnp.int32, (1, 8, 256), 2) >> 5
        )
        for b in range(LINE_BLOCKS):
            level = gmap_ref[b] & (NZ - 1)
            hot = (lax.broadcasted_iota(jnp.int32, (NZ, 256), 0) == level).astype(F32).astype(BF)
            picked = dot(line_ref[...], hot)
            tables = []
            for at in (0, LINE_ROWS):
                wide = jnp.broadcast_to(picked[at : at + rows][:, None, :], (rows, 8, 256))
                tables.append(jnp.where(keep, wide, 0.0).reshape(rows * 8, 256).astype(BF))
            block = w_ref[:, b * 256 : (b + 1) * 256]
            both = dot(jnp.concatenate(tables, axis=0), block, ((1,), (1,)))
            total = both[: rows * 8] + both[rows * 8 :]
            at = pl.multiple_of((step * LINE_BLOCKS + b) * 8, 8)
            lines_ref[:, pl.ds(at, 8), :] = total.reshape(rows, 8, 256)

    @pl.when(step >= LINE_STEPS)
    def _():
        z = step - LINE_STEPS
        real, imag = lines_ref[z], lines_ref[HALF + z]
        for odd in range(2):
            if odd:
                both = [real[:128] - real[128:], imag[:128] - imag[128:]]
            else:
                both = [real[:128] + real[128:], imag[:128] + imag[128:]]
            both = jnp.concatenate(both, axis=0)
            top = both.astype(BF)
            rest = (both - top.astype(F32)).astype(BF)
            high, low = high_ref[odd], low_ref[odd]
            prod = (dot(high, top) + (dot(high, rest) + dot(low, top))).astype(BF)
            for half in range(8):
                at = (2 * half + odd) * NY
                out_ref[0, at : at + NY] = prod[half * NY : (half + 1) * NY]
                out_ref[0, 256 + at : 256 + at + NY] = prod[128 + half * NY : 144 + half * NY]


def screened_transform(screened, gmap):
    angles = line_angles()[:HALF]
    table = np.concatenate([np.cos(angles), -np.sin(angles)], axis=0)
    padding = np.zeros((LINE_ROWS - 2 * HALF, NZ), BF)
    line = np.concatenate([x for part in split_table(table) for x in (part, padding)], axis=0)
    angles = plane_angles().reshape(NX, NY, PLANE)[:, :, :128]
    tables = []
    for odd in range(2):
        part = angles[odd::2].reshape(128, 128)
        cosine, sine = np.cos(part), np.sin(part)
        tables.append(np.block([[cosine, sine], [sine, -cosine]]))
    high, low = split_table(np.stack(tables))
    n = LINE_BLOCKS
    last = LINE_STEPS - 1
    return pl.pallas_call(
        screened_kernel,
        grid=(LINE_STEPS + HALF,),
        in_specs=[
            pl.BlockSpec((n, 1, 256), lambda i: (jnp.minimum(i, last), 0, 0)),
            pl.BlockSpec((2 * LINE_ROWS, NZ), lambda i: (0, 0)),
            pl.BlockSpec((2, 256, 256), lambda i: (0, 0, 0)),
            pl.BlockSpec((2, 256, 256), lambda i: (0, 0, 0)),
            pl.BlockSpec((256, n * 256), lambda i: (0, jnp.minimum(i, last))),
        ],
        out_specs=pl.BlockSpec((1, 512, 256), lambda i: (jnp.maximum(i - LINE_STEPS, 0), 0, 0)),
        out_shape=jax.ShapeDtypeStruct((HALF, 512, 256), BF),
        scratch_shapes=[pltpu.VMEM((2 * HALF, PLANE, 256), F32)],
        compiler_params=pltpu.CompilerParams(vmem_limit_bytes=40 * MIB),
        cost_estimate=pl.CostEstimate(
            flops=48 * 256 * 256 * 256 * HALF, bytes_accessed=9 * MIB, transcendentals=0
        ),
        name="screened_transform",
    )(gmap.reshape(32, 1, 256), jnp.asarray(line), jnp.asarray(high), jnp.asarray(low), screened)


def choose_kernel(partner_ref, place_ref, flip_ref, near_ref, far_ref, val_ref, cond_ref):
    level, core = place_ref[0], place_ref[1]
    for m in range(8):
        val_ref[0, m] = dot(near_ref[m, :16], flip_ref[...]).astype(BF)
        wanted = partner_ref[(level * 2 + core) * 8 + m]
        back = (level - wanted // 16) & 3
        at = back * 8 + (wanted & 7)
        near = (wanted // 8) % 2 == core

        def take(ref, m=m, at=at):
            row = ref[at]
            val_ref[1, m] = dot(row[:16], flip_ref[...]).astype(BF)
            cond_ref[m] = row[16:]

        pl.when(near)(functools.partial(take, near_ref))
        pl.when(jnp.logical_not(near))(functools.partial(take, far_ref))


def choose(partner, near, far, flip):
    shape = jax.ShapeDtypeStruct((8, 16, 256), BF)
    place = jnp.stack([lax.axis_index("zl"), lax.axis_index("co")]).astype(jnp.int32)
    return pl.pallas_call(
        choose_kernel,
        in_specs=[pl.BlockSpec(memory_space=pltpu.SMEM)] * 2
        + [pl.BlockSpec(memory_space=pltpu.VMEM)] * 3,
        out_specs=[pl.BlockSpec(memory_space=pltpu.VMEM)] * 2,
        out_shape=[jax.ShapeDtypeStruct((2, 8, 16, 256), BF), shape],
        compiler_params=pltpu.CompilerParams(vmem_limit_bytes=16 * MIB),
        name="partner_choice",
    )(partner, place, flip, near, far)


def cond_kernel(table_ref, home_ref, away_ref, x_ref, rows_ref):
    for k in range(8):
        home, away = home_ref[k].astype(F32), away_ref[k].astype(F32)
        hr, hi = home[:8], home[8:]
        for place, band in enumerate((0, 2, 4, 6, 1, 3, 5, 7)):
            ar, ai = away[band : band + 1], away[8 + band : 9 + band]
            real = hr * ar + hi * ai
            imag = hr * ai - hi * ar
            at = k * 128 + place * 8
            rows_ref[at : at + 8, :256] = real
            rows_ref[at : at + 8, 256:] = imag
            rows_ref[at + 64 : at + 72, :256] = imag
            rows_ref[at + 64 : at + 72, 256:] = -real
    for k in range(8):
        x_ref[:, k * 128 : (k + 1) * 128] = dot(
            table_ref[...], rows_ref[k * 128 : (k + 1) * 128], ((1,), (1,)), EXACT
        )


def cond_planes(home, away):
    angles = plane_angles()
    table = np.concatenate([np.cos(angles), np.sin(angles)], axis=1).astype(np.float32)
    return pl.pallas_call(
        cond_kernel,
        out_shape=jax.ShapeDtypeStruct((256, 1024), F32),
        in_specs=[pl.BlockSpec(memory_space=pltpu.VMEM)] * 3,
        out_specs=pl.BlockSpec(memory_space=pltpu.VMEM),
        scratch_shapes=[pltpu.VMEM((1024, 512), F32)],
        compiler_params=pltpu.CompilerParams(vmem_limit_bytes=24 * MIB),
        cost_estimate=pl.CostEstimate(
            flops=12 * 256 * 512 * 1024, bytes_accessed=2 * MIB, transcendentals=0
        ),
        name="cond_planes",
    )(jnp.asarray(table), home, away)


def build_rows(rows_ref, waves, mirrored):
    home_ref, away_ref, home_back_ref, away_back_ref = waves

    def density(home, away, v):
        hr, hi = home[v : v + 1], home[8 + v : 9 + v]
        ar, ai = away[:8], away[8:]
        return hr * ar + hi * ai, hr * ai - hi * ar

    for k in range(8):
        home, away = home_ref[0, k].astype(F32), away_ref[0, k].astype(F32)
        home_back, away_back = home_back_ref[0, k].astype(F32), away_back_ref[0, k].astype(F32)
        if mirrored is not None:
            home_back = home_back * mirrored
        for pair in range(4):
            pieces = []
            for v in (2 * pair, 2 * pair + 1):
                real, imag = density(home, away, v)
                real_back, imag_back = density(home_back, away_back, v)
                pieces.append(
                    (real + real_back, imag - imag_back, imag + imag_back, real_back - real)
                )
            even_re, odd_im, even_im, odd_re = (
                jnp.concatenate(p, axis=0).astype(BF) for p in zip(*pieces)
            )
            at = k * 128 + pair * 16
            rows_ref[at : at + 16, :256] = even_re
            rows_ref[at : at + 16, 256:] = odd_im
            rows_ref[at + 64 : at + 80, :256] = even_im
            rows_ref[at + 64 : at + 80, 256:] = odd_re


def response_kernel(place_ref, *refs):
    first_waves, second_waves = refs[:4], refs[4:8]
    before_ref, w_ref, sum_ref, first_ref, second_ref = refs[8:]
    step = pl.program_id(0)
    mirrored = jnp.where(step % 8 == 0, 0.0, 1.0)
    before = dot(second_ref[...], before_ref[0])
    build_rows(first_ref, first_waves, mirrored)
    total = jnp.where(step == 0, 0.0, sum_ref[...] + before)
    total = total + dot(first_ref[...], w_ref[0])
    build_rows(second_ref, second_waves, None)
    sum_ref[...] = total


def response(place, waves, screened):
    def block(which, second, back):
        def index(step, place_ref):
            z = jnp.minimum(2 * step + second, HALF - 1)
            z = (NZ - z) & (NZ - 1) if back else z
            return (((z & 30) + ((place_ref[0] ^ z) & 1)) * 2 + which, 0, 0, 0)

        return pl.BlockSpec((1, 8, 16, 256), index)

    blocks = [block(w, s, b) for s in range(2) for b in (False, True) for w in range(2)]
    return pl.pallas_call(
        response_kernel,
        grid_spec=pltpu.PrefetchScalarGridSpec(
            num_scalar_prefetch=1,
            grid=(HALF // 2 + 1,),
            in_specs=blocks
            + [
                pl.BlockSpec((1, 512, 256), lambda i, p: (jnp.maximum(2 * i - 1, 0), 0, 0)),
                pl.BlockSpec((1, 512, 256), lambda i, p: (2 * i, 0, 0)),
            ],
            out_specs=pl.BlockSpec((1024, 256), lambda i, p: (0, 0)),
            scratch_shapes=[pltpu.VMEM((1024, 512), BF), pltpu.VMEM((1024, 512), BF)],
        ),
        out_shape=jax.ShapeDtypeStruct((1024, 256), F32),
        compiler_params=pltpu.CompilerParams(vmem_limit_bytes=20 * MIB),
        cost_estimate=pl.CostEstimate(
            flops=16 * 1024 * 512 * 256 * HALF, bytes_accessed=9 * MIB, transcendentals=0
        ),
        name="valence_response",
    )(place.reshape(1), *([waves] * 8), screened, screened)


def spectrum_kernel(cos_ref, sin_ref, x_ref, out_ref):
    first = lax.broadcasted_iota(jnp.int32, (1, 128), 1) < 64
    for k in range(8):
        x = x_ref[:, k * 128 : (k + 1) * 128]
        turned = pltpu.roll(x, 64, 1)
        turned = jnp.where(first, turned, -turned)
        cond = dot(cos_ref[...], x, precision=EXACT) + dot(sin_ref[...], turned, precision=EXACT)
        cond = (cond * NORM).astype(BF).astype(F32).T
        out_ref[k * 128 : (k + 1) * 128] = cond.astype(BF)


def cond_spectrum(cosine, sine, columns):
    return pl.pallas_call(
        spectrum_kernel,
        out_shape=jax.ShapeDtypeStruct((1024, 256), BF),
        in_specs=[pl.BlockSpec(memory_space=pltpu.VMEM)] * 3,
        out_specs=pl.BlockSpec(memory_space=pltpu.VMEM),
        compiler_params=pltpu.CompilerParams(vmem_limit_bytes=16 * MIB),
        cost_estimate=pl.CostEstimate(
            flops=24 * 256 * 256 * 1024, bytes_accessed=2 * MIB, transcendentals=0
        ),
        name="cond_spectrum",
    )(cosine, sine, columns)


def block_kernel(cond_ref, r_ref, out_ref):
    first = lax.broadcasted_iota(jnp.int32, (1, 128), 1) < 64
    for k in range(8):
        cond = cond_ref[k * 128 : (k + 1) * 128]
        rows = r_ref[k * 128 : (k + 1) * 128] * NORM
        top = rows.astype(BF)
        rest = (rows - top.astype(F32)).astype(BF)
        prod = dot(cond, top, ((1,), (1,))) + dot(cond, rest, ((1,), (1,)))
        swapped = pltpu.roll(prod[64:], 64, 1)
        both = prod[:64] + jnp.where(first, swapped, -swapped)
        even, odd = both[:32], both[32:]
        out_ref[:, 2 * k, :] = jnp.where(first, even, pltpu.roll(odd, 64, 1))
        out_ref[:, 2 * k + 1, :] = jnp.where(first, pltpu.roll(even, 64, 1), odd)


def kernel_blocks(cond, rows):
    return pl.pallas_call(
        block_kernel,
        out_shape=jax.ShapeDtypeStruct((32, 16, 128), F32),
        in_specs=[pl.BlockSpec(memory_space=pltpu.VMEM)] * 2,
        out_specs=pl.BlockSpec(memory_space=pltpu.VMEM),
        compiler_params=pltpu.CompilerParams(vmem_limit_bytes=16 * MIB),
        cost_estimate=pl.CostEstimate(
            flops=4 * 128 * 256 * 1024, bytes_accessed=2 * MIB, transcendentals=0
        ),
        name="kernel_blocks",
    )(cond, rows)


def line_tables(gmap, place):
    level = lax.dynamic_slice_in_dim(gmap, place * 256, 256) & (NZ - 1)
    column = jnp.arange(256, dtype=jnp.int32)
    angle = (level[:, None] * (column // 8)[None, :]) % NZ
    same = (column // NZ)[:, None] == (column % 8)[None, :]
    angle = angle.astype(F32) * (2.0 * math.pi / NZ)
    return jnp.where(same, jnp.cos(angle), 0.0), jnp.where(same, jnp.sin(angle), 0.0)


def lay_out_kernel(full_ref, rows_ref, mirror_ref):
    low = lax.broadcasted_iota(jnp.int32, (1, 128), 1) < 64
    for m in range(4):
        for n in range(4):
            for c in (2 * n, 2 * n + 1):
                piece = full_ref[m * 4 + n, 0, (c & 1) * 16 : (c & 1) * 16 + 16]
                at = (c * 4 + m) * 128
                rows_ref[:, :, at : at + 128] = piece.reshape(8, 2, 128)
            even, odd = full_ref[m * 4 + n, 1, :16], full_ref[m * 4 + n, 1, 16:]
            first = jnp.where(low, even, pltpu.roll(odd, 64, 1))
            second = jnp.where(low, pltpu.roll(even, 64, 1), odd)
            at = (2 * m * 4 + n) * 128
            mirror_ref[:, :, at : at + 128] = first.reshape(8, 2, 128)
            mirror_ref[:, :, at + 512 : at + 640] = second.reshape(8, 2, 128)


def lay_out(full):
    shape = jax.ShapeDtypeStruct((8, 2, 4096), F32)
    return pl.pallas_call(
        lay_out_kernel,
        in_specs=[pl.BlockSpec(memory_space=pltpu.VMEM)],
        out_specs=[pl.BlockSpec(memory_space=pltpu.VMEM)] * 2,
        out_shape=[shape, shape],
        compiler_params=pltpu.CompilerParams(vmem_limit_bytes=16 * MIB),
        name="lay_out",
    )(full)


def on_device(wavefunctions, partner, gmap, screened):
    ka_place = lax.axis_index(KA)
    place = lax.axis_index(GA)
    owned = ka_place * 8 + jnp.arange(8, dtype=jnp.int32)

    waves = wavefunctions.reshape(8, 2, 2, 8, 256).transpose(0, 2, 1, 3, 4).reshape(8, 32, 256)
    near = spread(waves, "zl").reshape(32, 32, 256)

    index = jnp.arange(PLANE, dtype=jnp.int32)
    negative = (NX - index // NY) % NX * NY + (NY - index % NY) % NY
    negative = jnp.where(place > NZ // 2, negative, index)
    flip = (index[:, None] == negative[None, :]).astype(BF)
    far = turned(near, "co", 1)

    vals, away_cond = choose(partner, near, far, flip)
    planes = cond_planes(waves[:, 16:], away_cond)
    vals = spread(vals, "zh")
    vals, screened = lax.optimization_barrier((vals, screened))
    wide = screened_transform(screened, gmap)
    vals = copies_to_all(vals, ("x", "y")).reshape(64, 8, 16, 256)

    vals, planes = lax.optimization_barrier((vals, planes))
    columns = lax.all_to_all(planes, GA, split_axis=0, concat_axis=0, tiled=True)
    rows = response(place, vals, wide)
    cond = cond_spectrum(*line_tables(gmap, place), columns)
    blocks = kernel_blocks(cond, rows)

    parts = lax.all_to_all(blocks, ("x", "y"), split_axis=0, concat_axis=0, tiled=True)
    mine = jnp.sum(parts.reshape(16, 2, 16, 128), axis=0)
    everyone = copies_to_all(mine, ("zl", "co", "zh")).reshape(8, 2, 2, 16, 128)
    everyone = everyone[:, 0] + everyone[:, 1]
    mine = lax.dynamic_index_in_dim(everyone, ka_place, keepdims=False)
    everyone = everyone.reshape(8, 2, 8, 256).transpose(0, 2, 1, 3).reshape(64, 512)
    select = (partner[None, :] == owned[:, None]).astype(F32)
    mirror = jnp.dot(select, everyone, precision=EXACT)
    mirror = mirror.reshape(8, 2, 2, 128).transpose(1, 0, 2, 3).reshape(32, 128)
    lane = jnp.arange(128, dtype=jnp.int32)
    moved = lane // 64 * 64 + lane % 8 * 8 + lane // 8 % 8
    turn = (lane[:, None] == moved[None, :]).astype(F32)
    sign = jnp.where(jnp.arange(32) % 2 == 0, 1.0, -1.0).astype(F32)
    mirror = jnp.dot(mirror, turn, precision=EXACT) * sign[:, None]
    full = copies_to_all(jnp.stack([mine.reshape(32, 128), mirror]), ("x", "y"))
    return lay_out(full)


def solution(mesh):
    fine = Mesh(mesh.devices.reshape(SIZES), AXES)
    in_specs = (P(KA, None, None, GA, None), P(), P(), P(GA, None))
    out_specs = (P(KA, None, None), P(KA, None, None))
    return jax.shard_map(
        on_device, mesh=fine, in_specs=in_specs, out_specs=out_specs, check_vma=False
    )
```

```python
import functools
import math

import jax
import jax.numpy as jnp
import numpy as np
from jax import lax
from jax.experimental import pallas as pl
from jax.experimental.pallas import tpu as pltpu
from jax.sharding import Mesh
from jax.sharding import PartitionSpec as P

NX = 16
NY = 16
NZ = 32
NG = 8192
PLANE = NX * NY
HALF = NZ // 2 + 1
LINE_BLOCKS = 4
LINE_STEPS = 32 // LINE_BLOCKS
LINE_ROWS = 48
NORM = 1.0 / math.sqrt(NG)
EXACT = lax.Precision.HIGHEST
BF = jnp.bfloat16
F32 = jnp.float32
MIB = 1 << 20

AXES = ("zl", "co", "x", "y", "zh")
SIZES = (4, 2, 4, 4, 2)
SIZE = dict(zip(AXES, SIZES))
KA = ("zl", "co")
GA = ("x", "y", "zh")


def split_table(table):
    high = table.astype(np.float32).astype(BF)
    low = (table - high.astype(np.float64)).astype(np.float32).astype(BF)
    return high, low


def plane_angles():
    index = np.arange(PLANE)
    x, y = index // NY, index % NY
    turns = (np.outer(x, x) % NX) / NX + (np.outer(y, y) % NY) / NY
    return 2.0 * np.pi * turns


def line_angles():
    index = np.arange(NZ)
    return 2.0 * np.pi * (np.outer(index, index) % NZ) / NZ


def turned(value, axis, step):
    size = SIZE[axis]
    return lax.ppermute(value, axis, [(i, (i + step) % size) for i in range(size)])


def spread(value, axis):
    return jnp.stack([value] + [turned(value, axis, d) for d in range(1, SIZE[axis])])


def copies_to_all(value, axes):
    count = math.prod(SIZE[axis] for axis in axes)
    copies = jnp.broadcast_to(value[None], (count,) + value.shape)
    return lax.all_to_all(copies, axes, split_axis=0, concat_axis=0, tiled=True)


def dot(a, b, contract=((1,), (0,)), precision=None):
    return lax.dot_general(
        a, b, (contract, ((), ())), precision=precision, preferred_element_type=F32
    )


def screened_kernel(gmap_ref, line_ref, high_ref, low_ref, w_ref, out_ref, lines_ref):
    step = pl.program_id(0)

    @pl.when(step < LINE_STEPS)
    def _():
        rows = 2 * HALF
        keep = lax.broadcasted_iota(jnp.int32, (1, 8, 256), 1) == (
            lax.broadcasted_iota(jnp.int32, (1, 8, 256), 2) >> 5
        )
        for b in range(LINE_BLOCKS):
            level = gmap_ref[b] & (NZ - 1)
            hot = (lax.broadcasted_iota(jnp.int32, (NZ, 256), 0) == level).astype(F32).astype(BF)
            picked = dot(line_ref[...], hot)
            tables = []
            for at in (0, LINE_ROWS):
                wide = jnp.broadcast_to(picked[at : at + rows][:, None, :], (rows, 8, 256))
                tables.append(jnp.where(keep, wide, 0.0).reshape(rows * 8, 256).astype(BF))
            block = w_ref[:, b * 256 : (b + 1) * 256]
            both = dot(jnp.concatenate(tables, axis=0), block, ((1,), (1,)))
            total = both[: rows * 8] + both[rows * 8 :]
            at = pl.multiple_of((step * LINE_BLOCKS + b) * 8, 8)
            lines_ref[:, pl.ds(at, 8), :] = total.reshape(rows, 8, 256)

    @pl.when(step >= LINE_STEPS)
    def _():
        z = step - LINE_STEPS
        real, imag = lines_ref[z], lines_ref[HALF + z]
        for odd in range(2):
            if odd:
                both = [real[:128] - real[128:], imag[:128] - imag[128:]]
            else:
                both = [real[:128] + real[128:], imag[:128] + imag[128:]]
            both = jnp.concatenate(both, axis=0)
            top = both.astype(BF)
            rest = (both - top.astype(F32)).astype(BF)
            high, low = high_ref[odd], low_ref[odd]
            prod = (dot(high, top) + (dot(high, rest) + dot(low, top))).astype(BF)
            for half in range(8):
                at = (2 * half + odd) * NY
                out_ref[0, at : at + NY] = prod[half * NY : (half + 1) * NY]
                out_ref[0, 256 + at : 256 + at + NY] = prod[128 + half * NY : 144 + half * NY]


def screened_transform(screened, gmap):
    angles = line_angles()[:HALF]
    table = np.concatenate([np.cos(angles), -np.sin(angles)], axis=0)
    padding = np.zeros((LINE_ROWS - 2 * HALF, NZ), BF)
    line = np.concatenate([x for part in split_table(table) for x in (part, padding)], axis=0)
    angles = plane_angles().reshape(NX, NY, PLANE)[:, :, :128]
    tables = []
    for odd in range(2):
        part = angles[odd::2].reshape(128, 128)
        cosine, sine = np.cos(part), np.sin(part)
        tables.append(np.block([[cosine, sine], [sine, -cosine]]))
    high, low = split_table(np.stack(tables))
    n = LINE_BLOCKS
    last = LINE_STEPS - 1
    return pl.pallas_call(
        screened_kernel,
        grid=(LINE_STEPS + HALF,),
        in_specs=[
            pl.BlockSpec((n, 1, 256), lambda i: (jnp.minimum(i, last), 0, 0)),
            pl.BlockSpec((2 * LINE_ROWS, NZ), lambda i: (0, 0)),
            pl.BlockSpec((2, 256, 256), lambda i: (0, 0, 0)),
            pl.BlockSpec((2, 256, 256), lambda i: (0, 0, 0)),
            pl.BlockSpec((256, n * 256), lambda i: (0, jnp.minimum(i, last))),
        ],
        out_specs=pl.BlockSpec((1, 512, 256), lambda i: (jnp.maximum(i - LINE_STEPS, 0), 0, 0)),
        out_shape=jax.ShapeDtypeStruct((HALF, 512, 256), BF),
        scratch_shapes=[pltpu.VMEM((2 * HALF, PLANE, 256), F32)],
        compiler_params=pltpu.CompilerParams(vmem_limit_bytes=40 * MIB),
        cost_estimate=pl.CostEstimate(
            flops=48 * 256 * 256 * 256 * HALF, bytes_accessed=9 * MIB, transcendentals=0
        ),
        name="screened_transform",
    )(gmap.reshape(32, 1, 256), jnp.asarray(line), jnp.asarray(high), jnp.asarray(low), screened)


def choose_kernel(partner_ref, place_ref, flip_ref, near_ref, far_ref, val_ref, cond_ref):
    level, core = place_ref[0], place_ref[1]
    for m in range(8):
        val_ref[0, m] = dot(near_ref[m, :16], flip_ref[...]).astype(BF)
        wanted = partner_ref[(level * 2 + core) * 8 + m]
        back = (level - wanted // 16) & 3
        at = back * 8 + (wanted & 7)
        near = (wanted // 8) % 2 == core

        def take(ref, m=m, at=at):
            row = ref[at]
            val_ref[1, m] = dot(row[:16], flip_ref[...]).astype(BF)
            cond_ref[m] = row[16:]

        pl.when(near)(functools.partial(take, near_ref))
        pl.when(jnp.logical_not(near))(functools.partial(take, far_ref))


def choose(partner, near, far, flip):
    shape = jax.ShapeDtypeStruct((8, 16, 256), BF)
    place = jnp.stack([lax.axis_index("zl"), lax.axis_index("co")]).astype(jnp.int32)
    return pl.pallas_call(
        choose_kernel,
        in_specs=[pl.BlockSpec(memory_space=pltpu.SMEM)] * 2
        + [pl.BlockSpec(memory_space=pltpu.VMEM)] * 3,
        out_specs=[pl.BlockSpec(memory_space=pltpu.VMEM)] * 2,
        out_shape=[jax.ShapeDtypeStruct((2, 8, 16, 256), BF), shape],
        compiler_params=pltpu.CompilerParams(vmem_limit_bytes=16 * MIB),
        name="partner_choice",
    )(partner, place, flip, near, far)


def cond_kernel(table_ref, home_ref, away_ref, x_ref, rows_ref):
    for k in range(8):
        home, away = home_ref[k].astype(F32), away_ref[k].astype(F32)
        hr, hi = home[:8], home[8:]
        for place, band in enumerate((0, 2, 4, 6, 1, 3, 5, 7)):
            ar, ai = away[band : band + 1], away[8 + band : 9 + band]
            real = hr * ar + hi * ai
            imag = hr * ai - hi * ar
            at = k * 128 + place * 8
            rows_ref[at : at + 8, :256] = real
            rows_ref[at : at + 8, 256:] = imag
            rows_ref[at + 64 : at + 72, :256] = imag
            rows_ref[at + 64 : at + 72, 256:] = -real
    for k in range(8):
        x_ref[:, k * 128 : (k + 1) * 128] = dot(
            table_ref[...], rows_ref[k * 128 : (k + 1) * 128], ((1,), (1,)), EXACT
        )


def cond_planes(home, away):
    angles = plane_angles()
    table = np.concatenate([np.cos(angles), np.sin(angles)], axis=1).astype(np.float32)
    return pl.pallas_call(
        cond_kernel,
        out_shape=jax.ShapeDtypeStruct((256, 1024), F32),
        in_specs=[pl.BlockSpec(memory_space=pltpu.VMEM)] * 3,
        out_specs=pl.BlockSpec(memory_space=pltpu.VMEM),
        scratch_shapes=[pltpu.VMEM((1024, 512), F32)],
        compiler_params=pltpu.CompilerParams(vmem_limit_bytes=24 * MIB),
        cost_estimate=pl.CostEstimate(
            flops=12 * 256 * 512 * 1024, bytes_accessed=2 * MIB, transcendentals=0
        ),
        name="cond_planes",
    )(jnp.asarray(table), home, away)


def build_rows(rows_ref, waves, mirrored):
    home_ref, away_ref, home_back_ref, away_back_ref = waves

    def density(home, away, v):
        hr, hi = home[v : v + 1], home[8 + v : 9 + v]
        ar, ai = away[:8], away[8:]
        return hr * ar + hi * ai, hr * ai - hi * ar

    for k in range(8):
        home, away = home_ref[0, k].astype(F32), away_ref[0, k].astype(F32)
        home_back, away_back = home_back_ref[0, k].astype(F32), away_back_ref[0, k].astype(F32)
        if mirrored is not None:
            home_back = home_back * mirrored
        for pair in range(4):
            pieces = []
            for v in (2 * pair, 2 * pair + 1):
                real, imag = density(home, away, v)
                real_back, imag_back = density(home_back, away_back, v)
                pieces.append(
                    (real + real_back, imag - imag_back, imag + imag_back, real_back - real)
                )
            even_re, odd_im, even_im, odd_re = (
                jnp.concatenate(p, axis=0).astype(BF) for p in zip(*pieces)
            )
            at = k * 128 + pair * 16
            rows_ref[at : at + 16, :256] = even_re
            rows_ref[at : at + 16, 256:] = odd_im
            rows_ref[at + 64 : at + 80, :256] = even_im
            rows_ref[at + 64 : at + 80, 256:] = odd_re


def response_kernel(place_ref, *refs):
    first_waves, second_waves = refs[:4], refs[4:8]
    before_ref, w_ref, sum_ref, first_ref, second_ref = refs[8:]
    step = pl.program_id(0)
    mirrored = jnp.where(step % 8 == 0, 0.0, 1.0)
    before = dot(second_ref[...], before_ref[0])
    build_rows(first_ref, first_waves, mirrored)
    total = jnp.where(step == 0, 0.0, sum_ref[...] + before)
    total = total + dot(first_ref[...], w_ref[0])
    build_rows(second_ref, second_waves, None)
    sum_ref[...] = total


def response(place, home, away, screened):
    def block(which, second, back):
        def index(step, place_ref):
            z = jnp.minimum(2 * step + second, HALF - 1)
            z = (NZ - z) & (NZ - 1) if back else z
            x = ((place_ref[0] >> 3) - (z >> 3)) & 3
            y = ((place_ref[0] >> 1) - (z >> 1)) & 3
            x, y = (x, y) if which == 0 else (y, x)
            return ((y * 4 + x) * 2 + ((place_ref[0] ^ z) & 1), 0, 0, 0)

        return pl.BlockSpec((1, 8, 16, 256), index)

    blocks = [block(w, s, b) for s in range(2) for b in (False, True) for w in range(2)]
    return pl.pallas_call(
        response_kernel,
        grid_spec=pltpu.PrefetchScalarGridSpec(
            num_scalar_prefetch=1,
            grid=(HALF // 2 + 1,),
            in_specs=blocks
            + [
                pl.BlockSpec((1, 512, 256), lambda i, p: (jnp.maximum(2 * i - 1, 0), 0, 0)),
                pl.BlockSpec((1, 512, 256), lambda i, p: (2 * i, 0, 0)),
            ],
            out_specs=pl.BlockSpec((1024, 256), lambda i, p: (0, 0)),
            scratch_shapes=[pltpu.VMEM((1024, 512), BF), pltpu.VMEM((1024, 512), BF)],
        ),
        out_shape=jax.ShapeDtypeStruct((1024, 256), F32),
        compiler_params=pltpu.CompilerParams(vmem_limit_bytes=20 * MIB),
        cost_estimate=pl.CostEstimate(
            flops=16 * 1024 * 512 * 256 * HALF, bytes_accessed=9 * MIB, transcendentals=0
        ),
        name="valence_response",
    )(place.reshape(1), *([home, away] * 4), screened, screened)


def spectrum_kernel(cos_ref, sin_ref, x_ref, out_ref):
    first = lax.broadcasted_iota(jnp.int32, (1, 128), 1) < 64
    for k in range(8):
        x = x_ref[:, k * 128 : (k + 1) * 128]
        turned = pltpu.roll(x, 64, 1)
        turned = jnp.where(first, turned, -turned)
        cond = dot(cos_ref[...], x, precision=EXACT) + dot(sin_ref[...], turned, precision=EXACT)
        cond = (cond * NORM).astype(BF).astype(F32).T
        out_ref[k * 128 : (k + 1) * 128] = cond.astype(BF)


def cond_spectrum(cosine, sine, columns):
    return pl.pallas_call(
        spectrum_kernel,
        out_shape=jax.ShapeDtypeStruct((1024, 256), BF),
        in_specs=[pl.BlockSpec(memory_space=pltpu.VMEM)] * 3,
        out_specs=pl.BlockSpec(memory_space=pltpu.VMEM),
        compiler_params=pltpu.CompilerParams(vmem_limit_bytes=16 * MIB),
        cost_estimate=pl.CostEstimate(
            flops=24 * 256 * 256 * 1024, bytes_accessed=2 * MIB, transcendentals=0
        ),
        name="cond_spectrum",
    )(cosine, sine, columns)


def block_kernel(cond_ref, r_ref, out_ref):
    first = lax.broadcasted_iota(jnp.int32, (1, 128), 1) < 64
    for k in range(8):
        cond = cond_ref[k * 128 : (k + 1) * 128]
        rows = r_ref[k * 128 : (k + 1) * 128] * NORM
        top = rows.astype(BF)
        rest = (rows - top.astype(F32)).astype(BF)
        prod = dot(cond, top, ((1,), (1,))) + dot(cond, rest, ((1,), (1,)))
        swapped = pltpu.roll(prod[64:], 64, 1)
        both = prod[:64] + jnp.where(first, swapped, -swapped)
        even, odd = both[:32], both[32:]
        out_ref[:, 2 * k, :] = jnp.where(first, even, pltpu.roll(odd, 64, 1))
        out_ref[:, 2 * k + 1, :] = jnp.where(first, pltpu.roll(even, 64, 1), odd)


def kernel_blocks(cond, rows):
    return pl.pallas_call(
        block_kernel,
        out_shape=jax.ShapeDtypeStruct((32, 16, 128), F32),
        in_specs=[pl.BlockSpec(memory_space=pltpu.VMEM)] * 2,
        out_specs=pl.BlockSpec(memory_space=pltpu.VMEM),
        compiler_params=pltpu.CompilerParams(vmem_limit_bytes=16 * MIB),
        cost_estimate=pl.CostEstimate(
            flops=4 * 128 * 256 * 1024, bytes_accessed=2 * MIB, transcendentals=0
        ),
        name="kernel_blocks",
    )(cond, rows)


def line_tables(gmap, place):
    level = lax.dynamic_slice_in_dim(gmap, place * 256, 256) & (NZ - 1)
    column = jnp.arange(256, dtype=jnp.int32)
    angle = (level[:, None] * (column // 8)[None, :]) % NZ
    same = (column // NZ)[:, None] == (column % 8)[None, :]
    angle = angle.astype(F32) * (2.0 * math.pi / NZ)
    return jnp.where(same, jnp.cos(angle), 0.0), jnp.where(same, jnp.sin(angle), 0.0)


def lay_out_kernel(full_ref, rows_ref, mirror_ref):
    low = lax.broadcasted_iota(jnp.int32, (1, 128), 1) < 64
    for m in range(4):
        for n in range(4):
            for c in (2 * n, 2 * n + 1):
                piece = full_ref[m * 4 + n, 0, (c & 1) * 16 : (c & 1) * 16 + 16]
                at = (c * 4 + m) * 128
                rows_ref[:, :, at : at + 128] = piece.reshape(8, 2, 128)
            even, odd = full_ref[m * 4 + n, 1, :16], full_ref[m * 4 + n, 1, 16:]
            first = jnp.where(low, even, pltpu.roll(odd, 64, 1))
            second = jnp.where(low, pltpu.roll(even, 64, 1), odd)
            at = (2 * m * 4 + n) * 128
            mirror_ref[:, :, at : at + 128] = first.reshape(8, 2, 128)
            mirror_ref[:, :, at + 512 : at + 640] = second.reshape(8, 2, 128)


def lay_out(full):
    shape = jax.ShapeDtypeStruct((8, 2, 4096), F32)
    return pl.pallas_call(
        lay_out_kernel,
        in_specs=[pl.BlockSpec(memory_space=pltpu.VMEM)],
        out_specs=[pl.BlockSpec(memory_space=pltpu.VMEM)] * 2,
        out_shape=[shape, shape],
        compiler_params=pltpu.CompilerParams(vmem_limit_bytes=16 * MIB),
        name="lay_out",
    )(full)


def on_device(wavefunctions, partner, gmap, screened):
    ka_place = lax.axis_index(KA)
    place = lax.axis_index(GA)
    owned = ka_place * 8 + jnp.arange(8, dtype=jnp.int32)

    waves = wavefunctions.reshape(8, 2, 2, 8, 256).transpose(0, 2, 1, 3, 4).reshape(8, 32, 256)
    near = spread(waves, "zl").reshape(32, 32, 256)

    index = jnp.arange(PLANE, dtype=jnp.int32)
    negative = (NX - index // NY) % NX * NY + (NY - index % NY) % NY
    negative = jnp.where(place > NZ // 2, negative, index)
    flip = (index[:, None] == negative[None, :]).astype(BF)
    far = turned(near, "co", 1)

    vals, away_cond = choose(partner, near, far, flip)
    planes = cond_planes(waves[:, 16:], away_cond)
    vals = spread(vals, "zh")
    home, away = spread(vals[:, 0], "x"), spread(vals[:, 1], "y")
    home, away, planes, screened = lax.optimization_barrier((home, away, planes, screened))
    homes = [home] + [turned(home, "y", d) for d in range(1, 4)]
    aways = [away] + [turned(away, "x", d) for d in range(1, 4)]
    wide = screened_transform(screened, gmap)

    wide, planes = lax.optimization_barrier((wide, planes))
    columns = lax.all_to_all(planes, GA, split_axis=0, concat_axis=0, tiled=True)
    home = jnp.stack(homes).reshape(32, 8, 16, 256)
    away = jnp.stack(aways).reshape(32, 8, 16, 256)
    rows = response(place, home, away, wide)
    cond = cond_spectrum(*line_tables(gmap, place), columns)
    blocks = kernel_blocks(cond, rows)

    parts = lax.all_to_all(blocks, ("x", "y"), split_axis=0, concat_axis=0, tiled=True)
    mine = jnp.sum(parts.reshape(16, 2, 16, 128), axis=0)
    everyone = copies_to_all(mine, ("zl", "co", "zh")).reshape(8, 2, 2, 16, 128)
    everyone = everyone[:, 0] + everyone[:, 1]
    mine = lax.dynamic_index_in_dim(everyone, ka_place, keepdims=False)
    everyone = everyone.reshape(8, 2, 8, 256).transpose(0, 2, 1, 3).reshape(64, 512)
    select = (partner[None, :] == owned[:, None]).astype(F32)
    mirror = jnp.dot(select, everyone, precision=EXACT)
    mirror = mirror.reshape(8, 2, 2, 128).transpose(1, 0, 2, 3).reshape(32, 128)
    lane = jnp.arange(128, dtype=jnp.int32)
    moved = lane // 64 * 64 + lane % 8 * 8 + lane // 8 % 8
    turn = (lane[:, None] == moved[None, :]).astype(F32)
    sign = jnp.where(jnp.arange(32) % 2 == 0, 1.0, -1.0).astype(F32)
    mirror = jnp.dot(mirror, turn, precision=EXACT) * sign[:, None]
    full = copies_to_all(jnp.stack([mine.reshape(32, 128), mirror]), ("x", "y"))
    return lay_out(full)


def solution(mesh):
    fine = Mesh(mesh.devices.reshape(SIZES), AXES)
    in_specs = (P(KA, None, None, GA, None), P(), P(), P(GA, None))
    out_specs = (P(KA, None, None), P(KA, None, None))
    return jax.shard_map(
        on_device, mesh=fine, in_specs=in_specs, out_specs=out_specs, check_vma=False
    )
```

```python
import functools
import math

import jax
import jax.numpy as jnp
import numpy as np
from jax import lax
from jax.experimental import pallas as pl
from jax.experimental.pallas import tpu as pltpu
from jax.sharding import Mesh
from jax.sharding import PartitionSpec as P

NX = 16
NY = 16
NZ = 32
NG = 8192
PLANE = NX * NY
HALF = NZ // 2 + 1
LINE_BLOCKS = 4
LINE_STEPS = 32 // LINE_BLOCKS
LINE_ROWS = 48
NORM = 1.0 / math.sqrt(NG)
EXACT = lax.Precision.HIGHEST
BF = jnp.bfloat16
F32 = jnp.float32
MIB = 1 << 20

AXES = ("zl", "co", "x", "y", "zh")
SIZES = (4, 2, 4, 4, 2)
SIZE = dict(zip(AXES, SIZES))
KA = ("zl", "co")
GA = ("x", "y", "zh")


def split_table(table):
    high = table.astype(np.float32).astype(BF)
    low = (table - high.astype(np.float64)).astype(np.float32).astype(BF)
    return high, low


def plane_angles():
    index = np.arange(PLANE)
    x, y = index // NY, index % NY
    turns = (np.outer(x, x) % NX) / NX + (np.outer(y, y) % NY) / NY
    return 2.0 * np.pi * turns


def line_angles():
    index = np.arange(NZ)
    return 2.0 * np.pi * (np.outer(index, index) % NZ) / NZ


def turned(value, axis, step):
    size = SIZE[axis]
    return lax.ppermute(value, axis, [(i, (i + step) % size) for i in range(size)])


def spread(value, axis):
    return jnp.stack([value] + [turned(value, axis, d) for d in range(1, SIZE[axis])])


def copies_to_all(value, axes):
    count = math.prod(SIZE[axis] for axis in axes)
    copies = jnp.broadcast_to(value[None], (count,) + value.shape)
    return lax.all_to_all(copies, axes, split_axis=0, concat_axis=0, tiled=True)


def dot(a, b, contract=((1,), (0,)), precision=None):
    return lax.dot_general(
        a, b, (contract, ((), ())), precision=precision, preferred_element_type=F32
    )


def screened_kernel(gmap_ref, line_ref, high_ref, low_ref, w_ref, out_ref, end_ref, lines_ref):
    step = pl.program_id(0)
    end_ref[...] = jnp.zeros_like(end_ref)

    @pl.when(step < LINE_STEPS)
    def _():
        rows = 2 * HALF
        keep = lax.broadcasted_iota(jnp.int32, (1, 8, 256), 1) == (
            lax.broadcasted_iota(jnp.int32, (1, 8, 256), 2) >> 5
        )
        for b in range(LINE_BLOCKS):
            level = gmap_ref[b] & (NZ - 1)
            hot = (lax.broadcasted_iota(jnp.int32, (NZ, 256), 0) == level).astype(F32).astype(BF)
            picked = dot(line_ref[...], hot)
            tables = []
            for at in (0, LINE_ROWS):
                wide = jnp.broadcast_to(picked[at : at + rows][:, None, :], (rows, 8, 256))
                tables.append(jnp.where(keep, wide, 0.0).reshape(rows * 8, 256).astype(BF))
            block = w_ref[:, b * 256 : (b + 1) * 256]
            both = dot(jnp.concatenate(tables, axis=0), block, ((1,), (1,)))
            total = both[: rows * 8] + both[rows * 8 :]
            at = pl.multiple_of((step * LINE_BLOCKS + b) * 8, 8)
            lines_ref[:, pl.ds(at, 8), :] = total.reshape(rows, 8, 256)

    @pl.when(step >= LINE_STEPS)
    def _():
        z = step - LINE_STEPS
        real, imag = lines_ref[z], lines_ref[HALF + z]
        for odd in range(2):
            if odd:
                both = [real[:128] - real[128:], imag[:128] - imag[128:]]
            else:
                both = [real[:128] + real[128:], imag[:128] + imag[128:]]
            both = jnp.concatenate(both, axis=0)
            top = both.astype(BF)
            rest = (both - top.astype(F32)).astype(BF)
            high, low = high_ref[odd], low_ref[odd]
            prod = (dot(high, top) + (dot(high, rest) + dot(low, top))).astype(BF)
            for half in range(8):
                at = (2 * half + odd) * NY
                out_ref[0, at : at + NY] = prod[half * NY : (half + 1) * NY]
                out_ref[0, 256 + at : 256 + at + NY] = prod[128 + half * NY : 144 + half * NY]


def screened_transform(screened, gmap):
    angles = line_angles()[:HALF]
    table = np.concatenate([np.cos(angles), -np.sin(angles)], axis=0)
    padding = np.zeros((LINE_ROWS - 2 * HALF, NZ), BF)
    line = np.concatenate([x for part in split_table(table) for x in (part, padding)], axis=0)
    angles = plane_angles().reshape(NX, NY, PLANE)[:, :, :128]
    tables = []
    for odd in range(2):
        part = angles[odd::2].reshape(128, 128)
        cosine, sine = np.cos(part), np.sin(part)
        tables.append(np.block([[cosine, sine], [sine, -cosine]]))
    high, low = split_table(np.stack(tables))
    n = LINE_BLOCKS
    last = LINE_STEPS - 1
    return pl.pallas_call(
        screened_kernel,
        grid=(LINE_STEPS + HALF,),
        in_specs=[
            pl.BlockSpec((n, 1, 256), lambda i: (jnp.minimum(i, last), 0, 0)),
            pl.BlockSpec((2 * LINE_ROWS, NZ), lambda i: (0, 0)),
            pl.BlockSpec((2, 256, 256), lambda i: (0, 0, 0)),
            pl.BlockSpec((2, 256, 256), lambda i: (0, 0, 0)),
            pl.BlockSpec((256, n * 256), lambda i: (0, jnp.minimum(i, last))),
        ],
        out_specs=[
            pl.BlockSpec((1, 512, 256), lambda i: (jnp.maximum(i - LINE_STEPS, 0), 0, 0)),
            pl.BlockSpec((8, 128), lambda i: (0, 0)),
        ],
        out_shape=[
            jax.ShapeDtypeStruct((HALF, 512, 256), BF),
            jax.ShapeDtypeStruct((8, 128), F32),
        ],
        scratch_shapes=[pltpu.VMEM((2 * HALF, PLANE, 256), F32)],
        compiler_params=pltpu.CompilerParams(vmem_limit_bytes=40 * MIB),
        cost_estimate=pl.CostEstimate(
            flops=48 * 256 * 256 * 256 * HALF, bytes_accessed=9 * MIB, transcendentals=0
        ),
        name="screened_transform",
    )(gmap.reshape(32, 1, 256), jnp.asarray(line), jnp.asarray(high), jnp.asarray(low), screened)


def choose_kernel(partner_ref, place_ref, flip_ref, near_ref, far_ref, val_ref, cond_ref):
    level, core = place_ref[0], place_ref[1]
    for m in range(8):
        val_ref[0, m] = dot(near_ref[m, :16], flip_ref[...]).astype(BF)
        wanted = partner_ref[(level * 2 + core) * 8 + m]
        back = (level - wanted // 16) & 3
        at = back * 8 + (wanted & 7)
        near = (wanted // 8) % 2 == core

        def take(ref, m=m, at=at):
            row = ref[at]
            val_ref[1, m] = dot(row[:16], flip_ref[...]).astype(BF)
            cond_ref[m] = row[16:]

        pl.when(near)(functools.partial(take, near_ref))
        pl.when(jnp.logical_not(near))(functools.partial(take, far_ref))


def choose(partner, near, far, flip):
    shape = jax.ShapeDtypeStruct((8, 16, 256), BF)
    place = jnp.stack([lax.axis_index("zl"), lax.axis_index("co")]).astype(jnp.int32)
    return pl.pallas_call(
        choose_kernel,
        in_specs=[pl.BlockSpec(memory_space=pltpu.SMEM)] * 2
        + [pl.BlockSpec(memory_space=pltpu.VMEM)] * 3,
        out_specs=[pl.BlockSpec(memory_space=pltpu.VMEM)] * 2,
        out_shape=[jax.ShapeDtypeStruct((2, 8, 16, 256), BF), shape],
        compiler_params=pltpu.CompilerParams(vmem_limit_bytes=16 * MIB),
        name="partner_choice",
    )(partner, place, flip, near, far)


def cond_kernel(table_ref, home_ref, away_ref, x_ref, rows_ref):
    for k in range(8):
        home, away = home_ref[k].astype(F32), away_ref[k].astype(F32)
        hr, hi = home[:8], home[8:]
        for place, band in enumerate((0, 2, 4, 6, 1, 3, 5, 7)):
            ar, ai = away[band : band + 1], away[8 + band : 9 + band]
            real = hr * ar + hi * ai
            imag = hr * ai - hi * ar
            at = k * 128 + place * 8
            rows_ref[at : at + 8, :256] = real
            rows_ref[at : at + 8, 256:] = imag
            rows_ref[at + 64 : at + 72, :256] = imag
            rows_ref[at + 64 : at + 72, 256:] = -real
    for k in range(8):
        x_ref[:, k * 128 : (k + 1) * 128] = dot(
            table_ref[...], rows_ref[k * 128 : (k + 1) * 128], ((1,), (1,)), EXACT
        )


def cond_planes(home, away):
    angles = plane_angles()
    table = np.concatenate([np.cos(angles), np.sin(angles)], axis=1).astype(np.float32)
    return pl.pallas_call(
        cond_kernel,
        out_shape=jax.ShapeDtypeStruct((256, 1024), F32),
        in_specs=[pl.BlockSpec(memory_space=pltpu.VMEM)] * 3,
        out_specs=pl.BlockSpec(memory_space=pltpu.VMEM),
        scratch_shapes=[pltpu.VMEM((1024, 512), F32)],
        compiler_params=pltpu.CompilerParams(vmem_limit_bytes=24 * MIB),
        cost_estimate=pl.CostEstimate(
            flops=12 * 256 * 512 * 1024, bytes_accessed=2 * MIB, transcendentals=0
        ),
        name="cond_planes",
    )(jnp.asarray(table), home, away)


def build_rows(rows_ref, waves, mirrored):
    home_ref, away_ref, home_back_ref, away_back_ref = waves

    def density(home, away, v):
        hr, hi = home[v : v + 1], home[8 + v : 9 + v]
        ar, ai = away[:8], away[8:]
        return hr * ar + hi * ai, hr * ai - hi * ar

    for k in range(8):
        home, away = home_ref[0, k].astype(F32), away_ref[0, k].astype(F32)
        home_back, away_back = home_back_ref[0, k].astype(F32), away_back_ref[0, k].astype(F32)
        if mirrored is not None:
            home_back = home_back * mirrored
        for pair in range(4):
            pieces = []
            for v in (2 * pair, 2 * pair + 1):
                real, imag = density(home, away, v)
                real_back, imag_back = density(home_back, away_back, v)
                pieces.append(
                    (real + real_back, imag - imag_back, imag + imag_back, real_back - real)
                )
            even_re, odd_im, even_im, odd_re = (
                jnp.concatenate(p, axis=0).astype(BF) for p in zip(*pieces)
            )
            at = k * 128 + pair * 16
            rows_ref[at : at + 16, :256] = even_re
            rows_ref[at : at + 16, 256:] = odd_im
            rows_ref[at + 64 : at + 80, :256] = even_im
            rows_ref[at + 64 : at + 80, 256:] = odd_re


def response_kernel(place_ref, *refs):
    first_waves, second_waves = refs[:4], refs[4:8]
    before_ref, w_ref, sum_ref, first_ref, second_ref = refs[8:]
    step = pl.program_id(0)
    mirrored = jnp.where(step % 8 == 0, 0.0, 1.0)
    before = dot(second_ref[...], before_ref[0])
    build_rows(first_ref, first_waves, mirrored)
    total = jnp.where(step == 0, 0.0, sum_ref[...] + before)
    total = total + dot(first_ref[...], w_ref[0])
    build_rows(second_ref, second_waves, None)
    sum_ref[...] = total


def response(place, home, away, screened):
    def block(which, second, back):
        def index(step, place_ref):
            z = jnp.minimum(2 * step + second, HALF - 1)
            z = (NZ - z) & (NZ - 1) if back else z
            x = ((place_ref[0] >> 3) - (z >> 3)) & 3
            y = ((place_ref[0] >> 1) - (z >> 1)) & 3
            x, y = (x, y) if which == 0 else (y, x)
            return ((y * 4 + x) * 2 + ((place_ref[0] ^ z) & 1), 0, 0, 0)

        return pl.BlockSpec((1, 8, 16, 256), index)

    blocks = [block(w, s, b) for s in range(2) for b in (False, True) for w in range(2)]
    return pl.pallas_call(
        response_kernel,
        grid_spec=pltpu.PrefetchScalarGridSpec(
            num_scalar_prefetch=1,
            grid=(HALF // 2 + 1,),
            in_specs=blocks
            + [
                pl.BlockSpec((1, 512, 256), lambda i, p: (jnp.maximum(2 * i - 1, 0), 0, 0)),
                pl.BlockSpec((1, 512, 256), lambda i, p: (2 * i, 0, 0)),
            ],
            out_specs=pl.BlockSpec((1024, 256), lambda i, p: (0, 0)),
            scratch_shapes=[pltpu.VMEM((1024, 512), BF), pltpu.VMEM((1024, 512), BF)],
        ),
        out_shape=jax.ShapeDtypeStruct((1024, 256), F32),
        compiler_params=pltpu.CompilerParams(vmem_limit_bytes=20 * MIB),
        cost_estimate=pl.CostEstimate(
            flops=16 * 1024 * 512 * 256 * HALF, bytes_accessed=9 * MIB, transcendentals=0
        ),
        name="valence_response",
    )(place.reshape(1), *([home, away] * 4), screened, screened)


def spectrum_kernel(cos_ref, sin_ref, x_ref, out_ref):
    first = lax.broadcasted_iota(jnp.int32, (1, 128), 1) < 64
    for k in range(8):
        x = x_ref[:, k * 128 : (k + 1) * 128]
        turned = pltpu.roll(x, 64, 1)
        turned = jnp.where(first, turned, -turned)
        cond = dot(cos_ref[...], x, precision=EXACT) + dot(sin_ref[...], turned, precision=EXACT)
        cond = (cond * NORM).astype(BF).astype(F32).T
        out_ref[k * 128 : (k + 1) * 128] = cond.astype(BF)


def cond_spectrum(cosine, sine, columns):
    return pl.pallas_call(
        spectrum_kernel,
        out_shape=jax.ShapeDtypeStruct((1024, 256), BF),
        in_specs=[pl.BlockSpec(memory_space=pltpu.VMEM)] * 3,
        out_specs=pl.BlockSpec(memory_space=pltpu.VMEM),
        compiler_params=pltpu.CompilerParams(vmem_limit_bytes=16 * MIB),
        cost_estimate=pl.CostEstimate(
            flops=24 * 256 * 256 * 1024, bytes_accessed=2 * MIB, transcendentals=0
        ),
        name="cond_spectrum",
    )(cosine, sine, columns)


def block_kernel(cond_ref, r_ref, out_ref):
    first = lax.broadcasted_iota(jnp.int32, (1, 128), 1) < 64
    for k in range(8):
        cond = cond_ref[k * 128 : (k + 1) * 128]
        rows = r_ref[k * 128 : (k + 1) * 128] * NORM
        top = rows.astype(BF)
        rest = (rows - top.astype(F32)).astype(BF)
        prod = dot(cond, top, ((1,), (1,))) + dot(cond, rest, ((1,), (1,)))
        swapped = pltpu.roll(prod[64:], 64, 1)
        both = prod[:64] + jnp.where(first, swapped, -swapped)
        even, odd = both[:32], both[32:]
        out_ref[:, 2 * k, :] = jnp.where(first, even, pltpu.roll(odd, 64, 1))
        out_ref[:, 2 * k + 1, :] = jnp.where(first, pltpu.roll(even, 64, 1), odd)


def kernel_blocks(cond, rows):
    return pl.pallas_call(
        block_kernel,
        out_shape=jax.ShapeDtypeStruct((32, 16, 128), F32),
        in_specs=[pl.BlockSpec(memory_space=pltpu.VMEM)] * 2,
        out_specs=pl.BlockSpec(memory_space=pltpu.VMEM),
        compiler_params=pltpu.CompilerParams(vmem_limit_bytes=16 * MIB),
        cost_estimate=pl.CostEstimate(
            flops=4 * 128 * 256 * 1024, bytes_accessed=2 * MIB, transcendentals=0
        ),
        name="kernel_blocks",
    )(cond, rows)


def line_tables(gmap, place):
    level = lax.dynamic_slice_in_dim(gmap, place * 256, 256) & (NZ - 1)
    column = jnp.arange(256, dtype=jnp.int32)
    angle = (level[:, None] * (column // 8)[None, :]) % NZ
    same = (column // NZ)[:, None] == (column % 8)[None, :]
    angle = angle.astype(F32) * (2.0 * math.pi / NZ)
    return jnp.where(same, jnp.cos(angle), 0.0), jnp.where(same, jnp.sin(angle), 0.0)


def lay_out_kernel(full_ref, rows_ref, mirror_ref):
    low = lax.broadcasted_iota(jnp.int32, (1, 128), 1) < 64
    for m in range(4):
        for n in range(4):
            for c in (2 * n, 2 * n + 1):
                piece = full_ref[m * 4 + n, 0, (c & 1) * 16 : (c & 1) * 16 + 16]
                at = (c * 4 + m) * 128
                rows_ref[:, :, at : at + 128] = piece.reshape(8, 2, 128)
            even, odd = full_ref[m * 4 + n, 1, :16], full_ref[m * 4 + n, 1, 16:]
            first = jnp.where(low, even, pltpu.roll(odd, 64, 1))
            second = jnp.where(low, pltpu.roll(even, 64, 1), odd)
            at = (2 * m * 4 + n) * 128
            mirror_ref[:, :, at : at + 128] = first.reshape(8, 2, 128)
            mirror_ref[:, :, at + 512 : at + 640] = second.reshape(8, 2, 128)


def lay_out(full):
    shape = jax.ShapeDtypeStruct((8, 2, 4096), F32)
    return pl.pallas_call(
        lay_out_kernel,
        in_specs=[pl.BlockSpec(memory_space=pltpu.VMEM)],
        out_specs=[pl.BlockSpec(memory_space=pltpu.VMEM)] * 2,
        out_shape=[shape, shape],
        compiler_params=pltpu.CompilerParams(vmem_limit_bytes=16 * MIB),
        name="lay_out",
    )(full)


def on_device(wavefunctions, partner, gmap, screened):
    ka_place = lax.axis_index(KA)
    place = lax.axis_index(GA)
    owned = ka_place * 8 + jnp.arange(8, dtype=jnp.int32)

    waves = wavefunctions.reshape(8, 2, 2, 8, 256).transpose(0, 2, 1, 3, 4).reshape(8, 32, 256)
    near = spread(waves, "zl").reshape(32, 32, 256)

    index = jnp.arange(PLANE, dtype=jnp.int32)
    negative = (NX - index // NY) % NX * NY + (NY - index % NY) % NY
    negative = jnp.where(place > NZ // 2, negative, index)
    flip = (index[:, None] == negative[None, :]).astype(BF)
    far = turned(near, "co", 1)

    vals, away_cond = choose(partner, near, far, flip)
    planes = cond_planes(waves[:, 16:], away_cond)
    vals = spread(vals, "zh")
    home, away = spread(vals[:, 0], "x"), spread(vals[:, 1], "y")
    home, away, planes, screened = lax.optimization_barrier((home, away, planes, screened))
    homes = [home] + [turned(home, "y", d) for d in range(1, 4)]
    aways = [away] + [turned(away, "x", d) for d in range(1, 3)]
    wide, end = screened_transform(screened, gmap)
    away, planes, end = lax.optimization_barrier((away, planes, end))
    aways.append(turned(away, "x", 3))
    columns = lax.all_to_all(planes, GA, split_axis=0, concat_axis=0, tiled=True)
    home = jnp.stack(homes).reshape(32, 8, 16, 256)
    away = jnp.stack(aways).reshape(32, 8, 16, 256)
    rows = response(place, home, away, wide)
    cond = cond_spectrum(*line_tables(gmap, place), columns)
    blocks = kernel_blocks(cond, rows)

    parts = lax.all_to_all(blocks, ("x", "y"), split_axis=0, concat_axis=0, tiled=True)
    mine = jnp.sum(parts.reshape(16, 2, 16, 128), axis=0)
    everyone = copies_to_all(mine, ("zl", "co", "zh")).reshape(8, 2, 2, 16, 128)
    everyone = everyone[:, 0] + everyone[:, 1]
    mine = lax.dynamic_index_in_dim(everyone, ka_place, keepdims=False)
    everyone = everyone.reshape(8, 2, 8, 256).transpose(0, 2, 1, 3).reshape(64, 512)
    select = (partner[None, :] == owned[:, None]).astype(F32)
    mirror = jnp.dot(select, everyone, precision=EXACT)
    mirror = mirror.reshape(8, 2, 2, 128).transpose(1, 0, 2, 3).reshape(32, 128)
    lane = jnp.arange(128, dtype=jnp.int32)
    moved = lane // 64 * 64 + lane % 8 * 8 + lane // 8 % 8
    turn = (lane[:, None] == moved[None, :]).astype(F32)
    sign = jnp.where(jnp.arange(32) % 2 == 0, 1.0, -1.0).astype(F32)
    mirror = jnp.dot(mirror, turn, precision=EXACT) * sign[:, None]
    full = copies_to_all(jnp.stack([mine.reshape(32, 128), mirror]), ("x", "y"))
    return lay_out(full)


def solution(mesh):
    fine = Mesh(mesh.devices.reshape(SIZES), AXES)
    in_specs = (P(KA, None, None, GA, None), P(), P(), P(GA, None))
    out_specs = (P(KA, None, None), P(KA, None, None))
    return jax.shard_map(
        on_device, mesh=fine, in_specs=in_specs, out_specs=out_specs, check_vma=False
    )
```

```python
import functools
import math

import jax
import jax.numpy as jnp
import numpy as np
from jax import lax
from jax.experimental import pallas as pl
from jax.experimental.pallas import tpu as pltpu
from jax.sharding import Mesh
from jax.sharding import PartitionSpec as P

NX = 16
NY = 16
NZ = 32
NG = 8192
PLANE = NX * NY
HALF = NZ // 2 + 1
LINE_BLOCKS = 4
LINE_STEPS = 32 // LINE_BLOCKS
LINE_ROWS = 32
NORM = 1.0 / math.sqrt(NG)
EXACT = lax.Precision.HIGHEST
BF = jnp.bfloat16
F32 = jnp.float32
MIB = 1 << 20

AXES = ("zl", "co", "x", "y", "zh")
SIZES = (4, 2, 4, 4, 2)
SIZE = dict(zip(AXES, SIZES))
KA = ("zl", "co")
GA = ("x", "y", "zh")


def split_table(table):
    high = table.astype(np.float32).astype(BF)
    low = (table - high.astype(np.float64)).astype(np.float32).astype(BF)
    return high, low


def plane_angles():
    index = np.arange(PLANE)
    x, y = index // NY, index % NY
    turns = (np.outer(x, x) % NX) / NX + (np.outer(y, y) % NY) / NY
    return 2.0 * np.pi * turns


def line_angles():
    index = np.arange(NZ)
    return 2.0 * np.pi * (np.outer(index, index) % NZ) / NZ


def turned(value, axis, step):
    size = SIZE[axis]
    return lax.ppermute(value, axis, [(i, (i + step) % size) for i in range(size)])


def spread(value, axis):
    return jnp.stack([value] + [turned(value, axis, d) for d in range(1, SIZE[axis])])


def copies_to_all(value, axes):
    count = math.prod(SIZE[axis] for axis in axes)
    copies = jnp.broadcast_to(value[None], (count,) + value.shape)
    return lax.all_to_all(copies, axes, split_axis=0, concat_axis=0, tiled=True)


def dot(a, b, contract=((1,), (0,)), precision=None):
    return lax.dot_general(
        a, b, (contract, ((), ())), precision=precision, preferred_element_type=F32
    )


def screened_kernel(n, gmap_ref, line_ref, high_ref, low_ref, w_ref, out_ref, end_ref, lines_ref):
    step = pl.program_id(0)
    end_ref[...] = jnp.zeros_like(end_ref)

    @pl.when(step < LINE_STEPS)
    def _():
        rows = 2 * n
        keep = lax.broadcasted_iota(jnp.int32, (1, 8, 256), 1) == (
            lax.broadcasted_iota(jnp.int32, (1, 8, 256), 2) >> 5
        )
        for b in range(LINE_BLOCKS):
            level = gmap_ref[b] & (NZ - 1)
            hot = (lax.broadcasted_iota(jnp.int32, (NZ, 256), 0) == level).astype(F32).astype(BF)
            picked = dot(line_ref[...], hot)
            tables = []
            for at in (0, LINE_ROWS):
                wide = jnp.broadcast_to(picked[at : at + rows][:, None, :], (rows, 8, 256))
                tables.append(jnp.where(keep, wide, 0.0).reshape(rows * 8, 256).astype(BF))
            block = w_ref[:, b * 256 : (b + 1) * 256]
            both = dot(jnp.concatenate(tables, axis=0), block, ((1,), (1,)))
            total = both[: rows * 8] + both[rows * 8 :]
            at = pl.multiple_of((step * LINE_BLOCKS + b) * 8, 8)
            lines_ref[:, pl.ds(at, 8), :] = total.reshape(rows, 8, 256)

    @pl.when(step >= LINE_STEPS)
    def _():
        z = step - LINE_STEPS
        real, imag = lines_ref[z], lines_ref[n + z]
        for odd in range(2):
            if odd:
                both = [real[:128] - real[128:], imag[:128] - imag[128:]]
            else:
                both = [real[:128] + real[128:], imag[:128] + imag[128:]]
            both = jnp.concatenate(both, axis=0)
            top = both.astype(BF)
            rest = (both - top.astype(F32)).astype(BF)
            high, low = high_ref[odd], low_ref[odd]
            prod = (dot(high, top) + (dot(high, rest) + dot(low, top))).astype(BF)
            for half in range(8):
                at = (2 * half + odd) * NY
                out_ref[0, at : at + NY] = prod[half * NY : (half + 1) * NY]
                out_ref[0, 256 + at : 256 + at + NY] = prod[128 + half * NY : 144 + half * NY]


def screened_transform(screened, gmap, first):
    angles = line_angles()[first:HALF:2]
    n = angles.shape[0]
    table = np.concatenate([np.cos(angles), -np.sin(angles)], axis=0)
    padding = np.zeros((LINE_ROWS - 2 * n, NZ), BF)
    line = np.concatenate([x for part in split_table(table) for x in (part, padding)], axis=0)
    angles = plane_angles().reshape(NX, NY, PLANE)[:, :, :128]
    tables = []
    for odd in range(2):
        part = angles[odd::2].reshape(128, 128)
        cosine, sine = np.cos(part), np.sin(part)
        tables.append(np.block([[cosine, sine], [sine, -cosine]]))
    high, low = split_table(np.stack(tables))
    m = LINE_BLOCKS
    last = LINE_STEPS - 1
    return pl.pallas_call(
        functools.partial(screened_kernel, n),
        grid=(LINE_STEPS + n,),
        in_specs=[
            pl.BlockSpec((m, 1, 256), lambda i: (jnp.minimum(i, last), 0, 0)),
            pl.BlockSpec((2 * LINE_ROWS, NZ), lambda i: (0, 0)),
            pl.BlockSpec((2, 256, 256), lambda i: (0, 0, 0)),
            pl.BlockSpec((2, 256, 256), lambda i: (0, 0, 0)),
            pl.BlockSpec((256, m * 256), lambda i: (0, jnp.minimum(i, last))),
        ],
        out_specs=[
            pl.BlockSpec((1, 512, 256), lambda i: (jnp.maximum(i - LINE_STEPS, 0), 0, 0)),
            pl.BlockSpec((8, 128), lambda i: (0, 0)),
        ],
        out_shape=[
            jax.ShapeDtypeStruct((n, 512, 256), BF),
            jax.ShapeDtypeStruct((8, 128), F32),
        ],
        scratch_shapes=[pltpu.VMEM((2 * n, PLANE, 256), F32)],
        compiler_params=pltpu.CompilerParams(vmem_limit_bytes=24 * MIB),
        cost_estimate=pl.CostEstimate(
            flops=24 * 256 * 256 * 256 * HALF, bytes_accessed=7 * MIB, transcendentals=0
        ),
        name="screened_transform",
    )(gmap.reshape(32, 1, 256), jnp.asarray(line), jnp.asarray(high), jnp.asarray(low), screened)


def choose_kernel(partner_ref, place_ref, flip_ref, near_ref, far_ref, end_ref, val_ref, cond_ref):
    level, core = place_ref[0], place_ref[1]
    for m in range(8):
        val_ref[0, m] = dot(near_ref[m, :16], flip_ref[...]).astype(BF)
        wanted = partner_ref[(level * 2 + core) * 8 + m]
        back = (level - wanted // 16) & 3
        at = back * 8 + (wanted & 7)
        near = (wanted // 8) % 2 == core

        def take(ref, m=m, at=at):
            row = ref[at]
            val_ref[1, m] = dot(row[:16], flip_ref[...]).astype(BF)
            cond_ref[m] = row[16:]

        pl.when(near)(functools.partial(take, near_ref))
        pl.when(jnp.logical_not(near))(functools.partial(take, far_ref))


def choose(partner, near, far, flip, end):
    shape = jax.ShapeDtypeStruct((8, 16, 256), BF)
    place = jnp.stack([lax.axis_index("zl"), lax.axis_index("co")]).astype(jnp.int32)
    return pl.pallas_call(
        choose_kernel,
        in_specs=[pl.BlockSpec(memory_space=pltpu.SMEM)] * 2
        + [pl.BlockSpec(memory_space=pltpu.VMEM)] * 4,
        out_specs=[pl.BlockSpec(memory_space=pltpu.VMEM)] * 2,
        out_shape=[jax.ShapeDtypeStruct((2, 8, 16, 256), BF), shape],
        compiler_params=pltpu.CompilerParams(vmem_limit_bytes=16 * MIB),
        name="partner_choice",
    )(partner, place, flip, near, far, end)


def cond_kernel(table_ref, home_ref, away_ref, x_ref, rows_ref):
    for k in range(8):
        home, away = home_ref[k].astype(F32), away_ref[k].astype(F32)
        hr, hi = home[:8], home[8:]
        for place, band in enumerate((0, 2, 4, 6, 1, 3, 5, 7)):
            ar, ai = away[band : band + 1], away[8 + band : 9 + band]
            real = hr * ar + hi * ai
            imag = hr * ai - hi * ar
            at = k * 128 + place * 8
            rows_ref[at : at + 8, :256] = real
            rows_ref[at : at + 8, 256:] = imag
            rows_ref[at + 64 : at + 72, :256] = imag
            rows_ref[at + 64 : at + 72, 256:] = -real
    for k in range(8):
        x_ref[:, k * 128 : (k + 1) * 128] = dot(
            table_ref[...], rows_ref[k * 128 : (k + 1) * 128], ((1,), (1,)), EXACT
        )


def cond_planes(home, away):
    angles = plane_angles()
    table = np.concatenate([np.cos(angles), np.sin(angles)], axis=1).astype(np.float32)
    return pl.pallas_call(
        cond_kernel,
        out_shape=jax.ShapeDtypeStruct((256, 1024), F32),
        in_specs=[pl.BlockSpec(memory_space=pltpu.VMEM)] * 3,
        out_specs=pl.BlockSpec(memory_space=pltpu.VMEM),
        scratch_shapes=[pltpu.VMEM((1024, 512), F32)],
        compiler_params=pltpu.CompilerParams(vmem_limit_bytes=24 * MIB),
        cost_estimate=pl.CostEstimate(
            flops=12 * 256 * 512 * 1024, bytes_accessed=2 * MIB, transcendentals=0
        ),
        name="cond_planes",
    )(jnp.asarray(table), home, away)


def build_rows(rows_ref, waves, mirrored):
    home_ref, away_ref, home_back_ref, away_back_ref = waves

    def density(home, away, v):
        hr, hi = home[v : v + 1], home[8 + v : 9 + v]
        ar, ai = away[:8], away[8:]
        return hr * ar + hi * ai, hr * ai - hi * ar

    for k in range(8):
        home, away = home_ref[0, k].astype(F32), away_ref[0, k].astype(F32)
        home_back, away_back = home_back_ref[0, k].astype(F32), away_back_ref[0, k].astype(F32)
        if mirrored is not None:
            home_back = home_back * mirrored
        for pair in range(4):
            pieces = []
            for v in (2 * pair, 2 * pair + 1):
                real, imag = density(home, away, v)
                real_back, imag_back = density(home_back, away_back, v)
                pieces.append(
                    (real + real_back, imag - imag_back, imag + imag_back, real_back - real)
                )
            even_re, odd_im, even_im, odd_re = (
                jnp.concatenate(p, axis=0).astype(BF) for p in zip(*pieces)
            )
            at = k * 128 + pair * 16
            rows_ref[at : at + 16, :256] = even_re
            rows_ref[at : at + 16, 256:] = odd_im
            rows_ref[at + 64 : at + 80, :256] = even_im
            rows_ref[at + 64 : at + 80, 256:] = odd_re


def response_kernel(place_ref, *refs):
    first_waves, second_waves = refs[:4], refs[4:8]
    before_ref, w_ref, sum_ref, first_ref, second_ref = refs[8:]
    step = pl.program_id(0)
    mirrored = jnp.where(step % 8 == 0, 0.0, 1.0)
    before = dot(second_ref[...], before_ref[0])
    build_rows(first_ref, first_waves, mirrored)
    total = jnp.where(step == 0, 0.0, sum_ref[...] + before)
    total = total + dot(first_ref[...], w_ref[0])
    build_rows(second_ref, second_waves, None)
    sum_ref[...] = total


def response(place, home, away, even, odd):
    def block(which, second, back):
        def index(step, place_ref):
            z = jnp.minimum(2 * step + second, HALF - 1)
            z = (NZ - z) & (NZ - 1) if back else z
            x = ((place_ref[0] >> 3) - (z >> 3)) & 3
            y = ((place_ref[0] >> 1) - (z >> 1)) & 3
            x, y = (x, y) if which == 0 else (y, x)
            return ((y * 4 + x) * 2 + ((place_ref[0] ^ z) & 1), 0, 0, 0)

        return pl.BlockSpec((1, 8, 16, 256), index)

    blocks = [block(w, s, b) for s in range(2) for b in (False, True) for w in range(2)]
    return pl.pallas_call(
        response_kernel,
        grid_spec=pltpu.PrefetchScalarGridSpec(
            num_scalar_prefetch=1,
            grid=(HALF // 2 + 1,),
            in_specs=blocks
            + [
                pl.BlockSpec((1, 512, 256), lambda i, p: (jnp.maximum(i - 1, 0), 0, 0)),
                pl.BlockSpec((1, 512, 256), lambda i, p: (i, 0, 0)),
            ],
            out_specs=pl.BlockSpec((1024, 256), lambda i, p: (0, 0)),
            scratch_shapes=[pltpu.VMEM((1024, 512), BF), pltpu.VMEM((1024, 512), BF)],
        ),
        out_shape=jax.ShapeDtypeStruct((1024, 256), F32),
        compiler_params=pltpu.CompilerParams(vmem_limit_bytes=20 * MIB),
        cost_estimate=pl.CostEstimate(
            flops=16 * 1024 * 512 * 256 * HALF, bytes_accessed=9 * MIB, transcendentals=0
        ),
        name="valence_response",
    )(place.reshape(1), *([home, away] * 4), odd, even)


def spectrum_kernel(cos_ref, sin_ref, x_ref, out_ref):
    first = lax.broadcasted_iota(jnp.int32, (1, 128), 1) < 64
    for k in range(8):
        x = x_ref[:, k * 128 : (k + 1) * 128]
        turned = pltpu.roll(x, 64, 1)
        turned = jnp.where(first, turned, -turned)
        cond = dot(cos_ref[...], x, precision=EXACT) + dot(sin_ref[...], turned, precision=EXACT)
        cond = (cond * NORM).astype(BF).astype(F32).T
        out_ref[k * 128 : (k + 1) * 128] = cond.astype(BF)


def cond_spectrum(cosine, sine, columns):
    return pl.pallas_call(
        spectrum_kernel,
        out_shape=jax.ShapeDtypeStruct((1024, 256), BF),
        in_specs=[pl.BlockSpec(memory_space=pltpu.VMEM)] * 3,
        out_specs=pl.BlockSpec(memory_space=pltpu.VMEM),
        compiler_params=pltpu.CompilerParams(vmem_limit_bytes=16 * MIB),
        cost_estimate=pl.CostEstimate(
            flops=24 * 256 * 256 * 1024, bytes_accessed=2 * MIB, transcendentals=0
        ),
        name="cond_spectrum",
    )(cosine, sine, columns)


def block_kernel(cond_ref, r_ref, out_ref):
    first = lax.broadcasted_iota(jnp.int32, (1, 128), 1) < 64
    for k in range(8):
        cond = cond_ref[k * 128 : (k + 1) * 128]
        rows = r_ref[k * 128 : (k + 1) * 128] * NORM
        top = rows.astype(BF)
        rest = (rows - top.astype(F32)).astype(BF)
        prod = dot(cond, top, ((1,), (1,))) + dot(cond, rest, ((1,), (1,)))
        swapped = pltpu.roll(prod[64:], 64, 1)
        both = prod[:64] + jnp.where(first, swapped, -swapped)
        even, odd = both[:32], both[32:]
        out_ref[:, 2 * k, :] = jnp.where(first, even, pltpu.roll(odd, 64, 1))
        out_ref[:, 2 * k + 1, :] = jnp.where(first, pltpu.roll(even, 64, 1), odd)


def kernel_blocks(cond, rows):
    return pl.pallas_call(
        block_kernel,
        out_shape=jax.ShapeDtypeStruct((32, 16, 128), F32),
        in_specs=[pl.BlockSpec(memory_space=pltpu.VMEM)] * 2,
        out_specs=pl.BlockSpec(memory_space=pltpu.VMEM),
        compiler_params=pltpu.CompilerParams(vmem_limit_bytes=16 * MIB),
        cost_estimate=pl.CostEstimate(
            flops=4 * 128 * 256 * 1024, bytes_accessed=2 * MIB, transcendentals=0
        ),
        name="kernel_blocks",
    )(cond, rows)


def line_tables(gmap, place):
    level = lax.dynamic_slice_in_dim(gmap, place * 256, 256) & (NZ - 1)
    column = jnp.arange(256, dtype=jnp.int32)
    angle = (level[:, None] * (column // 8)[None, :]) % NZ
    same = (column // NZ)[:, None] == (column % 8)[None, :]
    angle = angle.astype(F32) * (2.0 * math.pi / NZ)
    return jnp.where(same, jnp.cos(angle), 0.0), jnp.where(same, jnp.sin(angle), 0.0)


def lay_out_kernel(full_ref, rows_ref, mirror_ref):
    low = lax.broadcasted_iota(jnp.int32, (1, 128), 1) < 64
    for m in range(4):
        for n in range(4):
            for c in (2 * n, 2 * n + 1):
                piece = full_ref[m * 4 + n, 0, (c & 1) * 16 : (c & 1) * 16 + 16]
                at = (c * 4 + m) * 128
                rows_ref[:, :, at : at + 128] = piece.reshape(8, 2, 128)
            even, odd = full_ref[m * 4 + n, 1, :16], full_ref[m * 4 + n, 1, 16:]
            first = jnp.where(low, even, pltpu.roll(odd, 64, 1))
            second = jnp.where(low, pltpu.roll(even, 64, 1), odd)
            at = (2 * m * 4 + n) * 128
            mirror_ref[:, :, at : at + 128] = first.reshape(8, 2, 128)
            mirror_ref[:, :, at + 512 : at + 640] = second.reshape(8, 2, 128)


def lay_out(full):
    shape = jax.ShapeDtypeStruct((8, 2, 4096), F32)
    return pl.pallas_call(
        lay_out_kernel,
        in_specs=[pl.BlockSpec(memory_space=pltpu.VMEM)],
        out_specs=[pl.BlockSpec(memory_space=pltpu.VMEM)] * 2,
        out_shape=[shape, shape],
        compiler_params=pltpu.CompilerParams(vmem_limit_bytes=16 * MIB),
        name="lay_out",
    )(full)


def on_device(wavefunctions, partner, gmap, screened):
    ka_place = lax.axis_index(KA)
    place = lax.axis_index(GA)
    owned = ka_place * 8 + jnp.arange(8, dtype=jnp.int32)

    waves = wavefunctions.reshape(8, 2, 2, 8, 256).transpose(0, 2, 1, 3, 4).reshape(8, 32, 256)
    near = spread(waves, "zl").reshape(32, 32, 256)

    index = jnp.arange(PLANE, dtype=jnp.int32)
    negative = (NX - index // NY) % NX * NY + (NY - index % NY) % NY
    negative = jnp.where(place > NZ // 2, negative, index)
    flip = (index[:, None] == negative[None, :]).astype(BF)
    even, end = screened_transform(screened, gmap, 0)
    near, end = lax.optimization_barrier((near, end))
    far = turned(near, "co", 1)

    vals, away_cond = choose(partner, near, far, flip, end)
    planes = cond_planes(waves[:, 16:], away_cond)
    vals = spread(vals, "zh")
    home, away = spread(vals[:, 0], "x"), spread(vals[:, 1], "y")
    home, away, planes, screened = lax.optimization_barrier((home, away, planes, screened))
    homes = [home] + [turned(home, "y", d) for d in range(1, 4)]
    aways = [away] + [turned(away, "x", d) for d in range(1, 3)]
    odd, _ = screened_transform(screened, gmap, 1)
    away, planes = lax.optimization_barrier((away, planes))
    aways.append(turned(away, "x", 3))
    columns = lax.all_to_all(planes, GA, split_axis=0, concat_axis=0, tiled=True)
    home = jnp.stack(homes).reshape(32, 8, 16, 256)
    away = jnp.stack(aways).reshape(32, 8, 16, 256)
    rows = response(place, home, away, even, odd)
    cond = cond_spectrum(*line_tables(gmap, place), columns)
    blocks = kernel_blocks(cond, rows)

    parts = lax.all_to_all(blocks, ("x", "y"), split_axis=0, concat_axis=0, tiled=True)
    mine = jnp.sum(parts.reshape(16, 2, 16, 128), axis=0)
    everyone = copies_to_all(mine, ("zl", "co", "zh")).reshape(8, 2, 2, 16, 128)
    everyone = everyone[:, 0] + everyone[:, 1]
    mine = lax.dynamic_index_in_dim(everyone, ka_place, keepdims=False)
    everyone = everyone.reshape(8, 2, 8, 256).transpose(0, 2, 1, 3).reshape(64, 512)
    select = (partner[None, :] == owned[:, None]).astype(F32)
    mirror = jnp.dot(select, everyone, precision=EXACT)
    mirror = mirror.reshape(8, 2, 2, 128).transpose(1, 0, 2, 3).reshape(32, 128)
    lane = jnp.arange(128, dtype=jnp.int32)
    moved = lane // 64 * 64 + lane % 8 * 8 + lane // 8 % 8
    turn = (lane[:, None] == moved[None, :]).astype(F32)
    sign = jnp.where(jnp.arange(32) % 2 == 0, 1.0, -1.0).astype(F32)
    mirror = jnp.dot(mirror, turn, precision=EXACT) * sign[:, None]
    full = copies_to_all(jnp.stack([mine.reshape(32, 128), mirror]), ("x", "y"))
    return lay_out(full)


def solution(mesh):
    fine = Mesh(mesh.devices.reshape(SIZES), AXES)
    in_specs = (P(KA, None, None, GA, None), P(), P(), P(GA, None))
    out_specs = (P(KA, None, None), P(KA, None, None))
    return jax.shard_map(
        on_device, mesh=fine, in_specs=in_specs, out_specs=out_specs, check_vma=False
    )
```

```python
import functools
import math

import jax
import jax.numpy as jnp
import numpy as np
from jax import lax
from jax.experimental import pallas as pl
from jax.experimental.pallas import tpu as pltpu
from jax.sharding import Mesh
from jax.sharding import PartitionSpec as P

NX = 16
NY = 16
NZ = 32
NG = 8192
PLANE = NX * NY
HALF = NZ // 2 + 1
LINE_BLOCKS = 4
LINE_STEPS = 32 // LINE_BLOCKS
LINE_ROWS = 32
NORM = 1.0 / math.sqrt(NG)
EXACT = lax.Precision.HIGHEST
BF = jnp.bfloat16
F32 = jnp.float32
MIB = 1 << 20

AXES = ("zl", "co", "x", "y", "zh")
SIZES = (4, 2, 4, 4, 2)
SIZE = dict(zip(AXES, SIZES))
KA = ("zl", "co")
GA = ("x", "y", "zh")


def split_table(table):
    high = table.astype(np.float32).astype(BF)
    low = (table - high.astype(np.float64)).astype(np.float32).astype(BF)
    return high, low


def plane_angles():
    index = np.arange(PLANE)
    x, y = index // NY, index % NY
    turns = (np.outer(x, x) % NX) / NX + (np.outer(y, y) % NY) / NY
    return 2.0 * np.pi * turns


def line_angles():
    index = np.arange(NZ)
    return 2.0 * np.pi * (np.outer(index, index) % NZ) / NZ


def turned(value, axis, step):
    size = SIZE[axis]
    return lax.ppermute(value, axis, [(i, (i + step) % size) for i in range(size)])


def spread(value, axis):
    return jnp.stack([value] + [turned(value, axis, d) for d in range(1, SIZE[axis])])


def copies_to_all(value, axes):
    count = math.prod(SIZE[axis] for axis in axes)
    copies = jnp.broadcast_to(value[None], (count,) + value.shape)
    return lax.all_to_all(copies, axes, split_axis=0, concat_axis=0, tiled=True)


def dot(a, b, contract=((1,), (0,)), precision=None):
    return lax.dot_general(
        a, b, (contract, ((), ())), precision=precision, preferred_element_type=F32
    )


def screened_kernel(n, gmap_ref, line_ref, high_ref, low_ref, w_ref, out_ref, end_ref, lines_ref):
    step = pl.program_id(0)
    end_ref[...] = jnp.zeros_like(end_ref)

    @pl.when(step < LINE_STEPS)
    def _():
        rows = 2 * n
        keep = lax.broadcasted_iota(jnp.int32, (1, 8, 256), 1) == (
            lax.broadcasted_iota(jnp.int32, (1, 8, 256), 2) >> 5
        )
        for b in range(LINE_BLOCKS):
            level = gmap_ref[b] & (NZ - 1)
            hot = (lax.broadcasted_iota(jnp.int32, (NZ, 256), 0) == level).astype(F32).astype(BF)
            picked = dot(line_ref[...], hot)
            tables = []
            for at in (0, LINE_ROWS):
                wide = jnp.broadcast_to(picked[at : at + rows][:, None, :], (rows, 8, 256))
                tables.append(jnp.where(keep, wide, 0.0).reshape(rows * 8, 256).astype(BF))
            block = w_ref[:, b * 256 : (b + 1) * 256]
            both = dot(jnp.concatenate(tables, axis=0), block, ((1,), (1,)))
            total = both[: rows * 8] + both[rows * 8 :]
            at = pl.multiple_of((step * LINE_BLOCKS + b) * 8, 8)
            lines_ref[:, pl.ds(at, 8), :] = total.reshape(rows, 8, 256)

    @pl.when(step >= LINE_STEPS)
    def _():
        z = step - LINE_STEPS
        real, imag = lines_ref[z], lines_ref[n + z]
        for odd in range(2):
            if odd:
                both = [real[:128] - real[128:], imag[:128] - imag[128:]]
            else:
                both = [real[:128] + real[128:], imag[:128] + imag[128:]]
            both = jnp.concatenate(both, axis=0)
            top = both.astype(BF)
            rest = (both - top.astype(F32)).astype(BF)
            high, low = high_ref[odd], low_ref[odd]
            prod = (dot(high, top) + (dot(high, rest) + dot(low, top))).astype(BF)
            for half in range(8):
                at = (2 * half + odd) * NY
                out_ref[0, at : at + NY] = prod[half * NY : (half + 1) * NY]
                out_ref[0, 256 + at : 256 + at + NY] = prod[128 + half * NY : 144 + half * NY]


def screened_transform(screened, gmap, first, room):
    angles = line_angles()[first:HALF:2]
    n = angles.shape[0]
    table = np.concatenate([np.cos(angles), -np.sin(angles)], axis=0)
    padding = np.zeros((LINE_ROWS - 2 * n, NZ), BF)
    line = np.concatenate([x for part in split_table(table) for x in (part, padding)], axis=0)
    angles = plane_angles().reshape(NX, NY, PLANE)[:, :, :128]
    tables = []
    for odd in range(2):
        part = angles[odd::2].reshape(128, 128)
        cosine, sine = np.cos(part), np.sin(part)
        tables.append(np.block([[cosine, sine], [sine, -cosine]]))
    high, low = split_table(np.stack(tables))
    m = LINE_BLOCKS
    last = LINE_STEPS - 1
    return pl.pallas_call(
        functools.partial(screened_kernel, n),
        grid=(LINE_STEPS + n,),
        in_specs=[
            pl.BlockSpec((m, 1, 256), lambda i: (jnp.minimum(i, last), 0, 0)),
            pl.BlockSpec((2 * LINE_ROWS, NZ), lambda i: (0, 0)),
            pl.BlockSpec((2, 256, 256), lambda i: (0, 0, 0)),
            pl.BlockSpec((2, 256, 256), lambda i: (0, 0, 0)),
            pl.BlockSpec((256, m * 256), lambda i: (0, jnp.minimum(i, last))),
        ],
        out_specs=[
            pl.BlockSpec((1, 512, 256), lambda i: (jnp.maximum(i - LINE_STEPS, 0), 0, 0)),
            pl.BlockSpec((8, 128), lambda i: (0, 0)),
        ],
        out_shape=[
            jax.ShapeDtypeStruct((n, 512, 256), BF),
            jax.ShapeDtypeStruct((8, 128), F32),
        ],
        scratch_shapes=[pltpu.VMEM((2 * n, PLANE, 256), F32)],
        compiler_params=pltpu.CompilerParams(vmem_limit_bytes=room * MIB),
        cost_estimate=pl.CostEstimate(
            flops=24 * 256 * 256 * 256 * HALF, bytes_accessed=7 * MIB, transcendentals=0
        ),
        name="screened_transform",
    )(gmap.reshape(32, 1, 256), jnp.asarray(line), jnp.asarray(high), jnp.asarray(low), screened)


def choose_kernel(partner_ref, place_ref, flip_ref, near_ref, far_ref, end_ref, val_ref, cond_ref):
    level, core = place_ref[0], place_ref[1]
    for m in range(8):
        val_ref[0, m] = dot(near_ref[m, :16], flip_ref[...]).astype(BF)
        wanted = partner_ref[(level * 2 + core) * 8 + m]
        back = (level - wanted // 16) & 3
        at = back * 8 + (wanted & 7)
        near = (wanted // 8) % 2 == core

        def take(ref, m=m, at=at):
            row = ref[at]
            val_ref[1, m] = dot(row[:16], flip_ref[...]).astype(BF)
            cond_ref[m] = row[16:]

        pl.when(near)(functools.partial(take, near_ref))
        pl.when(jnp.logical_not(near))(functools.partial(take, far_ref))


def choose(partner, near, far, flip, end):
    shape = jax.ShapeDtypeStruct((8, 16, 256), BF)
    place = jnp.stack([lax.axis_index("zl"), lax.axis_index("co")]).astype(jnp.int32)
    return pl.pallas_call(
        choose_kernel,
        in_specs=[pl.BlockSpec(memory_space=pltpu.SMEM)] * 2
        + [pl.BlockSpec(memory_space=pltpu.VMEM)] * 4,
        out_specs=[pl.BlockSpec(memory_space=pltpu.VMEM)] * 2,
        out_shape=[jax.ShapeDtypeStruct((2, 8, 16, 256), BF), shape],
        compiler_params=pltpu.CompilerParams(vmem_limit_bytes=16 * MIB),
        name="partner_choice",
    )(partner, place, flip, near, far, end)


def cond_kernel(table_ref, home_ref, away_ref, x_ref, rows_ref):
    for k in range(8):
        home, away = home_ref[k].astype(F32), away_ref[k].astype(F32)
        hr, hi = home[:8], home[8:]
        for place, band in enumerate((0, 2, 4, 6, 1, 3, 5, 7)):
            ar, ai = away[band : band + 1], away[8 + band : 9 + band]
            real = hr * ar + hi * ai
            imag = hr * ai - hi * ar
            at = k * 128 + place * 8
            rows_ref[at : at + 8, :256] = real
            rows_ref[at : at + 8, 256:] = imag
            rows_ref[at + 64 : at + 72, :256] = imag
            rows_ref[at + 64 : at + 72, 256:] = -real
    for k in range(8):
        x_ref[:, k * 128 : (k + 1) * 128] = dot(
            table_ref[...], rows_ref[k * 128 : (k + 1) * 128], ((1,), (1,)), EXACT
        )


def cond_planes(home, away):
    angles = plane_angles()
    table = np.concatenate([np.cos(angles), np.sin(angles)], axis=1).astype(np.float32)
    return pl.pallas_call(
        cond_kernel,
        out_shape=jax.ShapeDtypeStruct((256, 1024), F32),
        in_specs=[pl.BlockSpec(memory_space=pltpu.VMEM)] * 3,
        out_specs=pl.BlockSpec(memory_space=pltpu.VMEM),
        scratch_shapes=[pltpu.VMEM((1024, 512), F32)],
        compiler_params=pltpu.CompilerParams(vmem_limit_bytes=24 * MIB),
        cost_estimate=pl.CostEstimate(
            flops=12 * 256 * 512 * 1024, bytes_accessed=2 * MIB, transcendentals=0
        ),
        name="cond_planes",
    )(jnp.asarray(table), home, away)


def build_rows(rows_ref, waves, mirrored):
    home_ref, away_ref, home_back_ref, away_back_ref = waves

    def density(home, away, v):
        hr, hi = home[v : v + 1], home[8 + v : 9 + v]
        ar, ai = away[:8], away[8:]
        return hr * ar + hi * ai, hr * ai - hi * ar

    for k in range(8):
        home, away = home_ref[0, k].astype(F32), away_ref[0, k].astype(F32)
        home_back, away_back = home_back_ref[0, k].astype(F32), away_back_ref[0, k].astype(F32)
        if mirrored is not None:
            home_back = home_back * mirrored
        for pair in range(4):
            pieces = []
            for v in (2 * pair, 2 * pair + 1):
                real, imag = density(home, away, v)
                real_back, imag_back = density(home_back, away_back, v)
                pieces.append(
                    (real + real_back, imag - imag_back, imag + imag_back, real_back - real)
                )
            even_re, odd_im, even_im, odd_re = (
                jnp.concatenate(p, axis=0).astype(BF) for p in zip(*pieces)
            )
            at = k * 128 + pair * 16
            rows_ref[at : at + 16, :256] = even_re
            rows_ref[at : at + 16, 256:] = odd_im
            rows_ref[at + 64 : at + 80, :256] = even_im
            rows_ref[at + 64 : at + 80, 256:] = odd_re


def response_kernel(place_ref, *refs):
    first_waves, second_waves = refs[:4], refs[4:8]
    before_ref, w_ref, sum_ref, first_ref, second_ref = refs[8:]
    step = pl.program_id(0)
    mirrored = jnp.where(step % 8 == 0, 0.0, 1.0)
    before = dot(second_ref[...], before_ref[0])
    build_rows(first_ref, first_waves, mirrored)
    total = jnp.where(step == 0, 0.0, sum_ref[...] + before)
    total = total + dot(first_ref[...], w_ref[0])
    build_rows(second_ref, second_waves, None)
    sum_ref[...] = total


def response(place, home, away, even, odd):
    def block(which, second, back):
        def index(step, place_ref):
            z = jnp.minimum(2 * step + second, HALF - 1)
            z = (NZ - z) & (NZ - 1) if back else z
            x = ((place_ref[0] >> 3) - (z >> 3)) & 3
            y = ((place_ref[0] >> 1) - (z >> 1)) & 3
            x, y = (x, y) if which == 0 else (y, x)
            return ((y * 4 + x) * 2 + ((place_ref[0] ^ z) & 1), 0, 0, 0)

        return pl.BlockSpec((1, 8, 16, 256), index)

    blocks = [block(w, s, b) for s in range(2) for b in (False, True) for w in range(2)]
    return pl.pallas_call(
        response_kernel,
        grid_spec=pltpu.PrefetchScalarGridSpec(
            num_scalar_prefetch=1,
            grid=(HALF // 2 + 1,),
            in_specs=blocks
            + [
                pl.BlockSpec((1, 512, 256), lambda i, p: (jnp.maximum(i - 1, 0), 0, 0)),
                pl.BlockSpec((1, 512, 256), lambda i, p: (i, 0, 0)),
            ],
            out_specs=pl.BlockSpec((1024, 256), lambda i, p: (0, 0)),
            scratch_shapes=[pltpu.VMEM((1024, 512), BF), pltpu.VMEM((1024, 512), BF)],
        ),
        out_shape=jax.ShapeDtypeStruct((1024, 256), F32),
        compiler_params=pltpu.CompilerParams(vmem_limit_bytes=20 * MIB),
        cost_estimate=pl.CostEstimate(
            flops=16 * 1024 * 512 * 256 * HALF, bytes_accessed=9 * MIB, transcendentals=0
        ),
        name="valence_response",
    )(place.reshape(1), *([home, away] * 4), odd, even)


def spectrum_kernel(cos_ref, sin_ref, x_ref, out_ref):
    first = lax.broadcasted_iota(jnp.int32, (1, 128), 1) < 64
    for k in range(8):
        x = x_ref[:, k * 128 : (k + 1) * 128]
        turned = pltpu.roll(x, 64, 1)
        turned = jnp.where(first, turned, -turned)
        cond = dot(cos_ref[...], x, precision=EXACT) + dot(sin_ref[...], turned, precision=EXACT)
        cond = (cond * NORM).astype(BF).astype(F32).T
        out_ref[k * 128 : (k + 1) * 128] = cond.astype(BF)


def cond_spectrum(cosine, sine, columns):
    return pl.pallas_call(
        spectrum_kernel,
        out_shape=jax.ShapeDtypeStruct((1024, 256), BF),
        in_specs=[pl.BlockSpec(memory_space=pltpu.VMEM)] * 3,
        out_specs=pl.BlockSpec(memory_space=pltpu.VMEM),
        compiler_params=pltpu.CompilerParams(vmem_limit_bytes=16 * MIB),
        cost_estimate=pl.CostEstimate(
            flops=24 * 256 * 256 * 1024, bytes_accessed=2 * MIB, transcendentals=0
        ),
        name="cond_spectrum",
    )(cosine, sine, columns)


def block_kernel(cond_ref, r_ref, out_ref):
    first = lax.broadcasted_iota(jnp.int32, (1, 128), 1) < 64
    for k in range(8):
        cond = cond_ref[k * 128 : (k + 1) * 128]
        rows = r_ref[k * 128 : (k + 1) * 128] * NORM
        top = rows.astype(BF)
        rest = (rows - top.astype(F32)).astype(BF)
        prod = dot(cond, top, ((1,), (1,))) + dot(cond, rest, ((1,), (1,)))
        swapped = pltpu.roll(prod[64:], 64, 1)
        both = prod[:64] + jnp.where(first, swapped, -swapped)
        even, odd = both[:32], both[32:]
        out_ref[:, 2 * k, :] = jnp.where(first, even, pltpu.roll(odd, 64, 1))
        out_ref[:, 2 * k + 1, :] = jnp.where(first, pltpu.roll(even, 64, 1), odd)


def kernel_blocks(cond, rows):
    return pl.pallas_call(
        block_kernel,
        out_shape=jax.ShapeDtypeStruct((32, 16, 128), F32),
        in_specs=[pl.BlockSpec(memory_space=pltpu.VMEM)] * 2,
        out_specs=pl.BlockSpec(memory_space=pltpu.VMEM),
        compiler_params=pltpu.CompilerParams(vmem_limit_bytes=16 * MIB),
        cost_estimate=pl.CostEstimate(
            flops=4 * 128 * 256 * 1024, bytes_accessed=2 * MIB, transcendentals=0
        ),
        name="kernel_blocks",
    )(cond, rows)


def line_tables(gmap, place):
    level = lax.dynamic_slice_in_dim(gmap, place * 256, 256) & (NZ - 1)
    column = jnp.arange(256, dtype=jnp.int32)
    angle = (level[:, None] * (column // 8)[None, :]) % NZ
    same = (column // NZ)[:, None] == (column % 8)[None, :]
    angle = angle.astype(F32) * (2.0 * math.pi / NZ)
    return jnp.where(same, jnp.cos(angle), 0.0), jnp.where(same, jnp.sin(angle), 0.0)


def lay_out_kernel(full_ref, rows_ref, mirror_ref):
    low = lax.broadcasted_iota(jnp.int32, (1, 128), 1) < 64
    for m in range(4):
        for n in range(4):
            for c in (2 * n, 2 * n + 1):
                piece = full_ref[m * 4 + n, 0, (c & 1) * 16 : (c & 1) * 16 + 16]
                at = (c * 4 + m) * 128
                rows_ref[:, :, at : at + 128] = piece.reshape(8, 2, 128)
            even, odd = full_ref[m * 4 + n, 1, :16], full_ref[m * 4 + n, 1, 16:]
            first = jnp.where(low, even, pltpu.roll(odd, 64, 1))
            second = jnp.where(low, pltpu.roll(even, 64, 1), odd)
            at = (2 * m * 4 + n) * 128
            mirror_ref[:, :, at : at + 128] = first.reshape(8, 2, 128)
            mirror_ref[:, :, at + 512 : at + 640] = second.reshape(8, 2, 128)


def lay_out(full):
    shape = jax.ShapeDtypeStruct((8, 2, 4096), F32)
    return pl.pallas_call(
        lay_out_kernel,
        in_specs=[pl.BlockSpec(memory_space=pltpu.VMEM)],
        out_specs=[pl.BlockSpec(memory_space=pltpu.VMEM)] * 2,
        out_shape=[shape, shape],
        compiler_params=pltpu.CompilerParams(vmem_limit_bytes=16 * MIB),
        name="lay_out",
    )(full)


def on_device(wavefunctions, partner, gmap, screened):
    ka_place = lax.axis_index(KA)
    place = lax.axis_index(GA)
    owned = ka_place * 8 + jnp.arange(8, dtype=jnp.int32)

    waves = wavefunctions.reshape(8, 2, 2, 8, 256).transpose(0, 2, 1, 3, 4).reshape(8, 32, 256)
    near = spread(waves, "zl").reshape(32, 32, 256)

    index = jnp.arange(PLANE, dtype=jnp.int32)
    negative = (NX - index // NY) % NX * NY + (NY - index % NY) % NY
    negative = jnp.where(place > NZ // 2, negative, index)
    flip = (index[:, None] == negative[None, :]).astype(BF)
    even, end = screened_transform(screened, gmap, 0, 54)
    near, end = lax.optimization_barrier((near, end))
    far = turned(near, "co", 1)

    vals, away_cond = choose(partner, near, far, flip, end)
    planes = cond_planes(waves[:, 16:], away_cond)
    vals = spread(vals, "zh")
    home, away = spread(vals[:, 0], "x"), spread(vals[:, 1], "y")
    home, away, planes, screened = lax.optimization_barrier((home, away, planes, screened))
    homes = [home] + [turned(home, "y", d) for d in range(1, 4)]
    aways = [away] + [turned(away, "x", d) for d in range(1, 3)]
    odd, _ = screened_transform(screened, gmap, 1, 24)
    away, planes = lax.optimization_barrier((away, planes))
    aways.append(turned(away, "x", 3))
    columns = lax.all_to_all(planes, GA, split_axis=0, concat_axis=0, tiled=True)
    home = jnp.stack(homes).reshape(32, 8, 16, 256)
    away = jnp.stack(aways).reshape(32, 8, 16, 256)
    cond = cond_spectrum(*line_tables(gmap, place), columns)
    home, cond = lax.optimization_barrier((home, cond))
    rows = response(place, home, away, even, odd)
    blocks = kernel_blocks(cond, rows)

    parts = lax.all_to_all(blocks, ("x", "y"), split_axis=0, concat_axis=0, tiled=True)
    mine = jnp.sum(parts.reshape(16, 2, 16, 128), axis=0)
    everyone = copies_to_all(mine, ("zl", "co", "zh")).reshape(8, 2, 2, 16, 128)
    everyone = everyone[:, 0] + everyone[:, 1]
    mine = lax.dynamic_index_in_dim(everyone, ka_place, keepdims=False)
    everyone = everyone.reshape(8, 2, 8, 256).transpose(0, 2, 1, 3).reshape(64, 512)
    select = (partner[None, :] == owned[:, None]).astype(F32)
    mirror = jnp.dot(select, everyone, precision=EXACT)
    mirror = mirror.reshape(8, 2, 2, 128).transpose(1, 0, 2, 3).reshape(32, 128)
    lane = jnp.arange(128, dtype=jnp.int32)
    moved = lane // 64 * 64 + lane % 8 * 8 + lane // 8 % 8
    turn = (lane[:, None] == moved[None, :]).astype(F32)
    sign = jnp.where(jnp.arange(32) % 2 == 0, 1.0, -1.0).astype(F32)
    mirror = jnp.dot(mirror, turn, precision=EXACT) * sign[:, None]
    full = copies_to_all(jnp.stack([mine.reshape(32, 128), mirror]), ("x", "y"))
    return lay_out(full)


def solution(mesh):
    fine = Mesh(mesh.devices.reshape(SIZES), AXES)
    in_specs = (P(KA, None, None, GA, None), P(), P(), P(GA, None))
    out_specs = (P(KA, None, None), P(KA, None, None))
    return jax.shard_map(
        on_device, mesh=fine, in_specs=in_specs, out_specs=out_specs, check_vma=False
    )
```

```python
import functools
import math

import jax
import jax.numpy as jnp
import numpy as np
from jax import lax
from jax.experimental import pallas as pl
from jax.experimental.pallas import tpu as pltpu
from jax.sharding import Mesh
from jax.sharding import PartitionSpec as P

NX = 16
NY = 16
NZ = 32
NG = 8192
PLANE = NX * NY
HALF = NZ // 2 + 1
LINE_BLOCKS = 4
LINE_STEPS = 32 // LINE_BLOCKS
LINE_ROWS = 48
NORM = 1.0 / math.sqrt(NG)
EXACT = lax.Precision.HIGHEST
BF = jnp.bfloat16
F32 = jnp.float32
MIB = 1 << 20

AXES = ("zl", "co", "x", "y", "zh")
SIZES = (4, 2, 4, 4, 2)
SIZE = dict(zip(AXES, SIZES))
KA = ("zl", "co")
GA = ("x", "y", "zh")


def split_table(table):
    high = table.astype(np.float32).astype(BF)
    low = (table - high.astype(np.float64)).astype(np.float32).astype(BF)
    return high, low


def plane_angles():
    index = np.arange(PLANE)
    x, y = index // NY, index % NY
    turns = (np.outer(x, x) % NX) / NX + (np.outer(y, y) % NY) / NY
    return 2.0 * np.pi * turns


def line_angles():
    index = np.arange(NZ)
    return 2.0 * np.pi * (np.outer(index, index) % NZ) / NZ


def turned(value, axis, step):
    size = SIZE[axis]
    return lax.ppermute(value, axis, [(i, (i + step) % size) for i in range(size)])


def spread(value, axis):
    return jnp.stack([value] + [turned(value, axis, d) for d in range(1, SIZE[axis])])


def copies_to_all(value, axes):
    count = math.prod(SIZE[axis] for axis in axes)
    copies = jnp.broadcast_to(value[None], (count,) + value.shape)
    return lax.all_to_all(copies, axes, split_axis=0, concat_axis=0, tiled=True)


def dot(a, b, contract=((1,), (0,)), precision=None):
    return lax.dot_general(
        a, b, (contract, ((), ())), precision=precision, preferred_element_type=F32
    )


def screened_kernel(gmap_ref, line_ref, high_ref, low_ref, w_ref, out_ref, end_ref, lines_ref):
    step = pl.program_id(0)
    end_ref[...] = jnp.zeros_like(end_ref)

    @pl.when(step < LINE_STEPS)
    def _():
        rows = 2 * HALF
        keep = lax.broadcasted_iota(jnp.int32, (1, 8, 256), 1) == (
            lax.broadcasted_iota(jnp.int32, (1, 8, 256), 2) >> 5
        )
        for b in range(LINE_BLOCKS):
            level = gmap_ref[b] & (NZ - 1)
            hot = (lax.broadcasted_iota(jnp.int32, (NZ, 256), 0) == level).astype(F32).astype(BF)
            picked = dot(line_ref[...], hot)
            tables = []
            for at in (0, LINE_ROWS):
                wide = jnp.broadcast_to(picked[at : at + rows][:, None, :], (rows, 8, 256))
                tables.append(jnp.where(keep, wide, 0.0).reshape(rows * 8, 256).astype(BF))
            block = w_ref[:, b * 256 : (b + 1) * 256]
            both = dot(jnp.concatenate(tables, axis=0), block, ((1,), (1,)))
            total = both[: rows * 8] + both[rows * 8 :]
            at = pl.multiple_of((step * LINE_BLOCKS + b) * 8, 8)
            lines_ref[:, pl.ds(at, 8), :] = total.reshape(rows, 8, 256)

    @pl.when(step >= LINE_STEPS)
    def _():
        z = step - LINE_STEPS
        real, imag = lines_ref[z], lines_ref[HALF + z]
        for odd in range(2):
            if odd:
                both = [real[:128] - real[128:], imag[:128] - imag[128:]]
            else:
                both = [real[:128] + real[128:], imag[:128] + imag[128:]]
            both = jnp.concatenate(both, axis=0)
            top = both.astype(BF)
            rest = (both - top.astype(F32)).astype(BF)
            high, low = high_ref[odd], low_ref[odd]
            prod = (dot(high, top) + (dot(high, rest) + dot(low, top))).astype(BF)
            for half in range(8):
                at = (2 * half + odd) * NY
                out_ref[0, at : at + NY] = prod[half * NY : (half + 1) * NY]
                out_ref[0, 256 + at : 256 + at + NY] = prod[128 + half * NY : 144 + half * NY]


def screened_transform(screened, gmap):
    angles = line_angles()[:HALF]
    table = np.concatenate([np.cos(angles), -np.sin(angles)], axis=0)
    padding = np.zeros((LINE_ROWS - 2 * HALF, NZ), BF)
    line = np.concatenate([x for part in split_table(table) for x in (part, padding)], axis=0)
    angles = plane_angles().reshape(NX, NY, PLANE)[:, :, :128]
    tables = []
    for odd in range(2):
        part = angles[odd::2].reshape(128, 128)
        cosine, sine = np.cos(part), np.sin(part)
        tables.append(np.block([[cosine, sine], [sine, -cosine]]))
    high, low = split_table(np.stack(tables))
    n = LINE_BLOCKS
    last = LINE_STEPS - 1
    return pl.pallas_call(
        screened_kernel,
        grid=(LINE_STEPS + HALF,),
        in_specs=[
            pl.BlockSpec((n, 1, 256), lambda i: (jnp.minimum(i, last), 0, 0)),
            pl.BlockSpec((2 * LINE_ROWS, NZ), lambda i: (0, 0)),
            pl.BlockSpec((2, 256, 256), lambda i: (0, 0, 0)),
            pl.BlockSpec((2, 256, 256), lambda i: (0, 0, 0)),
            pl.BlockSpec((256, n * 256), lambda i: (0, jnp.minimum(i, last))),
        ],
        out_specs=[
            pl.BlockSpec((1, 512, 256), lambda i: (jnp.maximum(i - LINE_STEPS, 0), 0, 0)),
            pl.BlockSpec((8, 128), lambda i: (0, 0)),
        ],
        out_shape=[
            jax.ShapeDtypeStruct((HALF, 512, 256), BF),
            jax.ShapeDtypeStruct((8, 128), F32),
        ],
        scratch_shapes=[pltpu.VMEM((2 * HALF, PLANE, 256), F32)],
        compiler_params=pltpu.CompilerParams(vmem_limit_bytes=40 * MIB),
        cost_estimate=pl.CostEstimate(
            flops=48 * 256 * 256 * 256 * HALF, bytes_accessed=9 * MIB, transcendentals=0
        ),
        name="screened_transform",
    )(gmap.reshape(32, 1, 256), jnp.asarray(line), jnp.asarray(high), jnp.asarray(low), screened)


def halves(value):
    high = value.astype(BF)
    return high, (value - high.astype(F32)).astype(BF)


def dot_halves(a, b, contract=((1,), (0,))):
    return dot(a[0], b[0], contract) + (dot(a[0], b[1], contract) + dot(a[1], b[0], contract))


def choose_kernel(partner_ref, place_ref, flip_ref, near_ref, far_ref, val_ref, cond_ref):
    level, core = place_ref[0], place_ref[1]
    for m in range(8):
        val_ref[0, m] = dot(near_ref[m, :16], flip_ref[...]).astype(BF)
        wanted = partner_ref[(level * 2 + core) * 8 + m]
        back = (level - wanted // 16) & 3
        at = back * 8 + (wanted & 7)
        near = (wanted // 8) % 2 == core

        def take(ref, m=m, at=at):
            row = ref[at]
            val_ref[1, m] = dot(row[:16], flip_ref[...]).astype(BF)
            cond_ref[m] = row[16:]

        pl.when(near)(functools.partial(take, near_ref))
        pl.when(jnp.logical_not(near))(functools.partial(take, far_ref))


def choose(partner, near, far, flip):
    shape = jax.ShapeDtypeStruct((8, 16, 256), BF)
    place = jnp.stack([lax.axis_index("zl"), lax.axis_index("co")]).astype(jnp.int32)
    return pl.pallas_call(
        choose_kernel,
        in_specs=[pl.BlockSpec(memory_space=pltpu.SMEM)] * 2
        + [pl.BlockSpec(memory_space=pltpu.VMEM)] * 3,
        out_specs=[pl.BlockSpec(memory_space=pltpu.VMEM)] * 2,
        out_shape=[jax.ShapeDtypeStruct((2, 8, 16, 256), BF), shape],
        compiler_params=pltpu.CompilerParams(vmem_limit_bytes=16 * MIB),
        name="partner_choice",
    )(partner, place, flip, near, far)


def cond_kernel(high_ref, low_ref, home_ref, away_ref, x_ref, rows_ref):
    for k in range(8):
        home, away = home_ref[k].astype(F32), away_ref[k].astype(F32)
        hr, hi = home[:8], home[8:]
        for place, band in enumerate((0, 2, 4, 6, 1, 3, 5, 7)):
            ar, ai = away[band : band + 1], away[8 + band : 9 + band]
            real = hr * ar + hi * ai
            imag = hr * ai - hi * ar
            at = k * 128 + place * 8
            rows_ref[at : at + 8, :256] = real
            rows_ref[at : at + 8, 256:] = imag
            rows_ref[at + 64 : at + 72, :256] = imag
            rows_ref[at + 64 : at + 72, 256:] = -real
    table = high_ref[...], low_ref[...]
    for k in range(4):
        rows = halves(rows_ref[k * 256 : (k + 1) * 256])
        x_ref[:, k * 256 : (k + 1) * 256] = dot_halves(table, rows, ((1,), (1,)))


def cond_planes(home, away):
    angles = plane_angles()
    high, low = split_table(np.concatenate([np.cos(angles), np.sin(angles)], axis=1))
    return pl.pallas_call(
        cond_kernel,
        out_shape=jax.ShapeDtypeStruct((256, 1024), F32),
        in_specs=[pl.BlockSpec(memory_space=pltpu.VMEM)] * 4,
        out_specs=pl.BlockSpec(memory_space=pltpu.VMEM),
        scratch_shapes=[pltpu.VMEM((1024, 512), F32)],
        compiler_params=pltpu.CompilerParams(vmem_limit_bytes=24 * MIB),
        cost_estimate=pl.CostEstimate(
            flops=12 * 256 * 512 * 1024, bytes_accessed=2 * MIB, transcendentals=0
        ),
        name="cond_planes",
    )(jnp.asarray(high), jnp.asarray(low), home, away)


def build_rows(rows_ref, waves, mirrored):
    home_ref, away_ref, home_back_ref, away_back_ref = waves

    def density(home, away, v):
        hr, hi = home[v : v + 1], home[8 + v : 9 + v]
        ar, ai = away[:8], away[8:]
        return hr * ar + hi * ai, hr * ai - hi * ar

    for k in range(8):
        home, away = home_ref[0, k].astype(F32), away_ref[0, k].astype(F32)
        home_back, away_back = home_back_ref[0, k].astype(F32), away_back_ref[0, k].astype(F32)
        if mirrored is not None:
            home_back = home_back * mirrored
        for pair in range(4):
            pieces = []
            for v in (2 * pair, 2 * pair + 1):
                real, imag = density(home, away, v)
                real_back, imag_back = density(home_back, away_back, v)
                pieces.append(
                    (real + real_back, imag - imag_back, imag + imag_back, real_back - real)
                )
            even_re, odd_im, even_im, odd_re = (
                jnp.concatenate(p, axis=0).astype(BF) for p in zip(*pieces)
            )
            at = k * 128 + pair * 16
            rows_ref[at : at + 16, :256] = even_re
            rows_ref[at : at + 16, 256:] = odd_im
            rows_ref[at + 64 : at + 80, :256] = even_im
            rows_ref[at + 64 : at + 80, 256:] = odd_re


def response_kernel(place_ref, *refs):
    first_waves, second_waves = refs[:4], refs[4:8]
    before_ref, w_ref, sum_ref, first_ref, second_ref = refs[8:]
    step = pl.program_id(0)
    mirrored = jnp.where(step % 8 == 0, 0.0, 1.0)
    before = dot(second_ref[...], before_ref[0])
    build_rows(first_ref, first_waves, mirrored)
    total = jnp.where(step == 0, 0.0, sum_ref[...] + before)
    total = total + dot(first_ref[...], w_ref[0])
    build_rows(second_ref, second_waves, None)
    sum_ref[...] = total


def response(place, home, away, screened):
    def block(which, second, back):
        def index(step, place_ref):
            z = jnp.minimum(2 * step + second, HALF - 1)
            z = (NZ - z) & (NZ - 1) if back else z
            x = ((place_ref[0] >> 3) - (z >> 3)) & 3
            y = ((place_ref[0] >> 1) - (z >> 1)) & 3
            x, y = (x, y) if which == 0 else (y, x)
            return ((y * 4 + x) * 2 + ((place_ref[0] ^ z) & 1), 0, 0, 0)

        return pl.BlockSpec((1, 8, 16, 256), index)

    blocks = [block(w, s, b) for s in range(2) for b in (False, True) for w in range(2)]
    return pl.pallas_call(
        response_kernel,
        grid_spec=pltpu.PrefetchScalarGridSpec(
            num_scalar_prefetch=1,
            grid=(HALF // 2 + 1,),
            in_specs=blocks
            + [
                pl.BlockSpec((1, 512, 256), lambda i, p: (jnp.maximum(2 * i - 1, 0), 0, 0)),
                pl.BlockSpec((1, 512, 256), lambda i, p: (2 * i, 0, 0)),
            ],
            out_specs=pl.BlockSpec((1024, 256), lambda i, p: (0, 0)),
            scratch_shapes=[pltpu.VMEM((1024, 512), BF), pltpu.VMEM((1024, 512), BF)],
        ),
        out_shape=jax.ShapeDtypeStruct((1024, 256), F32),
        compiler_params=pltpu.CompilerParams(vmem_limit_bytes=20 * MIB),
        cost_estimate=pl.CostEstimate(
            flops=16 * 1024 * 512 * 256 * HALF, bytes_accessed=9 * MIB, transcendentals=0
        ),
        name="valence_response",
    )(place.reshape(1), *([home, away] * 4), screened, screened)


def spectrum_kernel(cos_ref, sin_ref, x_ref, out_ref):
    first = lax.broadcasted_iota(jnp.int32, (1, 128), 1) < 64
    table = halves(jnp.concatenate([cos_ref[...], sin_ref[...]], axis=1))
    for pair in range(4):
        straight, crossed = [], []
        for k in (2 * pair, 2 * pair + 1):
            x = x_ref[:, k * 128 : (k + 1) * 128]
            other = pltpu.roll(x, 64, 1)
            straight.append(x)
            crossed.append(jnp.where(first, other, -other))
        both = [jnp.concatenate(part, axis=1) for part in (straight, crossed)]
        cond = dot_halves(table, halves(jnp.concatenate(both, axis=0)))
        cond = (cond * NORM).astype(BF).astype(F32).T
        out_ref[pair * 256 : (pair + 1) * 256] = cond.astype(BF)


def cond_spectrum(cosine, sine, columns):
    return pl.pallas_call(
        spectrum_kernel,
        out_shape=jax.ShapeDtypeStruct((1024, 256), BF),
        in_specs=[pl.BlockSpec(memory_space=pltpu.VMEM)] * 3,
        out_specs=pl.BlockSpec(memory_space=pltpu.VMEM),
        compiler_params=pltpu.CompilerParams(vmem_limit_bytes=16 * MIB),
        cost_estimate=pl.CostEstimate(
            flops=24 * 256 * 256 * 1024, bytes_accessed=2 * MIB, transcendentals=0
        ),
        name="cond_spectrum",
    )(cosine, sine, columns)


def block_kernel(cond_ref, r_ref, out_ref):
    first = lax.broadcasted_iota(jnp.int32, (1, 128), 1) < 64
    for k in range(8):
        cond = cond_ref[k * 128 : (k + 1) * 128]
        rows = r_ref[k * 128 : (k + 1) * 128] * NORM
        top = rows.astype(BF)
        rest = (rows - top.astype(F32)).astype(BF)
        prod = dot(cond, top, ((1,), (1,))) + dot(cond, rest, ((1,), (1,)))
        swapped = pltpu.roll(prod[64:], 64, 1)
        both = prod[:64] + jnp.where(first, swapped, -swapped)
        even, odd = both[:32], both[32:]
        out_ref[:, 2 * k, :] = jnp.where(first, even, pltpu.roll(odd, 64, 1))
        out_ref[:, 2 * k + 1, :] = jnp.where(first, pltpu.roll(even, 64, 1), odd)


def kernel_blocks(cond, rows):
    return pl.pallas_call(
        block_kernel,
        out_shape=jax.ShapeDtypeStruct((32, 16, 128), F32),
        in_specs=[pl.BlockSpec(memory_space=pltpu.VMEM)] * 2,
        out_specs=pl.BlockSpec(memory_space=pltpu.VMEM),
        compiler_params=pltpu.CompilerParams(vmem_limit_bytes=16 * MIB),
        cost_estimate=pl.CostEstimate(
            flops=4 * 128 * 256 * 1024, bytes_accessed=2 * MIB, transcendentals=0
        ),
        name="kernel_blocks",
    )(cond, rows)


def line_tables(gmap, place):
    level = lax.dynamic_slice_in_dim(gmap, place * 256, 256) & (NZ - 1)
    column = jnp.arange(256, dtype=jnp.int32)
    angle = (level[:, None] * (column // 8)[None, :]) % NZ
    same = (column // NZ)[:, None] == (column % 8)[None, :]
    angle = angle.astype(F32) * (2.0 * math.pi / NZ)
    return jnp.where(same, jnp.cos(angle), 0.0), jnp.where(same, jnp.sin(angle), 0.0)


def lay_out_kernel(full_ref, rows_ref, mirror_ref):
    low = lax.broadcasted_iota(jnp.int32, (1, 128), 1) < 64
    for m in range(4):
        for n in range(4):
            for c in (2 * n, 2 * n + 1):
                piece = full_ref[m * 4 + n, 0, (c & 1) * 16 : (c & 1) * 16 + 16].astype(F32)
                at = (c * 4 + m) * 128
                rows_ref[:, :, at : at + 128] = piece.reshape(8, 2, 128)
            even = full_ref[m * 4 + n, 1, :16].astype(F32)
            odd = full_ref[m * 4 + n, 1, 16:].astype(F32)
            first = jnp.where(low, even, pltpu.roll(odd, 64, 1))
            second = jnp.where(low, pltpu.roll(even, 64, 1), odd)
            at = (2 * m * 4 + n) * 128
            mirror_ref[:, :, at : at + 128] = first.reshape(8, 2, 128)
            mirror_ref[:, :, at + 512 : at + 640] = second.reshape(8, 2, 128)


def lay_out(full):
    shape = jax.ShapeDtypeStruct((8, 2, 4096), F32)
    return pl.pallas_call(
        lay_out_kernel,
        in_specs=[pl.BlockSpec(memory_space=pltpu.VMEM)],
        out_specs=[pl.BlockSpec(memory_space=pltpu.VMEM)] * 2,
        out_shape=[shape, shape],
        compiler_params=pltpu.CompilerParams(vmem_limit_bytes=16 * MIB),
        name="lay_out",
    )(full)


def on_device(wavefunctions, partner, gmap, screened):
    ka_place = lax.axis_index(KA)
    place = lax.axis_index(GA)
    owned = ka_place * 8 + jnp.arange(8, dtype=jnp.int32)

    waves = wavefunctions.reshape(8, 2, 2, 8, 256).transpose(0, 2, 1, 3, 4).reshape(8, 32, 256)
    near = spread(waves, "zl").reshape(32, 32, 256)

    index = jnp.arange(PLANE, dtype=jnp.int32)
    negative = (NX - index // NY) % NX * NY + (NY - index % NY) % NY
    negative = jnp.where(place > NZ // 2, negative, index)
    flip = (index[:, None] == negative[None, :]).astype(BF)
    far = turned(near, "co", 1)

    vals, away_cond = choose(partner, near, far, flip)
    planes = cond_planes(waves[:, 16:], away_cond)
    vals = spread(vals, "zh")
    home, away = spread(vals[:, 0], "x"), spread(vals[:, 1], "y")
    home, away, planes, screened = lax.optimization_barrier((home, away, planes, screened))
    homes = [home] + [turned(home, "y", d) for d in range(1, 4)]
    aways = [away] + [turned(away, "x", d) for d in range(1, 3)]
    wide, end = screened_transform(screened, gmap)
    away, planes, end = lax.optimization_barrier((away, planes, end))
    aways.append(turned(away, "x", 3))
    columns = lax.all_to_all(planes, GA, split_axis=0, concat_axis=0, tiled=True)
    home = jnp.stack(homes).reshape(32, 8, 16, 256)
    away = jnp.stack(aways).reshape(32, 8, 16, 256)
    rows = response(place, home, away, wide)
    cond = cond_spectrum(*line_tables(gmap, place), columns)
    blocks = kernel_blocks(cond, rows)

    parts = lax.all_to_all(blocks, ("x", "y"), split_axis=0, concat_axis=0, tiled=True)
    mine = jnp.sum(parts.reshape(16, 2, 16, 128), axis=0)
    everyone = copies_to_all(mine, ("zl", "co", "zh")).reshape(8, 2, 2, 16, 128)
    everyone = everyone[:, 0] + everyone[:, 1]
    mine = lax.dynamic_index_in_dim(everyone, ka_place, keepdims=False)
    everyone = everyone.reshape(8, 2, 8, 256).transpose(0, 2, 1, 3).reshape(64, 512)
    select = (partner[None, :] == owned[:, None]).astype(F32)
    mirror = jnp.dot(select, everyone, precision=EXACT)
    mirror = mirror.reshape(8, 2, 2, 128).transpose(1, 0, 2, 3).reshape(32, 128)
    lane = jnp.arange(128, dtype=jnp.int32)
    moved = lane // 64 * 64 + lane % 8 * 8 + lane // 8 % 8
    turn = (lane[:, None] == moved[None, :]).astype(F32)
    sign = jnp.where(jnp.arange(32) % 2 == 0, 1.0, -1.0).astype(F32)
    mirror = jnp.dot(mirror, turn, precision=EXACT) * sign[:, None]
    both = jnp.stack([mine.reshape(32, 128), mirror]).astype(BF)
    full = copies_to_all(both, ("x", "y"))
    return lay_out(full)


def solution(mesh):
    fine = Mesh(mesh.devices.reshape(SIZES), AXES)
    in_specs = (P(KA, None, None, GA, None), P(), P(), P(GA, None))
    out_specs = (P(KA, None, None), P(KA, None, None))
    return jax.shard_map(
        on_device, mesh=fine, in_specs=in_specs, out_specs=out_specs, check_vma=False
    )
```

```python
import functools
import math

import jax
import jax.numpy as jnp
import numpy as np
from jax import lax
from jax.experimental import pallas as pl
from jax.experimental.pallas import tpu as pltpu
from jax.sharding import Mesh
from jax.sharding import PartitionSpec as P

NX = 16
NY = 16
NZ = 32
NG = 8192
PLANE = NX * NY
HALF = NZ // 2 + 1
LINE_BLOCKS = 8
LINE_STEPS = 32 // LINE_BLOCKS
LINE_ROWS = 48
NORM = 1.0 / math.sqrt(NG)
EXACT = lax.Precision.HIGHEST
BF = jnp.bfloat16
F32 = jnp.float32
MIB = 1 << 20

AXES = ("zl", "co", "x", "y", "zh")
SIZES = (4, 2, 4, 4, 2)
SIZE = dict(zip(AXES, SIZES))
KA = ("zl", "co")
GA = ("x", "y", "zh")


def split_table(table):
    high = table.astype(np.float32).astype(BF)
    low = (table - high.astype(np.float64)).astype(np.float32).astype(BF)
    return high, low


def plane_angles():
    index = np.arange(PLANE)
    x, y = index // NY, index % NY
    turns = (np.outer(x, x) % NX) / NX + (np.outer(y, y) % NY) / NY
    return 2.0 * np.pi * turns


def line_angles():
    index = np.arange(NZ)
    return 2.0 * np.pi * (np.outer(index, index) % NZ) / NZ


def turned(value, axis, step):
    size = SIZE[axis]
    return lax.ppermute(value, axis, [(i, (i + step) % size) for i in range(size)])


def spread(value, axis):
    return jnp.stack([value] + [turned(value, axis, d) for d in range(1, SIZE[axis])])


def copies_to_all(value, axes):
    count = math.prod(SIZE[axis] for axis in axes)
    copies = jnp.broadcast_to(value[None], (count,) + value.shape)
    return lax.all_to_all(copies, axes, split_axis=0, concat_axis=0, tiled=True)


def dot(a, b, contract=((1,), (0,)), precision=None):
    return lax.dot_general(
        a, b, (contract, ((), ())), precision=precision, preferred_element_type=F32
    )


def screened_kernel(gmap_ref, line_ref, high_ref, low_ref, w_ref, out_ref, end_ref, lines_ref):
    step = pl.program_id(0)
    end_ref[...] = jnp.zeros_like(end_ref)

    @pl.when(step < LINE_STEPS)
    def _():
        rows = 2 * HALF
        keep = lax.broadcasted_iota(jnp.int32, (1, 8, 256), 1) == (
            lax.broadcasted_iota(jnp.int32, (1, 8, 256), 2) >> 5
        )
        for b in range(LINE_BLOCKS):
            level = gmap_ref[b] & (NZ - 1)
            hot = (lax.broadcasted_iota(jnp.int32, (NZ, 256), 0) == level).astype(F32).astype(BF)
            picked = dot(line_ref[...], hot)
            tables = []
            for at in (0, LINE_ROWS):
                wide = jnp.broadcast_to(picked[at : at + rows][:, None, :], (rows, 8, 256))
                tables.append(jnp.where(keep, wide, 0.0).reshape(rows * 8, 256).astype(BF))
            block = w_ref[:, b * 256 : (b + 1) * 256]
            both = dot(jnp.concatenate(tables, axis=0), block, ((1,), (1,)))
            total = both[: rows * 8] + both[rows * 8 :]
            at = pl.multiple_of((step * LINE_BLOCKS + b) * 8, 8)
            lines_ref[:, pl.ds(at, 8), :] = total.reshape(rows, 8, 256)

    @pl.when(step >= LINE_STEPS)
    def _():
        z = step - LINE_STEPS
        real, imag = lines_ref[z], lines_ref[HALF + z]
        for odd in range(2):
            if odd:
                both = [real[:128] - real[128:], imag[:128] - imag[128:]]
            else:
                both = [real[:128] + real[128:], imag[:128] + imag[128:]]
            both = jnp.concatenate(both, axis=0)
            top = both.astype(BF)
            rest = (both - top.astype(F32)).astype(BF)
            high, low = high_ref[odd], low_ref[odd]
            prod = (dot(high, top) + (dot(high, rest) + dot(low, top))).astype(BF)
            for half in range(8):
                at = (2 * half + odd) * NY
                out_ref[0, at : at + NY] = prod[half * NY : (half + 1) * NY]
                out_ref[0, 256 + at : 256 + at + NY] = prod[128 + half * NY : 144 + half * NY]


def screened_transform(screened, gmap):
    angles = line_angles()[:HALF]
    table = np.concatenate([np.cos(angles), -np.sin(angles)], axis=0)
    padding = np.zeros((LINE_ROWS - 2 * HALF, NZ), BF)
    line = np.concatenate([x for part in split_table(table) for x in (part, padding)], axis=0)
    angles = plane_angles().reshape(NX, NY, PLANE)[:, :, :128]
    tables = []
    for odd in range(2):
        part = angles[odd::2].reshape(128, 128)
        cosine, sine = np.cos(part), np.sin(part)
        tables.append(np.block([[cosine, sine], [sine, -cosine]]))
    high, low = split_table(np.stack(tables))
    n = LINE_BLOCKS
    last = LINE_STEPS - 1
    return pl.pallas_call(
        screened_kernel,
        grid=(LINE_STEPS + HALF,),
        in_specs=[
            pl.BlockSpec((n, 1, 256), lambda i: (jnp.minimum(i, last), 0, 0)),
            pl.BlockSpec((2 * LINE_ROWS, NZ), lambda i: (0, 0)),
            pl.BlockSpec((2, 256, 256), lambda i: (0, 0, 0)),
            pl.BlockSpec((2, 256, 256), lambda i: (0, 0, 0)),
            pl.BlockSpec((256, n * 256), lambda i: (0, jnp.minimum(i, last))),
        ],
        out_specs=[
            pl.BlockSpec((1, 512, 256), lambda i: (jnp.maximum(i - LINE_STEPS, 0), 0, 0)),
            pl.BlockSpec((8, 128), lambda i: (0, 0)),
        ],
        out_shape=[
            jax.ShapeDtypeStruct((HALF, 512, 256), BF),
            jax.ShapeDtypeStruct((8, 128), F32),
        ],
        scratch_shapes=[pltpu.VMEM((2 * HALF, PLANE, 256), F32)],
        compiler_params=pltpu.CompilerParams(vmem_limit_bytes=40 * MIB),
        cost_estimate=pl.CostEstimate(
            flops=48 * 256 * 256 * 256 * HALF, bytes_accessed=9 * MIB, transcendentals=0
        ),
        name="screened_transform",
    )(gmap.reshape(32, 1, 256), jnp.asarray(line), jnp.asarray(high), jnp.asarray(low), screened)


def halves(value):
    high = value.astype(BF)
    return high, (value - high.astype(F32)).astype(BF)


def dot_halves(a, b, contract=((1,), (0,))):
    return dot(a[0], b[0], contract) + (dot(a[0], b[1], contract) + dot(a[1], b[0], contract))


def choose_kernel(partner_ref, place_ref, flip_ref, near_ref, far_ref, val_ref, cond_ref):
    level, core = place_ref[0], place_ref[1]
    for m in range(8):
        val_ref[0, m] = dot(near_ref[m, :16], flip_ref[...]).astype(BF)
        wanted = partner_ref[(level * 2 + core) * 8 + m]
        back = (level - wanted // 16) & 3
        at = back * 8 + (wanted & 7)
        near = (wanted // 8) % 2 == core

        def take(ref, m=m, at=at):
            row = ref[at]
            val_ref[1, m] = dot(row[:16], flip_ref[...]).astype(BF)
            cond_ref[m] = row[16:]

        pl.when(near)(functools.partial(take, near_ref))
        pl.when(jnp.logical_not(near))(functools.partial(take, far_ref))


def choose(partner, near, far, flip):
    shape = jax.ShapeDtypeStruct((8, 16, 256), BF)
    place = jnp.stack([lax.axis_index("zl"), lax.axis_index("co")]).astype(jnp.int32)
    return pl.pallas_call(
        choose_kernel,
        in_specs=[pl.BlockSpec(memory_space=pltpu.SMEM)] * 2
        + [pl.BlockSpec(memory_space=pltpu.VMEM)] * 3,
        out_specs=[pl.BlockSpec(memory_space=pltpu.VMEM)] * 2,
        out_shape=[jax.ShapeDtypeStruct((2, 8, 16, 256), BF), shape],
        compiler_params=pltpu.CompilerParams(vmem_limit_bytes=16 * MIB),
        name="partner_choice",
    )(partner, place, flip, near, far)


def cond_kernel(high_ref, low_ref, home_ref, away_ref, x_ref, rows_ref):
    for k in range(8):
        home, away = home_ref[k].astype(F32), away_ref[k].astype(F32)
        hr, hi = home[:8], home[8:]
        for place, band in enumerate((0, 2, 4, 6, 1, 3, 5, 7)):
            ar, ai = away[band : band + 1], away[8 + band : 9 + band]
            real = hr * ar + hi * ai
            imag = hr * ai - hi * ar
            at = k * 128 + place * 8
            rows_ref[at : at + 8, :256] = real
            rows_ref[at : at + 8, 256:] = imag
            rows_ref[at + 64 : at + 72, :256] = imag
            rows_ref[at + 64 : at + 72, 256:] = -real
    table = high_ref[...], low_ref[...]
    for k in range(4):
        rows = halves(rows_ref[k * 256 : (k + 1) * 256])
        x_ref[:, k * 256 : (k + 1) * 256] = dot_halves(table, rows, ((1,), (1,)))


def cond_planes(home, away):
    angles = plane_angles()
    high, low = split_table(np.concatenate([np.cos(angles), np.sin(angles)], axis=1))
    return pl.pallas_call(
        cond_kernel,
        out_shape=jax.ShapeDtypeStruct((256, 1024), F32),
        in_specs=[pl.BlockSpec(memory_space=pltpu.VMEM)] * 4,
        out_specs=pl.BlockSpec(memory_space=pltpu.VMEM),
        scratch_shapes=[pltpu.VMEM((1024, 512), F32)],
        compiler_params=pltpu.CompilerParams(vmem_limit_bytes=24 * MIB),
        cost_estimate=pl.CostEstimate(
            flops=12 * 256 * 512 * 1024, bytes_accessed=2 * MIB, transcendentals=0
        ),
        name="cond_planes",
    )(jnp.asarray(high), jnp.asarray(low), home, away)


def build_rows(rows_ref, waves, mirrored):
    home_ref, away_ref, home_back_ref, away_back_ref = waves

    def density(home, away, v):
        hr, hi = home[v : v + 1], home[8 + v : 9 + v]
        ar, ai = away[:8], away[8:]
        return hr * ar + hi * ai, hr * ai - hi * ar

    for k in range(8):
        home, away = home_ref[0, k].astype(F32), away_ref[0, k].astype(F32)
        home_back, away_back = home_back_ref[0, k].astype(F32), away_back_ref[0, k].astype(F32)
        if mirrored is not None:
            home_back = home_back * mirrored
        for pair in range(4):
            pieces = []
            for v in (2 * pair, 2 * pair + 1):
                real, imag = density(home, away, v)
                real_back, imag_back = density(home_back, away_back, v)
                pieces.append(
                    (real + real_back, imag - imag_back, imag + imag_back, real_back - real)
                )
            even_re, odd_im, even_im, odd_re = (
                jnp.concatenate(p, axis=0).astype(BF) for p in zip(*pieces)
            )
            at = k * 128 + pair * 16
            rows_ref[at : at + 16, :256] = even_re
            rows_ref[at : at + 16, 256:] = odd_im
            rows_ref[at + 64 : at + 80, :256] = even_im
            rows_ref[at + 64 : at + 80, 256:] = odd_re


def response_kernel(place_ref, *refs):
    first_waves, second_waves = refs[:4], refs[4:8]
    before_ref, w_ref, sum_ref, first_ref, second_ref = refs[8:]
    step = pl.program_id(0)
    mirrored = jnp.where(step % 8 == 0, 0.0, 1.0)
    before = dot(second_ref[...], before_ref[0])
    build_rows(first_ref, first_waves, mirrored)
    total = jnp.where(step == 0, 0.0, sum_ref[...] + before)
    total = total + dot(first_ref[...], w_ref[0])
    build_rows(second_ref, second_waves, None)
    sum_ref[...] = total


def response(place, home, away, screened):
    def block(which, second, back):
        def index(step, place_ref):
            z = jnp.minimum(2 * step + second, HALF - 1)
            z = (NZ - z) & (NZ - 1) if back else z
            x = ((place_ref[0] >> 3) - (z >> 3)) & 3
            y = ((place_ref[0] >> 1) - (z >> 1)) & 3
            x, y = (x, y) if which == 0 else (y, x)
            return ((y * 4 + x) * 2 + ((place_ref[0] ^ z) & 1), 0, 0, 0)

        return pl.BlockSpec((1, 8, 16, 256), index)

    blocks = [block(w, s, b) for s in range(2) for b in (False, True) for w in range(2)]
    return pl.pallas_call(
        response_kernel,
        grid_spec=pltpu.PrefetchScalarGridSpec(
            num_scalar_prefetch=1,
            grid=(HALF // 2 + 1,),
            in_specs=blocks
            + [
                pl.BlockSpec((1, 512, 256), lambda i, p: (jnp.maximum(2 * i - 1, 0), 0, 0)),
                pl.BlockSpec((1, 512, 256), lambda i, p: (2 * i, 0, 0)),
            ],
            out_specs=pl.BlockSpec((1024, 256), lambda i, p: (0, 0)),
            scratch_shapes=[pltpu.VMEM((1024, 512), BF), pltpu.VMEM((1024, 512), BF)],
        ),
        out_shape=jax.ShapeDtypeStruct((1024, 256), F32),
        compiler_params=pltpu.CompilerParams(vmem_limit_bytes=20 * MIB),
        cost_estimate=pl.CostEstimate(
            flops=16 * 1024 * 512 * 256 * HALF, bytes_accessed=9 * MIB, transcendentals=0
        ),
        name="valence_response",
    )(place.reshape(1), *([home, away] * 4), screened, screened)


def spectrum_kernel(cos_ref, sin_ref, x_ref, out_ref):
    first = lax.broadcasted_iota(jnp.int32, (1, 128), 1) < 64
    table = halves(jnp.concatenate([cos_ref[...], sin_ref[...]], axis=1))
    for pair in range(4):
        straight, crossed = [], []
        for k in (2 * pair, 2 * pair + 1):
            x = x_ref[:, k * 128 : (k + 1) * 128]
            other = pltpu.roll(x, 64, 1)
            straight.append(x)
            crossed.append(jnp.where(first, other, -other))
        both = [jnp.concatenate(part, axis=1) for part in (straight, crossed)]
        cond = dot_halves(table, halves(jnp.concatenate(both, axis=0)))
        cond = (cond * NORM).astype(BF).astype(F32).T
        out_ref[pair * 256 : (pair + 1) * 256] = cond.astype(BF)


def cond_spectrum(cosine, sine, columns):
    return pl.pallas_call(
        spectrum_kernel,
        out_shape=jax.ShapeDtypeStruct((1024, 256), BF),
        in_specs=[pl.BlockSpec(memory_space=pltpu.VMEM)] * 3,
        out_specs=pl.BlockSpec(memory_space=pltpu.VMEM),
        compiler_params=pltpu.CompilerParams(vmem_limit_bytes=16 * MIB),
        cost_estimate=pl.CostEstimate(
            flops=24 * 256 * 256 * 1024, bytes_accessed=2 * MIB, transcendentals=0
        ),
        name="cond_spectrum",
    )(cosine, sine, columns)


def block_kernel(cond_ref, r_ref, out_ref):
    first = lax.broadcasted_iota(jnp.int32, (1, 128), 1) < 64
    for k in range(8):
        cond = cond_ref[k * 128 : (k + 1) * 128]
        rows = r_ref[k * 128 : (k + 1) * 128] * NORM
        top = rows.astype(BF)
        rest = (rows - top.astype(F32)).astype(BF)
        prod = dot(cond, top, ((1,), (1,))) + dot(cond, rest, ((1,), (1,)))
        swapped = pltpu.roll(prod[64:], 64, 1)
        both = prod[:64] + jnp.where(first, swapped, -swapped)
        even, odd = both[:32], both[32:]
        out_ref[:, 2 * k, :] = jnp.where(first, even, pltpu.roll(odd, 64, 1))
        out_ref[:, 2 * k + 1, :] = jnp.where(first, pltpu.roll(even, 64, 1), odd)


def kernel_blocks(cond, rows):
    return pl.pallas_call(
        block_kernel,
        out_shape=jax.ShapeDtypeStruct((32, 16, 128), F32),
        in_specs=[pl.BlockSpec(memory_space=pltpu.VMEM)] * 2,
        out_specs=pl.BlockSpec(memory_space=pltpu.VMEM),
        compiler_params=pltpu.CompilerParams(vmem_limit_bytes=16 * MIB),
        cost_estimate=pl.CostEstimate(
            flops=4 * 128 * 256 * 1024, bytes_accessed=2 * MIB, transcendentals=0
        ),
        name="kernel_blocks",
    )(cond, rows)


def line_tables(gmap, place):
    level = lax.dynamic_slice_in_dim(gmap, place * 256, 256) & (NZ - 1)
    column = jnp.arange(256, dtype=jnp.int32)
    angle = (level[:, None] * (column // 8)[None, :]) % NZ
    same = (column // NZ)[:, None] == (column % 8)[None, :]
    angle = angle.astype(F32) * (2.0 * math.pi / NZ)
    return jnp.where(same, jnp.cos(angle), 0.0), jnp.where(same, jnp.sin(angle), 0.0)


def lay_out_kernel(full_ref, rows_ref, mirror_ref):
    low = lax.broadcasted_iota(jnp.int32, (1, 128), 1) < 64
    for m in range(4):
        for n in range(4):
            for c in (2 * n, 2 * n + 1):
                piece = full_ref[m * 4 + n, 0, (c & 1) * 16 : (c & 1) * 16 + 16].astype(F32)
                at = (c * 4 + m) * 128
                rows_ref[:, :, at : at + 128] = piece.reshape(8, 2, 128)
            even = full_ref[m * 4 + n, 1, :16].astype(F32)
            odd = full_ref[m * 4 + n, 1, 16:].astype(F32)
            first = jnp.where(low, even, pltpu.roll(odd, 64, 1))
            second = jnp.where(low, pltpu.roll(even, 64, 1), odd)
            at = (2 * m * 4 + n) * 128
            mirror_ref[:, :, at : at + 128] = first.reshape(8, 2, 128)
            mirror_ref[:, :, at + 512 : at + 640] = second.reshape(8, 2, 128)


def lay_out(full):
    shape = jax.ShapeDtypeStruct((8, 2, 4096), F32)
    return pl.pallas_call(
        lay_out_kernel,
        in_specs=[pl.BlockSpec(memory_space=pltpu.VMEM)],
        out_specs=[pl.BlockSpec(memory_space=pltpu.VMEM)] * 2,
        out_shape=[shape, shape],
        compiler_params=pltpu.CompilerParams(vmem_limit_bytes=16 * MIB),
        name="lay_out",
    )(full)


def on_device(wavefunctions, partner, gmap, screened):
    ka_place = lax.axis_index(KA)
    place = lax.axis_index(GA)
    owned = ka_place * 8 + jnp.arange(8, dtype=jnp.int32)

    waves = wavefunctions.reshape(8, 2, 2, 8, 256).transpose(0, 2, 1, 3, 4).reshape(8, 32, 256)
    near = spread(waves, "zl").reshape(32, 32, 256)

    index = jnp.arange(PLANE, dtype=jnp.int32)
    negative = (NX - index // NY) % NX * NY + (NY - index % NY) % NY
    negative = jnp.where(place > NZ // 2, negative, index)
    flip = (index[:, None] == negative[None, :]).astype(BF)
    far = turned(near, "co", 1)

    vals, away_cond = choose(partner, near, far, flip)
    planes = cond_planes(waves[:, 16:], away_cond)
    vals = spread(vals, "zh")
    home, away = spread(vals[:, 0], "x"), spread(vals[:, 1], "y")
    home, away, planes, screened = lax.optimization_barrier((home, away, planes, screened))
    homes = [home] + [turned(home, "y", d) for d in range(1, 4)]
    aways = [away] + [turned(away, "x", d) for d in range(1, 3)]
    wide, end = screened_transform(screened, gmap)
    away, planes, end = lax.optimization_barrier((away, planes, end))
    aways.append(turned(away, "x", 3))
    columns = lax.all_to_all(planes, GA, split_axis=0, concat_axis=0, tiled=True)
    home = jnp.stack(homes).reshape(32, 8, 16, 256)
    away = jnp.stack(aways).reshape(32, 8, 16, 256)
    rows = response(place, home, away, wide)
    cond = cond_spectrum(*line_tables(gmap, place), columns)
    blocks = kernel_blocks(cond, rows)

    parts = lax.all_to_all(blocks, ("x", "y"), split_axis=0, concat_axis=0, tiled=True)
    mine = jnp.sum(parts.reshape(16, 2, 16, 128), axis=0)
    mine = mine + turned(mine, "zh", 1)
    close = spread(mine, "zl")
    everyone = jnp.stack([close, turned(close, "co", 1)]).reshape(2, 4, 2, 8, 256)
    everyone = everyone.transpose(0, 1, 3, 2, 4).reshape(64, 512)
    slot = jnp.arange(64, dtype=jnp.int32)
    level = (lax.axis_index("zl") - slot // 8) & 3
    core = (lax.axis_index("co") + slot // 32) & 1
    holds = (level * 2 + core) * 8 + slot % 8
    number = jnp.arange(64, dtype=jnp.int32)
    source = jnp.sum(jnp.where(partner[None, :] == owned[:, None], number[None, :], 0), axis=1)
    select = (source[:, None] == holds[None, :]).astype(F32)
    mirror = jnp.dot(select, everyone, precision=EXACT)
    mirror = mirror.reshape(8, 2, 2, 128).transpose(1, 0, 2, 3).reshape(32, 128)
    lane = jnp.arange(128, dtype=jnp.int32)
    moved = lane // 64 * 64 + lane % 8 * 8 + lane // 8 % 8
    turn = (lane[:, None] == moved[None, :]).astype(F32)
    sign = jnp.where(jnp.arange(32) % 2 == 0, 1.0, -1.0).astype(F32)
    mirror = jnp.dot(mirror, turn, precision=EXACT) * sign[:, None]
    both = jnp.stack([mine.reshape(32, 128), mirror]).astype(BF)
    full = copies_to_all(both, ("x", "y"))
    return lay_out(full)


def solution(mesh):
    fine = Mesh(mesh.devices.reshape(SIZES), AXES)
    in_specs = (P(KA, None, None, GA, None), P(), P(), P(GA, None))
    out_specs = (P(KA, None, None), P(KA, None, None))
    return jax.shard_map(
        on_device, mesh=fine, in_specs=in_specs, out_specs=out_specs, check_vma=False
    )
```

```python
import functools
import math

import jax
import jax.numpy as jnp
import numpy as np
from jax import lax
from jax.experimental import pallas as pl
from jax.experimental.pallas import tpu as pltpu
from jax.sharding import Mesh
from jax.sharding import PartitionSpec as P

NX = 16
NY = 16
NZ = 32
NG = 8192
PLANE = NX * NY
HALF = NZ // 2 + 1
LINE_BLOCKS = 8
LINE_STEPS = 32 // LINE_BLOCKS
LINE_ROWS = 48
NORM = 1.0 / math.sqrt(NG)
EXACT = lax.Precision.HIGHEST
BF = jnp.bfloat16
F32 = jnp.float32
MIB = 1 << 20

AXES = ("zl", "co", "x", "y", "zh")
SIZES = (4, 2, 4, 4, 2)
SIZE = dict(zip(AXES, SIZES))
KA = ("zl", "co")
GA = ("x", "y", "zh")


def split_table(table):
    high = table.astype(np.float32).astype(BF)
    low = (table - high.astype(np.float64)).astype(np.float32).astype(BF)
    return high, low


def plane_angles():
    index = np.arange(PLANE)
    x, y = index // NY, index % NY
    turns = (np.outer(x, x) % NX) / NX + (np.outer(y, y) % NY) / NY
    return 2.0 * np.pi * turns


def line_angles():
    index = np.arange(NZ)
    return 2.0 * np.pi * (np.outer(index, index) % NZ) / NZ


def turned(value, axis, step):
    size = SIZE[axis]
    return lax.ppermute(value, axis, [(i, (i + step) % size) for i in range(size)])


def spread(value, axis):
    return jnp.stack([value] + [turned(value, axis, d) for d in range(1, SIZE[axis])])


def copies_to_all(value, axes):
    count = math.prod(SIZE[axis] for axis in axes)
    copies = jnp.broadcast_to(value[None], (count,) + value.shape)
    return lax.all_to_all(copies, axes, split_axis=0, concat_axis=0, tiled=True)


def dot(a, b, contract=((1,), (0,)), precision=None):
    return lax.dot_general(
        a, b, (contract, ((), ())), precision=precision, preferred_element_type=F32
    )


def screened_kernel(gmap_ref, line_ref, high_ref, low_ref, w_ref, out_ref, end_ref, lines_ref):
    step = pl.program_id(0)
    end_ref[...] = jnp.zeros_like(end_ref)

    @pl.when(step < LINE_STEPS)
    def _():
        rows = 2 * HALF
        keep = lax.broadcasted_iota(jnp.int32, (1, 8, 256), 1) == (
            lax.broadcasted_iota(jnp.int32, (1, 8, 256), 2) >> 5
        )
        for b in range(LINE_BLOCKS):
            level = gmap_ref[b] & (NZ - 1)
            hot = (lax.broadcasted_iota(jnp.int32, (NZ, 256), 0) == level).astype(F32).astype(BF)
            picked = dot(line_ref[...], hot)
            tables = []
            for at in (0, LINE_ROWS):
                wide = jnp.broadcast_to(picked[at : at + rows][:, None, :], (rows, 8, 256))
                tables.append(jnp.where(keep, wide, 0.0).reshape(rows * 8, 256).astype(BF))
            block = w_ref[:, b * 256 : (b + 1) * 256]
            both = dot(jnp.concatenate(tables, axis=0), block, ((1,), (1,)))
            total = both[: rows * 8] + both[rows * 8 :]
            at = pl.multiple_of((step * LINE_BLOCKS + b) * 8, 8)
            lines_ref[:, pl.ds(at, 8), :] = total.reshape(rows, 8, 256)

    @pl.when(step >= LINE_STEPS)
    def _():
        z = step - LINE_STEPS
        real, imag = lines_ref[z], lines_ref[HALF + z]
        for odd in range(2):
            if odd:
                both = [real[:128] - real[128:], imag[:128] - imag[128:]]
            else:
                both = [real[:128] + real[128:], imag[:128] + imag[128:]]
            both = jnp.concatenate(both, axis=0)
            top = both.astype(BF)
            rest = (both - top.astype(F32)).astype(BF)
            high, low = high_ref[odd], low_ref[odd]
            prod = (dot(high, top) + (dot(high, rest) + dot(low, top))).astype(BF)
            for half in range(8):
                at = (2 * half + odd) * NY
                out_ref[0, at : at + NY] = prod[half * NY : (half + 1) * NY]
                out_ref[0, 256 + at : 256 + at + NY] = prod[128 + half * NY : 144 + half * NY]


def screened_transform(screened, gmap):
    angles = line_angles()[:HALF]
    table = np.concatenate([np.cos(angles), -np.sin(angles)], axis=0)
    padding = np.zeros((LINE_ROWS - 2 * HALF, NZ), BF)
    line = np.concatenate([x for part in split_table(table) for x in (part, padding)], axis=0)
    angles = plane_angles().reshape(NX, NY, PLANE)[:, :, :128]
    tables = []
    for odd in range(2):
        part = angles[odd::2].reshape(128, 128)
        cosine, sine = np.cos(part), np.sin(part)
        tables.append(np.block([[cosine, sine], [sine, -cosine]]))
    high, low = split_table(np.stack(tables))
    n = LINE_BLOCKS
    last = LINE_STEPS - 1
    return pl.pallas_call(
        screened_kernel,
        grid=(LINE_STEPS + HALF,),
        in_specs=[
            pl.BlockSpec((n, 1, 256), lambda i: (jnp.minimum(i, last), 0, 0)),
            pl.BlockSpec((2 * LINE_ROWS, NZ), lambda i: (0, 0)),
            pl.BlockSpec((2, 256, 256), lambda i: (0, 0, 0)),
            pl.BlockSpec((2, 256, 256), lambda i: (0, 0, 0)),
            pl.BlockSpec((256, n * 256), lambda i: (0, jnp.minimum(i, last))),
        ],
        out_specs=[
            pl.BlockSpec((1, 512, 256), lambda i: (jnp.maximum(i - LINE_STEPS, 0), 0, 0)),
            pl.BlockSpec((8, 128), lambda i: (0, 0)),
        ],
        out_shape=[
            jax.ShapeDtypeStruct((HALF, 512, 256), BF),
            jax.ShapeDtypeStruct((8, 128), F32),
        ],
        scratch_shapes=[pltpu.VMEM((2 * HALF, PLANE, 256), F32)],
        compiler_params=pltpu.CompilerParams(vmem_limit_bytes=40 * MIB),
        cost_estimate=pl.CostEstimate(
            flops=48 * 256 * 256 * 256 * HALF, bytes_accessed=9 * MIB, transcendentals=0
        ),
        name="screened_transform",
    )(gmap.reshape(32, 1, 256), jnp.asarray(line), jnp.asarray(high), jnp.asarray(low), screened)


def halves(value):
    high = value.astype(BF)
    return high, (value - high.astype(F32)).astype(BF)


def dot_halves(a, b, contract=((1,), (0,))):
    return dot(a[0], b[0], contract) + (dot(a[0], b[1], contract) + dot(a[1], b[0], contract))


def choose_kernel(partner_ref, place_ref, flip_ref, near_ref, far_ref, val_ref, cond_ref):
    level, core = place_ref[0], place_ref[1]
    for m in range(8):
        wanted = partner_ref[(level * 2 + core) * 8 + m]
        back = (level - wanted // 16) & 3
        at = back * 8 + (wanted & 7)
        near = (wanted // 8) % 2 == core

        def take(ref, m=m, at=at):
            row = ref[at]
            val_ref[1, m] = row[:16]
            cond_ref[m] = row[16:]

        pl.when(near)(functools.partial(take, near_ref))
        pl.when(jnp.logical_not(near))(functools.partial(take, far_ref))
    for part, rows in ((0, near_ref[:8, :16]), (1, val_ref[1])):
        turned_rows = dot(rows.reshape(128, 256), flip_ref[...]).astype(BF)
        val_ref[part] = turned_rows.reshape(8, 16, 256)


def choose(partner, near, far, flip):
    shape = jax.ShapeDtypeStruct((8, 16, 256), BF)
    place = jnp.stack([lax.axis_index("zl"), lax.axis_index("co")]).astype(jnp.int32)
    return pl.pallas_call(
        choose_kernel,
        in_specs=[pl.BlockSpec(memory_space=pltpu.SMEM)] * 2
        + [pl.BlockSpec(memory_space=pltpu.VMEM)] * 3,
        out_specs=[pl.BlockSpec(memory_space=pltpu.VMEM)] * 2,
        out_shape=[jax.ShapeDtypeStruct((2, 8, 16, 256), BF), shape],
        compiler_params=pltpu.CompilerParams(vmem_limit_bytes=16 * MIB),
        name="partner_choice",
    )(partner, place, flip, near, far)


def cond_kernel(high_ref, low_ref, home_ref, away_ref, x_ref, rows_ref):
    for k in range(8):
        home, away = home_ref[k].astype(F32), away_ref[k].astype(F32)
        hr, hi = home[:8], home[8:]
        for place, band in enumerate((0, 2, 4, 6, 1, 3, 5, 7)):
            ar, ai = away[band : band + 1], away[8 + band : 9 + band]
            real = hr * ar + hi * ai
            imag = hr * ai - hi * ar
            at = k * 128 + place * 8
            rows_ref[at : at + 8, :256] = real
            rows_ref[at : at + 8, 256:] = imag
            rows_ref[at + 64 : at + 72, :256] = imag
            rows_ref[at + 64 : at + 72, 256:] = -real
    table = high_ref[...], low_ref[...]
    for k in range(4):
        rows = halves(rows_ref[k * 256 : (k + 1) * 256])
        x_ref[:, k * 256 : (k + 1) * 256] = dot_halves(table, rows, ((1,), (1,)))


def cond_planes(home, away):
    angles = plane_angles()
    high, low = split_table(np.concatenate([np.cos(angles), np.sin(angles)], axis=1))
    return pl.pallas_call(
        cond_kernel,
        out_shape=jax.ShapeDtypeStruct((256, 1024), F32),
        in_specs=[pl.BlockSpec(memory_space=pltpu.VMEM)] * 4,
        out_specs=pl.BlockSpec(memory_space=pltpu.VMEM),
        scratch_shapes=[pltpu.VMEM((1024, 512), F32)],
        compiler_params=pltpu.CompilerParams(vmem_limit_bytes=24 * MIB),
        cost_estimate=pl.CostEstimate(
            flops=12 * 256 * 512 * 1024, bytes_accessed=2 * MIB, transcendentals=0
        ),
        name="cond_planes",
    )(jnp.asarray(high), jnp.asarray(low), home, away)


def build_rows(rows_ref, waves, mirrored):
    home_ref, away_ref, home_back_ref, away_back_ref = waves

    def density(home, away, v):
        hr, hi = home[v : v + 1], home[8 + v : 9 + v]
        ar, ai = away[:8], away[8:]
        return hr * ar + hi * ai, hr * ai - hi * ar

    for k in range(8):
        home, away = home_ref[0, k].astype(F32), away_ref[0, k].astype(F32)
        home_back, away_back = home_back_ref[0, k].astype(F32), away_back_ref[0, k].astype(F32)
        if mirrored is not None:
            home_back = home_back * mirrored
        for pair in range(4):
            pieces = []
            for v in (2 * pair, 2 * pair + 1):
                real, imag = density(home, away, v)
                real_back, imag_back = density(home_back, away_back, v)
                pieces.append(
                    (real + real_back, imag - imag_back, imag + imag_back, real_back - real)
                )
            even_re, odd_im, even_im, odd_re = (
                jnp.concatenate(p, axis=0).astype(BF) for p in zip(*pieces)
            )
            at = k * 128 + pair * 16
            rows_ref[at : at + 16, :256] = even_re
            rows_ref[at : at + 16, 256:] = odd_im
            rows_ref[at + 64 : at + 80, :256] = even_im
            rows_ref[at + 64 : at + 80, 256:] = odd_re


def response_kernel(place_ref, *refs):
    first_waves, second_waves = refs[:4], refs[4:8]
    before_ref, w_ref, sum_ref, first_ref, second_ref = refs[8:]
    step = pl.program_id(0)
    mirrored = jnp.where(step % 8 == 0, 0.0, 1.0)
    before = dot(second_ref[...], before_ref[0])
    build_rows(first_ref, first_waves, mirrored)
    total = jnp.where(step == 0, 0.0, sum_ref[...] + before)
    total = total + dot(first_ref[...], w_ref[0])
    build_rows(second_ref, second_waves, None)
    sum_ref[...] = total


def response(place, home, away, screened):
    def block(which, second, back):
        def index(step, place_ref):
            z = jnp.minimum(2 * step + second, HALF - 1)
            z = (NZ - z) & (NZ - 1) if back else z
            x = ((place_ref[0] >> 3) - (z >> 3)) & 3
            y = ((place_ref[0] >> 1) - (z >> 1)) & 3
            x, y = (x, y) if which == 0 else (y, x)
            return ((y * 4 + x) * 2 + ((place_ref[0] ^ z) & 1), 0, 0, 0)

        return pl.BlockSpec((1, 8, 16, 256), index)

    blocks = [block(w, s, b) for s in range(2) for b in (False, True) for w in range(2)]
    return pl.pallas_call(
        response_kernel,
        grid_spec=pltpu.PrefetchScalarGridSpec(
            num_scalar_prefetch=1,
            grid=(HALF // 2 + 1,),
            in_specs=blocks
            + [
                pl.BlockSpec((1, 512, 256), lambda i, p: (jnp.maximum(2 * i - 1, 0), 0, 0)),
                pl.BlockSpec((1, 512, 256), lambda i, p: (2 * i, 0, 0)),
            ],
            out_specs=pl.BlockSpec((1024, 256), lambda i, p: (0, 0)),
            scratch_shapes=[pltpu.VMEM((1024, 512), BF), pltpu.VMEM((1024, 512), BF)],
        ),
        out_shape=jax.ShapeDtypeStruct((1024, 256), F32),
        compiler_params=pltpu.CompilerParams(vmem_limit_bytes=20 * MIB),
        cost_estimate=pl.CostEstimate(
            flops=16 * 1024 * 512 * 256 * HALF, bytes_accessed=9 * MIB, transcendentals=0
        ),
        name="valence_response",
    )(place.reshape(1), *([home, away] * 4), screened, screened)


def spectrum_kernel(cos_ref, sin_ref, x_ref, out_ref):
    first = lax.broadcasted_iota(jnp.int32, (1, 128), 1) < 64
    table = halves(jnp.concatenate([cos_ref[...], sin_ref[...]], axis=1))
    for pair in range(4):
        straight, crossed = [], []
        for k in (2 * pair, 2 * pair + 1):
            x = x_ref[:, k * 128 : (k + 1) * 128]
            other = pltpu.roll(x, 64, 1)
            straight.append(x)
            crossed.append(jnp.where(first, other, -other))
        both = [jnp.concatenate(part, axis=1) for part in (straight, crossed)]
        cond = dot_halves(table, halves(jnp.concatenate(both, axis=0)))
        cond = (cond * NORM).astype(BF).astype(F32).T
        out_ref[pair * 256 : (pair + 1) * 256] = cond.astype(BF)


def cond_spectrum(cosine, sine, columns):
    return pl.pallas_call(
        spectrum_kernel,
        out_shape=jax.ShapeDtypeStruct((1024, 256), BF),
        in_specs=[pl.BlockSpec(memory_space=pltpu.VMEM)] * 3,
        out_specs=pl.BlockSpec(memory_space=pltpu.VMEM),
        compiler_params=pltpu.CompilerParams(vmem_limit_bytes=16 * MIB),
        cost_estimate=pl.CostEstimate(
            flops=24 * 256 * 256 * 1024, bytes_accessed=2 * MIB, transcendentals=0
        ),
        name="cond_spectrum",
    )(cosine, sine, columns)


def block_kernel(cond_ref, r_ref, out_ref):
    first = lax.broadcasted_iota(jnp.int32, (1, 128), 1) < 64
    for k in range(8):
        cond = cond_ref[k * 128 : (k + 1) * 128]
        rows = r_ref[k * 128 : (k + 1) * 128] * NORM
        top = rows.astype(BF)
        rest = (rows - top.astype(F32)).astype(BF)
        prod = dot(cond, top, ((1,), (1,))) + dot(cond, rest, ((1,), (1,)))
        swapped = pltpu.roll(prod[64:], 64, 1)
        both = prod[:64] + jnp.where(first, swapped, -swapped)
        even, odd = both[:32], both[32:]
        out_ref[:, 2 * k, :] = jnp.where(first, even, pltpu.roll(odd, 64, 1))
        out_ref[:, 2 * k + 1, :] = jnp.where(first, pltpu.roll(even, 64, 1), odd)


def kernel_blocks(cond, rows):
    return pl.pallas_call(
        block_kernel,
        out_shape=jax.ShapeDtypeStruct((32, 16, 128), F32),
        in_specs=[pl.BlockSpec(memory_space=pltpu.VMEM)] * 2,
        out_specs=pl.BlockSpec(memory_space=pltpu.VMEM),
        compiler_params=pltpu.CompilerParams(vmem_limit_bytes=16 * MIB),
        cost_estimate=pl.CostEstimate(
            flops=4 * 128 * 256 * 1024, bytes_accessed=2 * MIB, transcendentals=0
        ),
        name="kernel_blocks",
    )(cond, rows)


def line_tables(gmap, place):
    level = lax.dynamic_slice_in_dim(gmap, place * 256, 256) & (NZ - 1)
    column = jnp.arange(256, dtype=jnp.int32)
    angle = (level[:, None] * (column // 8)[None, :]) % NZ
    same = (column // NZ)[:, None] == (column % 8)[None, :]
    angle = angle.astype(F32) * (2.0 * math.pi / NZ)
    return jnp.where(same, jnp.cos(angle), 0.0), jnp.where(same, jnp.sin(angle), 0.0)


def lay_out_kernel(full_ref, rows_ref, mirror_ref):
    low = lax.broadcasted_iota(jnp.int32, (1, 128), 1) < 64
    for m in range(4):
        for n in range(4):
            for c in (2 * n, 2 * n + 1):
                piece = full_ref[m * 4 + n, 0, (c & 1) * 16 : (c & 1) * 16 + 16].astype(F32)
                at = (c * 4 + m) * 128
                rows_ref[:, :, at : at + 128] = piece.reshape(8, 2, 128)
            even = full_ref[m * 4 + n, 1, :16].astype(F32)
            odd = full_ref[m * 4 + n, 1, 16:].astype(F32)
            first = jnp.where(low, even, pltpu.roll(odd, 64, 1))
            second = jnp.where(low, pltpu.roll(even, 64, 1), odd)
            at = (2 * m * 4 + n) * 128
            mirror_ref[:, :, at : at + 128] = first.reshape(8, 2, 128)
            mirror_ref[:, :, at + 512 : at + 640] = second.reshape(8, 2, 128)


def lay_out(full):
    shape = jax.ShapeDtypeStruct((8, 2, 4096), F32)
    return pl.pallas_call(
        lay_out_kernel,
        in_specs=[pl.BlockSpec(memory_space=pltpu.VMEM)],
        out_specs=[pl.BlockSpec(memory_space=pltpu.VMEM)] * 2,
        out_shape=[shape, shape],
        compiler_params=pltpu.CompilerParams(vmem_limit_bytes=16 * MIB),
        name="lay_out",
    )(full)


def on_device(wavefunctions, partner, gmap, screened):
    ka_place = lax.axis_index(KA)
    place = lax.axis_index(GA)
    owned = ka_place * 8 + jnp.arange(8, dtype=jnp.int32)

    waves = wavefunctions.reshape(8, 2, 2, 8, 256).transpose(0, 2, 1, 3, 4).reshape(8, 32, 256)
    near = spread(waves, "zl").reshape(32, 32, 256)

    index = jnp.arange(PLANE, dtype=jnp.int32)
    negative = (NX - index // NY) % NX * NY + (NY - index % NY) % NY
    negative = jnp.where(place > NZ // 2, negative, index)
    flip = (index[:, None] == negative[None, :]).astype(BF)
    far = turned(near, "co", 1)

    vals, away_cond = choose(partner, near, far, flip)
    planes = cond_planes(waves[:, 16:], away_cond)
    vals = spread(vals, "zh")
    home, away = spread(vals[:, 0], "x"), spread(vals[:, 1], "y")
    home, away, planes, screened = lax.optimization_barrier((home, away, planes, screened))
    homes = [home] + [turned(home, "y", d) for d in range(1, 4)]
    aways = [away] + [turned(away, "x", d) for d in range(1, 3)]
    wide, end = screened_transform(screened, gmap)
    away, planes, end = lax.optimization_barrier((away, planes, end))
    aways.append(turned(away, "x", 3))
    columns = lax.all_to_all(planes, GA, split_axis=0, concat_axis=0, tiled=True)
    home = jnp.stack(homes).reshape(32, 8, 16, 256)
    away = jnp.stack(aways).reshape(32, 8, 16, 256)
    rows = response(place, home, away, wide)
    cond = cond_spectrum(*line_tables(gmap, place), columns)
    blocks = kernel_blocks(cond, rows)

    parts = lax.all_to_all(blocks, ("x", "y"), split_axis=0, concat_axis=0, tiled=True)
    mine = jnp.sum(parts.reshape(16, 2, 16, 128), axis=0)
    mine = mine + turned(mine, "zh", 1)
    close = spread(mine, "zl")
    everyone = jnp.stack([close, turned(close, "co", 1)]).reshape(2, 4, 2, 8, 256)
    everyone = everyone.transpose(0, 1, 3, 2, 4).reshape(64, 512)
    slot = jnp.arange(64, dtype=jnp.int32)
    level = (lax.axis_index("zl") - slot // 8) & 3
    core = (lax.axis_index("co") + slot // 32) & 1
    holds = (level * 2 + core) * 8 + slot % 8
    number = jnp.arange(64, dtype=jnp.int32)
    source = jnp.sum(jnp.where(partner[None, :] == owned[:, None], number[None, :], 0), axis=1)
    select = (source[:, None] == holds[None, :]).astype(F32)
    mirror = jnp.dot(select, everyone, precision=EXACT)
    mirror = mirror.reshape(8, 2, 2, 128).transpose(1, 0, 2, 3).reshape(32, 128)
    lane = jnp.arange(128, dtype=jnp.int32)
    moved = lane // 64 * 64 + lane % 8 * 8 + lane // 8 % 8
    turn = (lane[:, None] == moved[None, :]).astype(F32)
    sign = jnp.where(jnp.arange(32) % 2 == 0, 1.0, -1.0).astype(F32)
    mirror = jnp.dot(mirror, turn, precision=EXACT) * sign[:, None]
    both = jnp.stack([mine.reshape(32, 128), mirror]).astype(BF)
    full = copies_to_all(both, ("x", "y"))
    return lay_out(full)


def solution(mesh):
    fine = Mesh(mesh.devices.reshape(SIZES), AXES)
    in_specs = (P(KA, None, None, GA, None), P(), P(), P(GA, None))
    out_specs = (P(KA, None, None), P(KA, None, None))
    return jax.shard_map(
        on_device, mesh=fine, in_specs=in_specs, out_specs=out_specs, check_vma=False
    )
```

```python
import functools
import math

import jax
import jax.numpy as jnp
import numpy as np
from jax import lax
from jax.experimental import pallas as pl
from jax.experimental.pallas import tpu as pltpu
from jax.sharding import Mesh
from jax.sharding import PartitionSpec as P

NX = 16
NY = 16
NZ = 32
NG = 8192
PLANE = NX * NY
HALF = NZ // 2 + 1
LINE_BLOCKS = 8
LINE_STEPS = 32 // LINE_BLOCKS
LINE_ROWS = 48
NORM = 1.0 / math.sqrt(NG)
EXACT = lax.Precision.HIGHEST
BF = jnp.bfloat16
F32 = jnp.float32
MIB = 1 << 20

AXES = ("zl", "co", "x", "y", "zh")
SIZES = (4, 2, 4, 4, 2)
SIZE = dict(zip(AXES, SIZES))
KA = ("zl", "co")
GA = ("x", "y", "zh")


def split_table(table):
    high = table.astype(np.float32).astype(BF)
    low = (table - high.astype(np.float64)).astype(np.float32).astype(BF)
    return high, low


def plane_angles():
    index = np.arange(PLANE)
    x, y = index // NY, index % NY
    turns = (np.outer(x, x) % NX) / NX + (np.outer(y, y) % NY) / NY
    return 2.0 * np.pi * turns


def line_angles():
    index = np.arange(NZ)
    return 2.0 * np.pi * (np.outer(index, index) % NZ) / NZ


def turned(value, axis, step):
    size = SIZE[axis]
    return lax.ppermute(value, axis, [(i, (i + step) % size) for i in range(size)])


def spread(value, axis):
    return jnp.stack([value] + [turned(value, axis, d) for d in range(1, SIZE[axis])])


def copies_to_all(value, axes):
    count = math.prod(SIZE[axis] for axis in axes)
    copies = jnp.broadcast_to(value[None], (count,) + value.shape)
    return lax.all_to_all(copies, axes, split_axis=0, concat_axis=0, tiled=True)


def dot(a, b, contract=((1,), (0,)), precision=None):
    return lax.dot_general(
        a, b, (contract, ((), ())), precision=precision, preferred_element_type=F32
    )


def screened_kernel(gmap_ref, line_ref, high_ref, low_ref, w_ref, out_ref, end_ref, lines_ref):
    step = pl.program_id(0)
    end_ref[...] = jnp.zeros_like(end_ref)

    @pl.when(step < LINE_STEPS)
    def _():
        rows = 2 * HALF
        keep = lax.broadcasted_iota(jnp.int32, (1, 8, 256), 1) == (
            lax.broadcasted_iota(jnp.int32, (1, 8, 256), 2) >> 5
        )
        for b in range(LINE_BLOCKS):
            level = gmap_ref[b] & (NZ - 1)
            hot = (lax.broadcasted_iota(jnp.int32, (NZ, 256), 0) == level).astype(F32).astype(BF)
            picked = dot(line_ref[...], hot)
            tables = []
            for at in (0, LINE_ROWS):
                wide = jnp.broadcast_to(picked[at : at + rows][:, None, :], (rows, 8, 256))
                tables.append(jnp.where(keep, wide, 0.0).reshape(rows * 8, 256).astype(BF))
            block = w_ref[:, b * 256 : (b + 1) * 256]
            both = dot(jnp.concatenate(tables, axis=0), block, ((1,), (1,)))
            total = both[: rows * 8] + both[rows * 8 :]
            at = pl.multiple_of((step * LINE_BLOCKS + b) * 8, 8)
            lines_ref[:, pl.ds(at, 8), :] = total.reshape(rows, 8, 256)

    @pl.when(step >= LINE_STEPS)
    def _():
        z = step - LINE_STEPS
        real, imag = lines_ref[z], lines_ref[HALF + z]
        for odd in range(2):
            if odd:
                both = [real[:128] - real[128:], imag[:128] - imag[128:]]
            else:
                both = [real[:128] + real[128:], imag[:128] + imag[128:]]
            both = jnp.concatenate(both, axis=0)
            top = both.astype(BF)
            rest = (both - top.astype(F32)).astype(BF)
            high, low = high_ref[odd], low_ref[odd]
            prod = (dot(high, top) + (dot(high, rest) + dot(low, top))).astype(BF)
            for half in range(8):
                at = (2 * half + odd) * NY
                out_ref[0, at : at + NY] = prod[half * NY : (half + 1) * NY]
                out_ref[0, 256 + at : 256 + at + NY] = prod[128 + half * NY : 144 + half * NY]


def screened_transform(screened, gmap):
    angles = line_angles()[:HALF]
    table = np.concatenate([np.cos(angles), -np.sin(angles)], axis=0)
    padding = np.zeros((LINE_ROWS - 2 * HALF, NZ), BF)
    line = np.concatenate([x for part in split_table(table) for x in (part, padding)], axis=0)
    angles = plane_angles().reshape(NX, NY, PLANE)[:, :, :128]
    tables = []
    for odd in range(2):
        part = angles[odd::2].reshape(128, 128)
        cosine, sine = np.cos(part), np.sin(part)
        tables.append(np.block([[cosine, sine], [sine, -cosine]]))
    high, low = split_table(np.stack(tables))
    n = LINE_BLOCKS
    last = LINE_STEPS - 1
    return pl.pallas_call(
        screened_kernel,
        grid=(LINE_STEPS + HALF,),
        in_specs=[
            pl.BlockSpec((n, 1, 256), lambda i: (jnp.minimum(i, last), 0, 0)),
            pl.BlockSpec((2 * LINE_ROWS, NZ), lambda i: (0, 0)),
            pl.BlockSpec((2, 256, 256), lambda i: (0, 0, 0)),
            pl.BlockSpec((2, 256, 256), lambda i: (0, 0, 0)),
            pl.BlockSpec((256, n * 256), lambda i: (0, jnp.minimum(i, last))),
        ],
        out_specs=[
            pl.BlockSpec((1, 512, 256), lambda i: (jnp.maximum(i - LINE_STEPS, 0), 0, 0)),
            pl.BlockSpec((8, 128), lambda i: (0, 0)),
        ],
        out_shape=[
            jax.ShapeDtypeStruct((HALF, 512, 256), BF),
            jax.ShapeDtypeStruct((8, 128), F32),
        ],
        scratch_shapes=[pltpu.VMEM((2 * HALF, PLANE, 256), F32)],
        compiler_params=pltpu.CompilerParams(vmem_limit_bytes=40 * MIB),
        cost_estimate=pl.CostEstimate(
            flops=48 * 256 * 256 * 256 * HALF, bytes_accessed=9 * MIB, transcendentals=0
        ),
        name="screened_transform",
    )(gmap.reshape(32, 1, 256), jnp.asarray(line), jnp.asarray(high), jnp.asarray(low), screened)


def halves(value):
    high = value.astype(BF)
    return high, (value - high.astype(F32)).astype(BF)


def dot_halves(a, b, contract=((1,), (0,))):
    return dot(a[0], b[0], contract) + (dot(a[0], b[1], contract) + dot(a[1], b[0], contract))


def choose_kernel(partner_ref, place_ref, flip_ref, near_ref, far_ref, val_ref, cond_ref):
    level, core = place_ref[0], place_ref[1]
    for m in range(8):
        wanted = partner_ref[(level * 2 + core) * 8 + m]
        back = (level - wanted // 16) & 3
        at = back * 8 + (wanted & 7)
        near = (wanted // 8) % 2 == core

        def take(ref, m=m, at=at):
            row = ref[at]
            val_ref[1, m] = row[:16]
            cond_ref[m] = row[16:]

        pl.when(near)(functools.partial(take, near_ref))
        pl.when(jnp.logical_not(near))(functools.partial(take, far_ref))
    for part, rows in ((0, near_ref[:8, :16]), (1, val_ref[1])):
        turned_rows = dot(rows.reshape(128, 256), flip_ref[...]).astype(BF)
        val_ref[part] = turned_rows.reshape(8, 16, 256)


def choose(partner, near, far, flip):
    shape = jax.ShapeDtypeStruct((8, 16, 256), BF)
    place = jnp.stack([lax.axis_index("zl"), lax.axis_index("co")]).astype(jnp.int32)
    return pl.pallas_call(
        choose_kernel,
        in_specs=[pl.BlockSpec(memory_space=pltpu.SMEM)] * 2
        + [pl.BlockSpec(memory_space=pltpu.VMEM)] * 3,
        out_specs=[pl.BlockSpec(memory_space=pltpu.VMEM)] * 2,
        out_shape=[jax.ShapeDtypeStruct((2, 8, 16, 256), BF), shape],
        compiler_params=pltpu.CompilerParams(vmem_limit_bytes=16 * MIB),
        name="partner_choice",
    )(partner, place, flip, near, far)


def cond_kernel(high_ref, low_ref, home_ref, away_ref, x_ref, rows_ref):
    for k in range(8):
        home, away = home_ref[k].astype(F32), away_ref[k].astype(F32)
        hr, hi = home[:8], home[8:]
        for place, band in enumerate((0, 2, 4, 6, 1, 3, 5, 7)):
            ar, ai = away[band : band + 1], away[8 + band : 9 + band]
            real = hr * ar + hi * ai
            imag = hr * ai - hi * ar
            at = k * 128 + place * 8
            rows_ref[at : at + 8, :256] = real
            rows_ref[at : at + 8, 256:] = imag
            rows_ref[at + 64 : at + 72, :256] = imag
            rows_ref[at + 64 : at + 72, 256:] = -real
    table = high_ref[...], low_ref[...]
    for k in range(4):
        rows = halves(rows_ref[k * 256 : (k + 1) * 256])
        x_ref[:, k * 256 : (k + 1) * 256] = dot_halves(table, rows, ((1,), (1,)))


def cond_planes(home, away):
    angles = plane_angles()
    high, low = split_table(np.concatenate([np.cos(angles), np.sin(angles)], axis=1))
    return pl.pallas_call(
        cond_kernel,
        out_shape=jax.ShapeDtypeStruct((256, 1024), F32),
        in_specs=[pl.BlockSpec(memory_space=pltpu.VMEM)] * 4,
        out_specs=pl.BlockSpec(memory_space=pltpu.VMEM),
        scratch_shapes=[pltpu.VMEM((1024, 512), F32)],
        compiler_params=pltpu.CompilerParams(vmem_limit_bytes=24 * MIB),
        cost_estimate=pl.CostEstimate(
            flops=12 * 256 * 512 * 1024, bytes_accessed=2 * MIB, transcendentals=0
        ),
        name="cond_planes",
    )(jnp.asarray(high), jnp.asarray(low), home, away)


def build_rows(rows_ref, waves, mirrored):
    home_ref, away_ref, home_back_ref, away_back_ref = waves

    def density(home, away, v):
        hr, hi = home[v : v + 1], home[8 + v : 9 + v]
        ar, ai = away[:8], away[8:]
        return hr * ar + hi * ai, hr * ai - hi * ar

    for k in range(8):
        home, away = home_ref[0, k].astype(F32), away_ref[0, k].astype(F32)
        home_back, away_back = home_back_ref[0, k].astype(F32), away_back_ref[0, k].astype(F32)
        if mirrored is not None:
            home_back = home_back * mirrored
        for pair in range(4):
            pieces = []
            for v in (2 * pair, 2 * pair + 1):
                real, imag = density(home, away, v)
                real_back, imag_back = density(home_back, away_back, v)
                pieces.append(
                    (real + real_back, imag - imag_back, imag + imag_back, real_back - real)
                )
            even_re, odd_im, even_im, odd_re = (
                jnp.concatenate(p, axis=0).astype(BF) for p in zip(*pieces)
            )
            at = k * 128 + pair * 16
            rows_ref[at : at + 16, :256] = even_re
            rows_ref[at : at + 16, 256:] = odd_im
            rows_ref[at + 64 : at + 80, :256] = even_im
            rows_ref[at + 64 : at + 80, 256:] = odd_re


def response_kernel(place_ref, *refs):
    first_waves, second_waves = refs[:4], refs[4:8]
    before_ref, w_ref, sum_ref, first_ref, second_ref = refs[8:]
    step = pl.program_id(0)
    mirrored = jnp.where(step % 8 == 0, 0.0, 1.0)
    before = dot(second_ref[...], before_ref[0])
    build_rows(first_ref, first_waves, mirrored)
    total = jnp.where(step == 0, 0.0, sum_ref[...] + before)
    total = total + dot(first_ref[...], w_ref[0])
    build_rows(second_ref, second_waves, None)
    sum_ref[...] = total


def response(place, home, away, screened):
    def block(which, second, back):
        def index(step, place_ref):
            z = jnp.minimum(2 * step + second, HALF - 1)
            z = (NZ - z) & (NZ - 1) if back else z
            x = ((place_ref[0] >> 3) - (z >> 3)) & 3
            y = ((place_ref[0] >> 1) - (z >> 1)) & 3
            x, y = (x, y) if which == 0 else (y, x)
            return ((y * 4 + x) * 2 + ((place_ref[0] ^ z) & 1), 0, 0, 0)

        return pl.BlockSpec((1, 8, 16, 256), index)

    blocks = [block(w, s, b) for s in range(2) for b in (False, True) for w in range(2)]
    return pl.pallas_call(
        response_kernel,
        grid_spec=pltpu.PrefetchScalarGridSpec(
            num_scalar_prefetch=1,
            grid=(HALF // 2 + 1,),
            in_specs=blocks
            + [
                pl.BlockSpec((1, 512, 256), lambda i, p: (jnp.maximum(2 * i - 1, 0), 0, 0)),
                pl.BlockSpec((1, 512, 256), lambda i, p: (2 * i, 0, 0)),
            ],
            out_specs=pl.BlockSpec((1024, 256), lambda i, p: (0, 0)),
            scratch_shapes=[pltpu.VMEM((1024, 512), BF), pltpu.VMEM((1024, 512), BF)],
        ),
        out_shape=jax.ShapeDtypeStruct((1024, 256), F32),
        compiler_params=pltpu.CompilerParams(vmem_limit_bytes=20 * MIB),
        cost_estimate=pl.CostEstimate(
            flops=16 * 1024 * 512 * 256 * HALF, bytes_accessed=9 * MIB, transcendentals=0
        ),
        name="valence_response",
    )(place.reshape(1), *([home, away] * 4), screened, screened)


def spectrum_kernel(cos_ref, sin_ref, x_ref, out_ref):
    first = lax.broadcasted_iota(jnp.int32, (1, 128), 1) < 64
    table = halves(jnp.concatenate([cos_ref[...], sin_ref[...]], axis=1))
    for pair in range(4):
        straight, crossed = [], []
        for k in (2 * pair, 2 * pair + 1):
            x = x_ref[:, k * 128 : (k + 1) * 128]
            other = pltpu.roll(x, 64, 1)
            straight.append(x)
            crossed.append(jnp.where(first, other, -other))
        both = [jnp.concatenate(part, axis=1) for part in (straight, crossed)]
        cond = dot_halves(table, halves(jnp.concatenate(both, axis=0)))
        cond = (cond * NORM).astype(BF).astype(F32).T
        out_ref[pair * 256 : (pair + 1) * 256] = cond.astype(BF)


def cond_spectrum(cosine, sine, columns):
    return pl.pallas_call(
        spectrum_kernel,
        out_shape=jax.ShapeDtypeStruct((1024, 256), BF),
        in_specs=[pl.BlockSpec(memory_space=pltpu.VMEM)] * 3,
        out_specs=pl.BlockSpec(memory_space=pltpu.VMEM),
        compiler_params=pltpu.CompilerParams(vmem_limit_bytes=16 * MIB),
        cost_estimate=pl.CostEstimate(
            flops=24 * 256 * 256 * 1024, bytes_accessed=2 * MIB, transcendentals=0
        ),
        name="cond_spectrum",
    )(cosine, sine, columns)


def block_kernel(cond_ref, r_ref, out_ref):
    first = lax.broadcasted_iota(jnp.int32, (1, 128), 1) < 64
    for k in range(8):
        cond = cond_ref[k * 128 : (k + 1) * 128]
        rows = r_ref[k * 128 : (k + 1) * 128] * NORM
        top = rows.astype(BF)
        rest = (rows - top.astype(F32)).astype(BF)
        prod = dot(cond, top, ((1,), (1,))) + dot(cond, rest, ((1,), (1,)))
        swapped = pltpu.roll(prod[64:], 64, 1)
        both = prod[:64] + jnp.where(first, swapped, -swapped)
        even, odd = both[:32], both[32:]
        out_ref[:, 2 * k, :] = jnp.where(first, even, pltpu.roll(odd, 64, 1))
        out_ref[:, 2 * k + 1, :] = jnp.where(first, pltpu.roll(even, 64, 1), odd)


def kernel_blocks(cond, rows):
    return pl.pallas_call(
        block_kernel,
        out_shape=jax.ShapeDtypeStruct((32, 16, 128), F32),
        in_specs=[pl.BlockSpec(memory_space=pltpu.VMEM)] * 2,
        out_specs=pl.BlockSpec(memory_space=pltpu.VMEM),
        compiler_params=pltpu.CompilerParams(vmem_limit_bytes=16 * MIB),
        cost_estimate=pl.CostEstimate(
            flops=4 * 128 * 256 * 1024, bytes_accessed=2 * MIB, transcendentals=0
        ),
        name="kernel_blocks",
    )(cond, rows)


def line_tables(gmap, place):
    level = lax.dynamic_slice_in_dim(gmap, place * 256, 256) & (NZ - 1)
    column = jnp.arange(256, dtype=jnp.int32)
    angle = (level[:, None] * (column // 8)[None, :]) % NZ
    same = (column // NZ)[:, None] == (column % 8)[None, :]
    angle = angle.astype(F32) * (2.0 * math.pi / NZ)
    return jnp.where(same, jnp.cos(angle), 0.0), jnp.where(same, jnp.sin(angle), 0.0)


def lay_out_kernel(full_ref, rows_ref, mirror_ref):
    low = lax.broadcasted_iota(jnp.int32, (1, 128), 1) < 64
    for m in range(4):
        for n in range(4):
            for c in (2 * n, 2 * n + 1):
                piece = full_ref[m * 4 + n, 0, (c & 1) * 16 : (c & 1) * 16 + 16].astype(F32)
                at = (c * 4 + m) * 128
                rows_ref[:, :, at : at + 128] = piece.reshape(8, 2, 128)
            even = full_ref[m * 4 + n, 1, :16].astype(F32)
            odd = full_ref[m * 4 + n, 1, 16:].astype(F32)
            first = jnp.where(low, even, pltpu.roll(odd, 64, 1))
            second = jnp.where(low, pltpu.roll(even, 64, 1), odd)
            at = (2 * m * 4 + n) * 128
            mirror_ref[:, :, at : at + 128] = first.reshape(8, 2, 128)
            mirror_ref[:, :, at + 512 : at + 640] = second.reshape(8, 2, 128)


def lay_out(full):
    shape = jax.ShapeDtypeStruct((8, 2, 4096), F32)
    return pl.pallas_call(
        lay_out_kernel,
        in_specs=[pl.BlockSpec(memory_space=pltpu.VMEM)],
        out_specs=[pl.BlockSpec(memory_space=pltpu.VMEM)] * 2,
        out_shape=[shape, shape],
        compiler_params=pltpu.CompilerParams(vmem_limit_bytes=16 * MIB),
        name="lay_out",
    )(full)


def on_device(wavefunctions, partner, gmap, screened):
    ka_place = lax.axis_index(KA)
    place = lax.axis_index(GA)
    owned = ka_place * 8 + jnp.arange(8, dtype=jnp.int32)

    waves = wavefunctions.reshape(8, 2, 2, 8, 256).transpose(0, 2, 1, 3, 4).reshape(8, 32, 256)
    near = spread(waves, "zl").reshape(32, 32, 256)

    index = jnp.arange(PLANE, dtype=jnp.int32)
    negative = (NX - index // NY) % NX * NY + (NY - index % NY) % NY
    negative = jnp.where(place > NZ // 2, negative, index)
    flip = (index[:, None] == negative[None, :]).astype(BF)
    tables = line_tables(gmap, place)
    near, tables = lax.optimization_barrier((near, tables))
    far = turned(near, "co", 1)

    vals, away_cond = choose(partner, near, far, flip)
    planes = cond_planes(waves[:, 16:], away_cond)
    vals = spread(vals, "zh")
    home, away = spread(vals[:, 0], "x"), spread(vals[:, 1], "y")
    home, away, planes, screened = lax.optimization_barrier((home, away, planes, screened))
    homes = [home] + [turned(home, "y", d) for d in range(1, 4)]
    aways = [away] + [turned(away, "x", d) for d in range(1, 3)]
    wide, end = screened_transform(screened, gmap)
    away, planes, end = lax.optimization_barrier((away, planes, end))
    aways.append(turned(away, "x", 3))
    columns = lax.all_to_all(planes, GA, split_axis=0, concat_axis=0, tiled=True)
    home = jnp.stack(homes).reshape(32, 8, 16, 256)
    away = jnp.stack(aways).reshape(32, 8, 16, 256)
    rows = response(place, home, away, wide)
    cond = cond_spectrum(*tables, columns)
    blocks = kernel_blocks(cond, rows)

    parts = lax.all_to_all(blocks, ("x", "y"), split_axis=0, concat_axis=0, tiled=True)
    mine = jnp.sum(parts.reshape(16, 2, 16, 128), axis=0)
    mine = mine + turned(mine, "zh", 1)
    close = spread(mine, "zl")
    everyone = jnp.stack([close, turned(close, "co", 1)]).reshape(2, 4, 2, 8, 256)
    everyone = everyone.transpose(0, 1, 3, 2, 4).reshape(64, 512)
    slot = jnp.arange(64, dtype=jnp.int32)
    level = (lax.axis_index("zl") - slot // 8) & 3
    core = (lax.axis_index("co") + slot // 32) & 1
    holds = (level * 2 + core) * 8 + slot % 8
    number = jnp.arange(64, dtype=jnp.int32)
    source = jnp.sum(jnp.where(partner[None, :] == owned[:, None], number[None, :], 0), axis=1)
    select = (source[:, None] == holds[None, :]).astype(F32)
    mirror = jnp.dot(select, everyone, precision=EXACT)
    mirror = mirror.reshape(8, 2, 2, 128).transpose(1, 0, 2, 3).reshape(32, 128)
    lane = jnp.arange(128, dtype=jnp.int32)
    moved = lane // 64 * 64 + lane % 8 * 8 + lane // 8 % 8
    turn = (lane[:, None] == moved[None, :]).astype(F32)
    sign = jnp.where(jnp.arange(32) % 2 == 0, 1.0, -1.0).astype(F32)
    mirror = jnp.dot(mirror, turn, precision=EXACT) * sign[:, None]
    both = jnp.stack([mine.reshape(32, 128), mirror]).astype(BF)
    full = copies_to_all(both, ("x", "y"))
    return lay_out(full)


def solution(mesh):
    fine = Mesh(mesh.devices.reshape(SIZES), AXES)
    in_specs = (P(KA, None, None, GA, None), P(), P(), P(GA, None))
    out_specs = (P(KA, None, None), P(KA, None, None))
    return jax.shard_map(
        on_device, mesh=fine, in_specs=in_specs, out_specs=out_specs, check_vma=False
    )
```
